256 devices in a mesh: dp: 4 (over x_lo, core), ctx: 64 (over y, z, x_hi).
Axes of the slice: x: 4 (x_hi: 2, x_lo: 2; x = x_hi * 2 + x_lo), y: 4, z: 8, core: 2. Of those that a mesh axis runs over, the one named last changes fastest.
Arguments:
- layer_input: bfloat16 [16384, 8192], P('ctx', 'dp'), may hold values from -16 to 16
- conv_output: bfloat16 [16384, 8192], P('ctx', 'dp'), may hold values from -6 to 6
- state_maps: bfloat16 [16384, 256], P('ctx'), may hold values from -0.1875 to 0.1875
- log_decay: float32 [128, 16384], P('dp', 'ctx'), may hold values from -1 to 0, as said below
- out_grad: bfloat16 [16384, 8192], P('ctx', 'dp'), may hold values from -6 to 6
Outputs:
- grad_conv: bfloat16 [16384, 8192], P('ctx', 'dp')
- grad_maps: float32 [16384, 256], P('ctx')
- grad_decay: float32 [128, 16384], P('dp', 'ctx')
- grad_weight: float32 [8192, 256], P(('dp', 'ctx'))
The draws below stay inside these ranges and needn't reach their ends.
Inputs may be any that keep to these rules, and one draw needn't show every extreme that they name: `log_decay`: negative.
All inputs are finite; a program needn't handle non-finite values.
Results may differ from the reference program's by a relative error of at most 0.0054.
Values sent between devices are 32-bit elements; how exact they have to be, the bound alone decides.
A program may use at most 320 MiB of HBM per device.

```python
import math
import jax
import jax.numpy as jnp
from jax import lax

D = 8192
H = 128
P_SIZE = 64
N = 128
BLOCK = 128
TOK_DEV = 256
TOKEN_SPAN = 16384


def draw_log_decay(key, part):
    key = jax.random.fold_in(key, 7)
    generator_seeds = jax.random.split(key, 7)
    slow_share = 0.5
    noise_perturbation = jnp.exp(jax.random.uniform(generator_seeds[4], (H, TOKEN_SPAN), jnp.float32, -0.69, 0.69))
    slow_heads = jax.random.uniform(generator_seeds[0], (H, 1), jnp.float32) < slow_share
    slow_rate = jnp.exp(jax.random.uniform(generator_seeds[1], (H, 1), jnp.float32, math.log(0.05), 0.0)) / TOKEN_SPAN
    fast_rate = jnp.exp(jax.random.uniform(generator_seeds[2], (H, 1), jnp.float32, math.log(1.0 / 50.0), math.log(1.0 / 30.0)))
    forgetting_speeds = jnp.where(slow_heads, slow_rate, fast_rate)
    division_multiplier = jnp.exp(jax.random.uniform(generator_seeds[3], (H, TOKEN_SPAN // TOK_DEV, 1), jnp.float32, -0.69, 0.69))
    division_multiplier = jnp.broadcast_to(division_multiplier, (H, TOKEN_SPAN // TOK_DEV, TOK_DEV)).reshape(H, TOKEN_SPAN)
    clustered_spans = jax.random.uniform(generator_seeds[5], (1, TOKEN_SPAN), jnp.float32) < 2.0 / TOKEN_SPAN
    stacked_levels = jax.random.uniform(generator_seeds[6], (1, TOKEN_SPAN), jnp.float32, math.log(0.5), math.log(0.8))
    return -forgetting_speeds * division_multiplier * noise_perturbation + jnp.where(clustered_spans, stacked_levels, 0.0)


def with_spikes(drawn, own_key, source, target, shards_of, factor):
    owner, partner = [(jnp.arange(drawn.shape[dim]) // (drawn.shape[dim] // shards_of)).reshape([-1 if axis == dim else 1 for axis in range(drawn.ndim)]) for dim in (source, target)]
    chosen = jax.random.permutation(own_key, shards_of)[partner]
    strong = (owner == chosen) | (owner == (partner + shards_of // 2) % shards_of)
    return jnp.where(strong, factor * drawn, drawn)


def steps_of(key, dims, shards, smallest, largest):
    factor_of = 1.0
    for position, parts in shards:
        draws = jax.random.uniform(jax.random.fold_in(jax.random.fold_in(key, 6), position), (parts,), jnp.float32, smallest / len(shards), largest / len(shards))
        factor_of = factor_of * jnp.repeat(jnp.exp(draws), dims[position] // parts).reshape((-1,) + (1,) * (len(dims) - 1 - position))
    return factor_of


def centred(own_key, dims, scale, bound, shards=(), kind=jnp.bfloat16):
    loudness = steps_of(own_key, dims, shards, -0.22, 0.18) if shards else 1.0
    array = jax.random.normal(own_key, dims, jnp.float32) * scale * loudness
    return jnp.minimum(jnp.maximum(array, -bound), bound).astype(kind)


def bell_draw_with(stream_key, extent, width, most, cuts, heavy, kind=jnp.bfloat16):
    array = width * jax.random.normal(stream_key, extent, jnp.float32)
    if cuts:
        array = array * steps_of(stream_key, extent, cuts, -0.22, 0.18)
    return jnp.clip(with_spikes(array, jax.random.fold_in(stream_key, 3), *heavy), -most, most).astype(kind)


def setup_inputs(seed: int = 0) -> dict:
    arg_keys = jax.random.split(jax.random.key(seed), 6)
    layer_input = bell_draw_with(arg_keys[0], (TOKEN_SPAN, D), 1.0, 16.0, ((0, 64), (1, 4)), (0, 1, 64, 4.0))
    conv_output = centred(arg_keys[1], (TOKEN_SPAN, H * P_SIZE), 1.0, 6.0, ((0, 64), (1, 4)))
    state_maps = centred(arg_keys[2], (TOKEN_SPAN, 2 * N), 0.03, 0.1875, ((0, 64),))
    log_decay = draw_log_decay(jax.random.fold_in(arg_keys[5], 71), 0)
    out_grad = centred(arg_keys[4], (TOKEN_SPAN, H * P_SIZE), 1.0, 6.0, ((0, 64), (1, 4)))
    return dict(layer_input=layer_input, conv_output=conv_output, state_maps=state_maps, log_decay=log_decay, out_grad=out_grad)


def round_trip(values):
    return lax.optimization_barrier(values.astype(jnp.bfloat16)).astype(jnp.float32)

def block_summary(block_item):
    conv_block, grad_block, maps_block, decay_block = block_item
    head_count = decay_block.shape[0]
    tok_count = conv_block.shape[0]
    head_size = conv_block.shape[1] // head_count
    state_size = maps_block.shape[1] // 2
    cumulative = jnp.cumsum(decay_block, axis=1)
    to_end = jnp.exp(cumulative[:, -1:] - cumulative)
    from_start = jnp.exp(cumulative)
    conv_heads = conv_block.reshape(tok_count, head_count, head_size).astype(jnp.float32)
    grad_heads = grad_block.reshape(tok_count, head_count, head_size).astype(jnp.float32)
    input_map = maps_block[:, :state_size].astype(jnp.float32)
    output_map = maps_block[:, state_size:].astype(jnp.float32)
    input_weighted = round_trip(to_end[:, :, None] * input_map[None])
    output_weighted = round_trip(from_start[:, :, None] * output_map[None])
    final_state = jnp.einsum('thp,htn->hpn', conv_heads, input_weighted, precision=lax.Precision.HIGHEST)
    back_grad = jnp.einsum('thp,htn->hpn', grad_heads, output_weighted, precision=lax.Precision.HIGHEST)
    return (jnp.exp(cumulative[:, -1]), final_state, back_grad)

def block_gradients(block_item):
    conv_block, grad_block, maps_block, decay_block, start_state, finish, final_state = block_item
    head_count = decay_block.shape[0]
    tok_count = conv_block.shape[0]
    head_size = conv_block.shape[1] // head_count
    state_size = maps_block.shape[1] // 2
    highest = lax.Precision.HIGHEST
    cumulative = jnp.cumsum(decay_block, axis=1)
    to_end = jnp.exp(cumulative[:, -1:] - cumulative)
    from_start = jnp.exp(cumulative)
    conv_heads = conv_block.reshape(tok_count, head_count, head_size).astype(jnp.float32)
    grad_heads = grad_block.reshape(tok_count, head_count, head_size).astype(jnp.float32)
    input_low = maps_block[:, :state_size]
    output_low = maps_block[:, state_size:]
    input_map = input_low.astype(jnp.float32)
    output_map = output_low.astype(jnp.float32)
    scores = jnp.dot(output_low, input_low.T, preferred_element_type=jnp.float32)
    positions = jnp.arange(tok_count)
    causal = positions[:, None] >= positions[None, :]
    spread = cumulative[:, :, None] - cumulative[:, None, :]
    decay_mat = jnp.where(causal[None], jnp.exp(jnp.minimum(spread, 0.0)), 0.0)
    inner_dots = jnp.einsum('thp,shp->hts', grad_heads, conv_heads, precision=highest)
    weight_low = round_trip(decay_mat * scores[None])
    decay_dots = decay_mat * inner_dots
    mix = lax.optimization_barrier(jnp.sum(decay_dots, axis=0))
    start_low = round_trip(start_state)
    finish_low = round_trip(finish)
    finish_b = jnp.einsum('sn,hpn->hsp', input_map, finish_low, precision=highest)
    conv_finish = jnp.einsum('thp,hpn->htn', conv_heads, finish_low, precision=highest)
    grad_start = jnp.einsum('thp,hpn->htn', grad_heads, start_low, precision=highest)
    grad_conv = jnp.einsum('hut,uhp->thp', weight_low, grad_heads, precision=highest)
    grad_conv = grad_conv + jnp.transpose(to_end[:, :, None] * finish_b, (1, 0, 2))
    grad_input = jnp.dot(mix.T, output_map, precision=highest)
    grad_input = grad_input + lax.optimization_barrier(jnp.sum(to_end[:, :, None] * conv_finish, axis=0))
    grad_output = jnp.dot(mix, input_map, precision=highest)
    grad_output = grad_output + lax.optimization_barrier(jnp.sum(from_start[:, :, None] * grad_start, axis=0))
    triple = decay_dots * scores[None]
    end_state = jnp.exp(cumulative[:, -1])[:, None, None] * start_state + final_state
    end_term = lax.optimization_barrier(jnp.sum(finish * end_state, axis=(1, 2)))
    change = from_start * lax.optimization_barrier(jnp.sum(grad_start * output_map[None], axis=2))
    change = change + lax.optimization_barrier(jnp.sum(triple, axis=2)) - lax.optimization_barrier(jnp.sum(triple, axis=1))
    change = change - to_end * lax.optimization_barrier(jnp.sum(conv_finish * input_map[None], axis=2))
    change = change.at[:, -1].add(end_term)
    grad_decay = jnp.flip(jnp.cumsum(jnp.flip(change, axis=1), axis=1), axis=1)
    grad_maps = jnp.concatenate([grad_input, grad_output], axis=1)
    return (grad_conv.reshape(tok_count, head_count * head_size).astype(jnp.bfloat16), grad_maps, grad_decay)

def forward_step(run_state, block_item):
    totals, final_state = block_item
    return (totals[:, None, None] * run_state + final_state, run_state)

def backward_step(run_grad, block_item):
    totals, back_grad = block_item
    return (back_grad + totals[:, None, None] * run_grad, run_grad)

def weight_step(running, block_item):
    input_rows, maps_rows = block_item
    return (running + jnp.dot(input_rows.T, maps_rows.astype(jnp.bfloat16), preferred_element_type=jnp.float32), None)

def reference(layer_input, conv_output, state_maps, log_decay, out_grad):
    block_count = TOKEN_SPAN // BLOCK
    conv_blocks = conv_output.reshape(block_count, BLOCK, conv_output.shape[1])
    grad_blocks = out_grad.reshape(block_count, BLOCK, out_grad.shape[1])
    maps_blocks = state_maps.reshape(block_count, BLOCK, state_maps.shape[1])
    decay_blocks = jnp.transpose(log_decay.reshape(H, block_count, BLOCK), (1, 0, 2))
    totals, finals, backs = lax.map(block_summary, (conv_blocks, grad_blocks, maps_blocks, decay_blocks))
    zero_state = jnp.zeros(finals.shape[1:], jnp.float32)
    _, starts = lax.scan(forward_step, zero_state, (totals, finals))
    _, finishes = lax.scan(backward_step, zero_state, (totals, backs), reverse=True)
    grad_conv, grad_maps, grad_decay = lax.map(block_gradients, (conv_blocks, grad_blocks, maps_blocks, decay_blocks, starts, finishes, finals))
    grad_conv = grad_conv.reshape(TOKEN_SPAN, grad_conv.shape[2])
    grad_maps = grad_maps.reshape(TOKEN_SPAN, grad_maps.shape[2])
    grad_decay = jnp.transpose(grad_decay, (1, 0, 2)).reshape(H, TOKEN_SPAN)
    input_blocks = layer_input.reshape(block_count, BLOCK, layer_input.shape[1])
    maps_grad_blocks = grad_maps.reshape(block_count, BLOCK, grad_maps.shape[1])
    running, _ = lax.scan(weight_step, jnp.zeros((D, 2 * N), jnp.float32), (input_blocks, maps_grad_blocks))
    grad_weight = running * (1.0 / math.sqrt(TOKEN_SPAN))
    return (grad_conv, grad_maps, grad_decay, grad_weight)
```

```python
import functools
import math

import jax
import jax.numpy as jnp
from jax import lax
from jax.experimental import pallas as pl
from jax.experimental.pallas import tpu as pltpu
from jax.sharding import PartitionSpec as P

BLOCK = 128
HEAD = 64
STATE = 128
PAIR = 2 * HEAD
ROWS = PAIR + 8
Z_SIZE = 8
Y_SIZE = 4
FAR_FIRST = (4, 3, 5, 2, 6, 1, 7)
MESH = pl.DeviceIdType.MESH
F32 = jnp.float32
BF16 = jnp.bfloat16
HIGHEST = lax.Precision.HIGHEST
NT = (((1,), (1,)), ((), ()))
TN = (((0,), (0,)), ((), ()))
NN = (((1,), (0,)), ((), ()))
VMEM = pl.BlockSpec(memory_space=pltpu.VMEM)
LIMIT = 56 * 1024 * 1024


def dot(a, b, dims=NN, precision=None):
    return lax.dot_general(a, b, dims, precision=precision, preferred_element_type=F32)


def iota(shape, axis):
    return lax.broadcasted_iota(jnp.int32, shape, axis)


def two_parts(values):
    high = values.astype(BF16)
    return high, (values - high.astype(F32)).astype(BF16)


def head_lanes(first_head, head_count, columns, width):
    shape = (head_count, columns)
    return (iota(shape, 0) == first_head + iota(shape, 1) // width).astype(BF16)


def widen(parts, lanes):
    return dot(parts[0], lanes) + dot(parts[1], lanes)


def summary_kernel(conv, grad, maps, decay, ahead, behind):
    heads, toks = decay.shape
    group = 8 * HEAD
    decays = decay[...]
    lower = (iota((toks, toks), 1) <= iota((toks, toks), 0)).astype(F32)
    cum = dot(lower, decays, NT, HIGHEST)
    to_end = two_parts(jnp.exp(cum[toks - 1 : toks, :] - cum))
    from_start = two_parts(jnp.exp(cum))
    total = jnp.exp(dot(decays, jnp.ones((toks, STATE), F32), NN, HIGHEST))
    spread = (iota((heads * 4, heads), 0) // 4 == iota((heads * 4, heads), 1)).astype(F32)
    tiles = dot(spread, total, NN, HIGHEST).reshape(heads // 2, 8, STATE)
    ahead[:, PAIR:, :] = tiles
    behind[:, PAIR:, :] = tiles
    input_map = maps[:, :STATE]
    output_map = maps[:, STATE:]
    for part in range(heads * HEAD // group):
        columns = slice(part * group, (part + 1) * group)
        slices = slice(part * group // PAIR, (part + 1) * group // PAIR)
        lanes = head_lanes(part * group // HEAD, heads, group, HEAD)
        weighted = (widen(to_end, lanes) * conv[:, columns].astype(F32)).astype(BF16)
        ahead[slices, :PAIR, :] = dot(weighted, input_map, TN).reshape(-1, PAIR, STATE)
        weighted = (widen(from_start, lanes) * grad[:, columns].astype(F32)).astype(BF16)
        behind[slices, :PAIR, :] = dot(weighted, output_map, TN).reshape(-1, PAIR, STATE)


def place():
    dp, ctx = lax.axis_index("dp"), lax.axis_index("ctx")
    return dp, ctx // (2 * Z_SIZE), (ctx // 2) % Z_SIZE, ctx % 2


def device(dp, y, z, x):
    return (dp, (y * Z_SIZE + z) * 2 + x)


def greet(partners):
    barrier = pltpu.get_barrier_semaphore()
    for partner in partners:
        pl.semaphore_signal(barrier, inc=1, device_id=partner, device_id_type=MESH)
    pl.semaphore_wait(barrier, len(partners))


def remote(src, dst, send, recv, target):
    return pltpu.make_async_remote_copy(
        src_ref=src, dst_ref=dst, send_sem=send, recv_sem=recv, device_id=target, device_id_type=MESH
    )


def per_head(tile, values):
    return jnp.concatenate([values[:HEAD] * tile[0:1], values[HEAD:] * tile[4:5]], axis=0)


def carry_kernel(
    ahead, behind, start, finish,
    x_in, t_out, z_in, y_in, before, back_out, back_in, x_out,
    x_send, x_recv, z_send, z_recv, y_send, y_recv, b_send, b_recv, r_send, r_recv,
):
    dp, y, z, x = place()
    other = device(dp, y, z, 1 - x)
    z_at = [device(dp, y, (z + k) % Z_SIZE, x) for k in range(Z_SIZE)]
    y_at = [device(dp, (y + m) % Y_SIZE, z, x) for m in range(Y_SIZE)]
    greet([other] + z_at[1:] + y_at[1:])
    own = (ahead, behind)
    result = (start, finish)
    order = FAR_FIRST + (0,)
    sent = []

    def x_copy(way, k):
        piece = (z + k) % Z_SIZE
        return remote(
            own[way].at[(1 - x) * Z_SIZE + piece], x_in.at[way, piece],
            x_send.at[way, k], x_recv.at[way, k], other,
        )

    def z_copy(way, k):
        return remote(t_out.at[way, k], z_in.at[way, k], z_send.at[way, k], z_recv.at[way, k], z_at[k])

    def y_copy(way, m):
        return remote(y_in.at[way, 0], y_in.at[way, m], y_send.at[way, m], y_recv.at[way, m], y_at[m])

    def b_copy(way, k):
        return remote(
            back_out.at[way, k], back_in.at[way, k], b_send.at[way, k], b_recv.at[way, k], z_at[k]
        )

    def r_copy(way, k):
        piece = x * Z_SIZE + (z + Z_SIZE - k) % Z_SIZE
        return remote(
            x_out.at[way, k], result[way].at[piece], r_send.at[way, k], r_recv.at[way, k], other
        )

    def begin(copy):
        copy.start()
        sent.append(copy)

    for way in range(2):
        for k in order:
            begin(x_copy(way, k))

    def join(way):
        first = x == way
        for k in order:
            x_copy(way, k).wait_recv()
            piece = (z + k) % Z_SIZE
            mine = own[way][x * Z_SIZE + piece]
            theirs = x_in[way, piece]
            early = jnp.where(first, mine, theirs)
            late = jnp.where(first, theirs, mine)
            state = per_head(late[PAIR:], early[:PAIR]) + late[:PAIR]
            target = z_in.at[way, 0] if k == 0 else t_out.at[way, k]
            target[:PAIR] = state
            target[PAIR:] = early[PAIR:] * late[PAIR:]
            if k:
                begin(z_copy(way, k))

    def scan(way):
        for k in FAR_FIRST:
            z_copy(way, k).wait_recv()
        state = jnp.zeros((PAIR, STATE), F32)
        decay = jnp.ones((8, STATE), F32)
        for step in range(Z_SIZE):
            at = Z_SIZE - 1 - step if way else step
            slot = (z + Z_SIZE - at) % Z_SIZE
            out = (at + Z_SIZE - z) % Z_SIZE
            before[way, out, :PAIR] = state
            before[way, out, PAIR:] = decay
            tile = z_in[way, slot, PAIR:]
            state = per_head(tile, state) + z_in[way, slot, :PAIR]
            decay = decay * tile
        y_in[way, 0, :PAIR] = state
        y_in[way, 0, PAIR:] = decay
        for m in range(1, Y_SIZE):
            begin(y_copy(way, m))

    def spread(way):
        for m in range(1, Y_SIZE):
            y_copy(way, m).wait_recv()
        state = jnp.zeros((PAIR, STATE), F32)
        for step in range(Y_SIZE):
            at = Y_SIZE - 1 - step if way else step
            slot = (y + Y_SIZE - at) % Y_SIZE
            counts = (at > y) if way else (at < y)
            new = per_head(y_in[way, slot, PAIR:], state) + y_in[way, slot, :PAIR]
            state = jnp.where(counts, new, state)
        for k in order:
            target = back_in.at[way, 0] if k == 0 else back_out.at[way, k]
            target[...] = before[way, k, :PAIR] + per_head(before[way, k, PAIR:], state)
            if k:
                begin(b_copy(way, k))

    def hand_on(way):
        first = x == way
        for k in (0, 1, 7, 2, 6, 3, 5, 4):
            if k:
                b_copy(way, k).wait_recv()
            piece = (z + Z_SIZE - k) % Z_SIZE
            early = back_in[way, k]
            left = jnp.where(first, own[way][x * Z_SIZE + piece], x_in[way, piece])
            late = per_head(left[PAIR:], early) + left[:PAIR]
            x_out[way, k] = jnp.where(first, late, early)
            result[way][x * Z_SIZE + piece] = jnp.where(first, early, late)
            begin(r_copy(way, k))

    join(0)
    join(1)
    scan(0)
    scan(1)
    spread(0)
    spread(1)
    hand_on(0)
    hand_on(1)
    for way in range(2):
        for k in order:
            r_copy(way, k).wait_recv()
    for copy in sent:
        copy.wait_send()


def block_kernel(
    conv, grad, maps, decay, start, finish, grad_conv, grad_decay, grad_maps,
    cum_rows, total_rows, change, ends, mix, ingoing, outgoing,
):
    heads, toks = decay.shape
    count = toks // BLOCK
    width = 4 * HEAD
    square = (BLOCK, BLOCK)
    causal = iota(square, 1) <= iota(square, 0)
    lower = causal.astype(F32)
    cum_parts, to_end, from_start, scores = [], [], [], []
    for block in range(count):
        rows = slice(block * BLOCK, (block + 1) * BLOCK)
        decays = decay[:, rows]
        cum = dot(lower, decays, NT, HIGHEST)
        high, middle = two_parts(cum)
        low = (cum - high.astype(F32) - middle.astype(F32)).astype(BF16)
        cum_parts.append((high, middle, low))
        to_end.append(two_parts(jnp.exp(cum[BLOCK - 1 : BLOCK, :] - cum)))
        from_start.append(two_parts(jnp.exp(cum)))
        cum_rows[block] = jnp.broadcast_to(dot(decays, lower, NT, HIGHEST)[:, None, :], (heads, 8, BLOCK))
        total = jnp.exp(dot(decays, jnp.ones((BLOCK, STATE), F32), NN, HIGHEST))
        total_rows[block] = jnp.broadcast_to(total[:, None, :], (heads, 8, STATE))
        scores.append(dot(maps[rows, STATE:], maps[rows, :STATE], NT))
    change[...] = jnp.zeros_like(change)
    mix[...] = jnp.zeros_like(mix)
    ingoing[...] = jnp.zeros_like(ingoing)
    outgoing[...] = jnp.zeros_like(outgoing)

    def one_group(index, _):
        columns = pl.ds(pl.multiple_of(index * width, width), width)
        group_heads = pl.ds(index * 4, 4)
        lanes = head_lanes(index * 4, heads, width, HEAD)
        broad = head_lanes(index * 4, heads, 4 * BLOCK, BLOCK)
        in_first = iota((BLOCK, PAIR), 1) < HEAD

        def decayed(block, state):
            return (state.reshape(4, 8, 8, STATE) * total_rows[block, group_heads][:, None]).reshape(width, STATE)

        x, g, te, fs, xw, gw, final, back = [], [], [], [], [], [], [], []
        for block in range(count):
            rows = slice(block * BLOCK, (block + 1) * BLOCK)
            x.append(conv[rows, columns])
            g.append(grad[rows, columns])
            te.append(widen(to_end[block], lanes))
            fs.append(widen(from_start[block], lanes))
            xw.append((te[block] * x[block].astype(F32)).astype(BF16))
            gw.append((fs[block] * g[block].astype(F32)).astype(BF16))
            final.append(dot(xw[block], maps[rows, :STATE], TN))
            back.append(dot(gw[block], maps[rows, STATE:], TN))
        starts = [start[pl.ds(index * 2, 2)].reshape(width, STATE)]
        for block in range(count):
            starts.append(decayed(block, starts[block]) + final[block])
        finishes = [finish[pl.ds(index * 2, 2)].reshape(width, STATE)]
        for block in reversed(range(1, count)):
            finishes.insert(0, decayed(block, finishes[0]) + back[block])
        for block in range(count):
            rows = slice(block * BLOCK, (block + 1) * BLOCK)
            input_map, output_map = maps[rows, :STATE], maps[rows, STATE:]
            ends[block, group_heads] = jnp.sum(
                (finishes[block] * starts[block + 1]).reshape(4, 8, 8, STATE), axis=1
            )
            start_low = starts[block].astype(BF16)
            finish_low = finishes[block].astype(BF16)
            ingoing[block] += dot(xw[block], finish_low)
            outgoing[block] += dot(gw[block], start_low)
            from_finish = te[block] * dot(input_map, finish_low, NT)
            from_state = fs[block] * dot(output_map, start_low, NT)
            column = sum(dot(part, broad) for part in cum_parts[block])
            y_parts, d_parts, mixed = [], [], None
            for pair in range(2):
                lane = slice(pair * PAIR, (pair + 1) * PAIR)
                x_pair, g_pair = x[block][:, lane], g[block][:, lane]
                zero = jnp.zeros_like(x_pair)
                x_own = [jnp.where(in_first, x_pair, zero), jnp.where(in_first, zero, x_pair)]
                g_own = [jnp.where(in_first, g_pair, zero), jnp.where(in_first, zero, g_pair)]
                weights = []
                for one in range(2):
                    head = 2 * pair + one
                    col = column[:, head * BLOCK : (head + 1) * BLOCK].reshape(16, 8, BLOCK)
                    gap = (col - cum_rows[block, index * 4 + head][None]).reshape(square)
                    falls = jnp.exp(jnp.where(causal, gap, -1e30))
                    inner = dot(g_own[one], x_pair, NT)
                    weights.append((falls * scores[block]).astype(BF16))
                    term = falls * inner
                    mixed = term if mixed is None else mixed + term
                y_parts.append(
                    dot(jnp.concatenate(weights, axis=1), jnp.concatenate(x_own, axis=0))
                )
                d_parts.append(
                    dot(jnp.concatenate(weights, axis=0), jnp.concatenate(g_own, axis=0), TN)
                )
            mix[block] += mixed
            y_all = jnp.concatenate(y_parts, axis=1) + from_state
            d_all = jnp.concatenate(d_parts, axis=1) + from_finish
            grad_conv[rows, columns] = d_all.astype(BF16)
            product = g[block].astype(F32) * y_all - x[block].astype(F32) * d_all
            high, low = two_parts(product)
            change[block] += dot(lanes, high, NT) + dot(lanes, low, NT)
        return 0

    lax.fori_loop(0, heads * HEAD // width, one_group, 0)
    for block in range(count):
        rows = slice(block * BLOCK, (block + 1) * BLOCK)
        input_map, output_map = maps[rows, :STATE].astype(F32), maps[rows, STATE:].astype(F32)
        grad_maps[rows, :STATE] = dot(mix[block], output_map, TN, HIGHEST) + ingoing[block]
        grad_maps[rows, STATE:] = dot(mix[block], input_map, NN, HIGHEST) + outgoing[block]
        end_term = jnp.sum(jnp.sum(ends[block], axis=1), axis=1, keepdims=True)
        at_last = iota((heads, BLOCK), 1) == BLOCK - 1
        changes = change[block] + jnp.where(at_last, end_term, 0.0)
        grad_decay[:, rows] = dot(changes, lower, NN, HIGHEST)


def weight_kernel(
    scale, part, layer, total, weight,
    gathered, flipped, by_z, by_y, z_in, y_in, z_sum, y_sum, z_late, y_late, x_own, x_in,
    p_send, p_recv, g_send, g_recv, z_send, z_recv, y_send, y_recv,
    zl_send, zl_recv, yl_send, yl_recv, x_send, x_recv,
):
    dp, y, z, x = place()
    other = device(dp, y, z, 1 - x)
    z_at = [device(dp, y, (z + k) % Z_SIZE, x) for k in range(Z_SIZE)]
    y_at = [device(dp, (y + m) % Y_SIZE, z, x) for m in range(Y_SIZE)]
    p_at = [device((dp + m) % 4, y, z, x) for m in range(4)]
    greet([other] + z_at[1:] + y_at[1:] + p_at[1:])
    toks = part.shape[0]
    share = toks // 4
    sent = []

    def begin(copy):
        copy.start()
        sent.append(copy)

    def p_copy(m):
        rows = pl.ds(pl.multiple_of((dp + m) % 4 * share, share), share)
        return remote(part.at[rows], gathered.at[m], p_send.at[m], p_recv.at[m], p_at[m])

    def g_copy(m):
        rows = pl.ds(pl.multiple_of(dp * share, share), share)
        return remote(total.at[rows], total.at[rows], g_send.at[m], g_recv.at[m], p_at[m])

    def z_copy(k):
        return remote(by_z.at[(z + k) % Z_SIZE], z_in.at[k], z_send.at[k], z_recv.at[k], z_at[k])

    def y_copy(m):
        return remote(by_y.at[(y + m) % Y_SIZE], y_in.at[m], y_send.at[m], y_recv.at[m], y_at[m])

    def y_late_copy(m):
        return remote(
            z_sum.at[(y + m) % Y_SIZE], y_late.at[m], yl_send.at[m], yl_recv.at[m], y_at[m]
        )

    def z_late_copy(k):
        return remote(
            y_sum.at[(z + k) % Z_SIZE], z_late.at[k], zl_send.at[k], zl_recv.at[k], z_at[k]
        )

    def x_copy(half):
        return remote(
            x_own.at[half, 1 - x], x_in.at[half], x_send.at[half], x_recv.at[half], other
        )

    for m in range(1, 4):
        begin(p_copy(m))
    span = layer.shape[1] // Y_SIZE
    for piece in range(Y_SIZE):
        flipped[piece] = layer[:, piece * span : (piece + 1) * span].T
    mine = pl.ds(pl.multiple_of(dp * share, share), share)
    for m in range(1, 4):
        p_copy(m).wait_recv()
    total[mine] = part[mine] + gathered[1] + gathered[2] + gathered[3]
    for m in range(1, 4):
        begin(g_copy(m))
    for m in range(1, 4):
        g_copy(m).wait_recv()
    low = total[...].astype(BF16)
    for piece in range(Y_SIZE):
        made = dot(flipped[piece], low) * scale
        made = made.reshape(Z_SIZE, span // Z_SIZE, 2 * STATE)
        by_z[:, piece] = made[:, :, :STATE]
        by_y[piece] = made[:, :, STATE:]
    for k in FAR_FIRST[:3]:
        begin(z_copy(k))
    for m in (2, 1, 3):
        begin(y_copy(m))
    for k in FAR_FIRST[3:]:
        begin(z_copy(k))
    for m in range(1, Y_SIZE):
        y_copy(m).wait_recv()
    y_sum[...] = by_y[y] + y_in[1] + y_in[2] + y_in[3]
    for k in FAR_FIRST:
        begin(z_late_copy(k))
    for k in range(1, Z_SIZE):
        z_copy(k).wait_recv()
    z_sum[...] = by_z[z] + sum(z_in[k] for k in range(1, Z_SIZE))
    for m in (2, 1, 3):
        begin(y_late_copy(m))
    for k in range(1, Z_SIZE):
        z_late_copy(k).wait_recv()
    x_own[1] = (y_sum[z] + sum(z_late[k] for k in range(1, Z_SIZE))).reshape(2, -1, STATE)
    begin(x_copy(1))
    for m in range(1, Y_SIZE):
        y_late_copy(m).wait_recv()
    x_own[0] = (z_sum[y] + sum(y_late[m] for m in range(1, Y_SIZE))).reshape(2, -1, STATE)
    begin(x_copy(0))
    for half in (1, 0):
        x_copy(half).wait_recv()
        weight[:, half * STATE : (half + 1) * STATE] = x_own[half, x] + x_in[half]
    for copy in sent:
        copy.wait_send()


def dma(*shape):
    return pltpu.SemaphoreType.DMA(shape)


def on_device(layer_input, conv_output, state_maps, log_decay, out_grad):
    toks, columns = conv_output.shape
    heads = log_decay.shape[0]
    slices = heads // 2
    half = slices // 2
    packed = jax.ShapeDtypeStruct((slices, ROWS, STATE), F32)
    plain = jax.ShapeDtypeStruct((slices, PAIR, STATE), F32)
    ahead, behind = pl.pallas_call(
        summary_kernel,
        out_shape=(packed, packed),
        in_specs=[VMEM] * 4,
        out_specs=(VMEM, VMEM),
        compiler_params=pltpu.CompilerParams(vmem_limit_bytes=LIMIT),
        name="summary",
    )(conv_output, out_grad, state_maps, log_decay)
    start, finish = pl.pallas_call(
        carry_kernel,
        out_shape=(plain, plain),
        in_specs=[VMEM] * 2,
        out_specs=(VMEM, VMEM),
        scratch_shapes=[
            pltpu.VMEM((2, half, ROWS, STATE), F32),
            pltpu.VMEM((2, Z_SIZE, ROWS, STATE), F32),
            pltpu.VMEM((2, Z_SIZE, ROWS, STATE), F32),
            pltpu.VMEM((2, Y_SIZE, ROWS, STATE), F32),
            pltpu.VMEM((2, Z_SIZE, ROWS, STATE), F32),
            pltpu.VMEM((2, Z_SIZE, PAIR, STATE), F32),
            pltpu.VMEM((2, Z_SIZE, PAIR, STATE), F32),
            pltpu.VMEM((2, Z_SIZE, PAIR, STATE), F32),
            dma(2, Z_SIZE), dma(2, Z_SIZE), dma(2, Z_SIZE), dma(2, Z_SIZE),
            dma(2, Y_SIZE), dma(2, Y_SIZE), dma(2, Z_SIZE), dma(2, Z_SIZE),
            dma(2, Z_SIZE), dma(2, Z_SIZE),
        ],
        compiler_params=pltpu.CompilerParams(
            collective_id=0, has_side_effects=True, vmem_limit_bytes=LIMIT
        ),
        name="carry",
    )(ahead, behind)
    count = toks // BLOCK
    grad_conv, grad_decay, part = pl.pallas_call(
        block_kernel,
        out_shape=(
            jax.ShapeDtypeStruct((toks, columns), BF16),
            jax.ShapeDtypeStruct((heads, toks), F32),
            jax.ShapeDtypeStruct((toks, 2 * STATE), F32),
        ),
        in_specs=[VMEM] * 6,
        out_specs=(VMEM,) * 3,
        scratch_shapes=[
            pltpu.VMEM((count, heads, 8, BLOCK), F32),
            pltpu.VMEM((count, heads, 8, STATE), F32),
            pltpu.VMEM((count, heads, BLOCK), F32),
            pltpu.VMEM((count, heads, 8, STATE), F32),
            pltpu.VMEM((count, BLOCK, BLOCK), F32),
            pltpu.VMEM((count, BLOCK, STATE), F32),
            pltpu.VMEM((count, BLOCK, STATE), F32),
        ],
        compiler_params=pltpu.CompilerParams(vmem_limit_bytes=LIMIT),
        name="blocks",
    )(conv_output, out_grad, state_maps, log_decay, start, finish)
    span = columns // Y_SIZE
    tile = span // Z_SIZE
    grad_maps, grad_weight = pl.pallas_call(
        functools.partial(weight_kernel, 1.0 / math.sqrt(toks * lax.axis_size("ctx"))),
        out_shape=(
            jax.ShapeDtypeStruct((toks, 2 * STATE), F32),
            jax.ShapeDtypeStruct((tile // 2, 2 * STATE), F32),
        ),
        in_specs=[VMEM] * 2,
        out_specs=(VMEM, VMEM),
        scratch_shapes=[
            pltpu.VMEM((4, toks // 4, 2 * STATE), F32),
            pltpu.VMEM((Y_SIZE, span, toks), BF16),
            pltpu.VMEM((Z_SIZE, Y_SIZE, tile, STATE), F32),
            pltpu.VMEM((Y_SIZE, Z_SIZE, tile, STATE), F32),
            pltpu.VMEM((Z_SIZE, Y_SIZE, tile, STATE), F32),
            pltpu.VMEM((Y_SIZE, Z_SIZE, tile, STATE), F32),
            pltpu.VMEM((Y_SIZE, tile, STATE), F32),
            pltpu.VMEM((Z_SIZE, tile, STATE), F32),
            pltpu.VMEM((Z_SIZE, tile, STATE), F32),
            pltpu.VMEM((Y_SIZE, tile, STATE), F32),
            pltpu.VMEM((2, 2, tile // 2, STATE), F32),
            pltpu.VMEM((2, tile // 2, STATE), F32),
            dma(4), dma(4), dma(4), dma(4),
            dma(Z_SIZE), dma(Z_SIZE), dma(Y_SIZE), dma(Y_SIZE),
            dma(Z_SIZE), dma(Z_SIZE), dma(Y_SIZE), dma(Y_SIZE),
            dma(2), dma(2),
        ],
        compiler_params=pltpu.CompilerParams(
            collective_id=1, has_side_effects=True, vmem_limit_bytes=LIMIT
        ),
        name="weight",
    )(part, layer_input)
    return (grad_conv, grad_maps, grad_decay, grad_weight)


def solution(mesh):
    placed = (P("ctx", "dp"), P("ctx", "dp"), P("ctx", None), P("dp", "ctx"), P("ctx", "dp"))
    return jax.shard_map(
        on_device,
        mesh=mesh,
        in_specs=placed,
        out_specs=(P("ctx", "dp"), P("ctx", None), P("dp", "ctx"), P(("dp", "ctx"), None)),
        check_vma=False,
    )
```

```python
import functools
import math

import jax
import jax.numpy as jnp
from jax import lax
from jax.experimental import pallas as pl
from jax.experimental.pallas import tpu as pltpu
from jax.sharding import PartitionSpec as P

BLOCK = 128
HEAD = 64
STATE = 128
PAIR = 2 * HEAD
ROWS = PAIR + 8
Z_SIZE = 8
Y_SIZE = 4
MESH = pl.DeviceIdType.MESH
F32 = jnp.float32
BF16 = jnp.bfloat16
HIGHEST = lax.Precision.HIGHEST
NT = (((1,), (1,)), ((), ()))
TN = (((0,), (0,)), ((), ()))
NN = (((1,), (0,)), ((), ()))
VMEM = pl.BlockSpec(memory_space=pltpu.VMEM)
LIMIT = 56 * 1024 * 1024


def dot(a, b, dims=NN, precision=None):
    return lax.dot_general(a, b, dims, precision=precision, preferred_element_type=F32)


def iota(shape, axis):
    return lax.broadcasted_iota(jnp.int32, shape, axis)


def two_parts(values):
    high = values.astype(BF16)
    return high, (values - high.astype(F32)).astype(BF16)


def head_lanes(first_head, head_count, columns, width):
    shape = (head_count, columns)
    return (iota(shape, 0) == first_head + iota(shape, 1) // width).astype(BF16)


def widen(parts, lanes):
    return dot(parts[0], lanes) + dot(parts[1], lanes)


def place():
    dp, ctx = lax.axis_index("dp"), lax.axis_index("ctx")
    return dp, ctx // (2 * Z_SIZE), (ctx // 2) % Z_SIZE, ctx % 2


def device(dp, y, z, x):
    return (dp, (y * Z_SIZE + z) * 2 + x)


def remote(src, dst, send, recv, target):
    return pltpu.make_async_remote_copy(
        src_ref=src, dst_ref=dst, send_sem=send, recv_sem=recv, device_id=target, device_id_type=MESH
    )


def per_head(tile, values):
    return jnp.concatenate([values[:HEAD] * tile[0:1], values[HEAD:] * tile[4:5]], axis=0)


def order(step):
    odd = step % 2
    return Z_SIZE // 2 + (step // 2) * (1 - odd) - ((step + 1) // 2) * odd


def kernel(
    scale, z_rows,
    conv, grad, maps, decay, layer, grad_conv, grad_maps, grad_decay, weight,
    own, x_in, t_out, z_in, y_in, before, back_out, back_in, x_out, result,
    cum_rows, total_rows, change, ends, mix, flow, wide, weighed, inner_out, finals, backs, states,
    part, gathered, total, flipped, by_y0, by_y1, by_z,
    ry_in0, ry_in1, rz_in, ry_sum0, ry_sum1, rz_sum, rz_late0, rz_late1, ry_late, rx_own, rx_in,
    x_send, x_recv, z_send, z_recv, y_send, y_recv, b_send, b_recv, r_send, r_recv,
    p_send, p_recv, g_send, g_recv, ry_send, ry_recv, rz_send, rz_recv,
    rzl_send, rzl_recv, ryl_send, ryl_recv, rx_send, rx_recv,
):
    dp, y, z, x = place()
    other = device(dp, y, z, 1 - x)

    def z_at(k):
        return device(dp, y, (z + k) % Z_SIZE, x)

    def y_at(m):
        return device(dp, (y + m) % Y_SIZE, z, x)

    def p_at(m):
        return device((dp + m) % 4, y, z, x)

    partners = [other] + [z_at(k) for k in range(1, Z_SIZE)]
    partners += [y_at(m) for m in range(1, Y_SIZE)] + [p_at(m) for m in range(1, 4)]
    barrier = pltpu.get_barrier_semaphore()
    for partner in partners:
        pl.semaphore_signal(barrier, inc=1, device_id=partner, device_id_type=MESH)

    heads, toks = decay.shape
    count = toks // BLOCK
    width = 4 * HEAD
    square = (BLOCK, BLOCK)
    blocks = [slice(block * BLOCK, (block + 1) * BLOCK) for block in range(count)]


    def x_copy(way, k):
        piece = (z + k) % Z_SIZE
        return remote(
            own.at[way, (1 - x) * Z_SIZE + piece], x_in.at[way, piece],
            x_send.at[way, k], x_recv.at[way, k], other,
        )

    def z_copy(way, k):
        return remote(t_out.at[way, k], z_in.at[way, k], z_send.at[way, k], z_recv.at[way, k], z_at(k))

    def y_copy(way, m):
        return remote(y_in.at[way, 0], y_in.at[way, m], y_send.at[way, m], y_recv.at[way, m], y_at(m))

    def b_copy(way, k):
        return remote(
            back_out.at[way, k], back_in.at[way, k], b_send.at[way, k], b_recv.at[way, k], z_at(k)
        )

    def r_copy(way, k):
        piece = x * Z_SIZE + (z + Z_SIZE - k) % Z_SIZE
        return remote(
            x_out.at[way, k], result.at[way, piece], r_send.at[way, k], r_recv.at[way, k], other
        )


    decays = decay[...]
    lower_all = (iota((toks, toks), 1) <= iota((toks, toks), 0)).astype(F32)
    cum_all = dot(lower_all, decays, NT, HIGHEST)
    factors = (two_parts(jnp.exp(cum_all[toks - 1 : toks, :] - cum_all)), two_parts(jnp.exp(cum_all)))
    sources = (conv, grad)
    total_all = jnp.exp(dot(decays, jnp.ones((toks, STATE), F32), NN, HIGHEST))
    expand = (iota((heads * 4, heads), 0) // 4 == iota((heads * 4, heads), 1)).astype(F32)
    tiles = dot(expand, total_all, NN, HIGHEST).reshape(heads // 2, 8, STATE)
    for way in range(2):
        own[way, :, PAIR:, :] = tiles

    def summarize(way, half):
        chunk = 8 * HEAD
        for piece in range(heads // 2 * HEAD // chunk):
            first = half * (heads // 2 * HEAD) + piece * chunk
            columns = pl.ds(pl.multiple_of(first, chunk), chunk)
            lanes = head_lanes(half * (heads // 2) + piece * 8, heads, chunk, HEAD)
            weighted = (widen(factors[way], lanes) * sources[way][:, columns].astype(F32)).astype(BF16)
            made = dot(weighted, maps[:, way * STATE : (way + 1) * STATE], TN)
            own[way, pl.ds(half * Z_SIZE + piece * 4, 4), :PAIR, :] = made.reshape(4, PAIR, STATE)

    summarize(0, 1 - x)
    pl.semaphore_wait(barrier, len(partners))
    for step in range(Z_SIZE):
        x_copy(0, order(step)).start()
    summarize(1, 1 - x)
    for step in range(Z_SIZE):
        x_copy(1, order(step)).start()
    summarize(0, x)
    summarize(1, x)


    causal = iota(square, 1) <= iota(square, 0)
    lower = causal.astype(F32)
    cum_parts, to_end, from_start, scores = [], [], [], []
    for block in range(count):
        rows = blocks[block]
        local = decay[:, rows]
        cum = dot(lower, local, NT, HIGHEST)
        high, middle = two_parts(cum)
        low = (cum - high.astype(F32) - middle.astype(F32)).astype(BF16)
        cum_parts.append((high, middle, low))
        to_end.append(two_parts(jnp.exp(cum[BLOCK - 1 : BLOCK, :] - cum)))
        from_start.append(two_parts(jnp.exp(cum)))
        cum_rows[block] = jnp.broadcast_to(dot(local, lower, NT, HIGHEST)[:, None, :], (heads, 8, BLOCK))
        whole = jnp.exp(dot(local, jnp.ones((BLOCK, STATE), F32), NN, HIGHEST))
        total_rows[block] = jnp.broadcast_to(whole[:, None, :], (heads, 8, STATE))
        scores.append(dot(maps[rows, STATE:], maps[rows, :STATE], NT))
    change[...] = jnp.zeros_like(change)
    mix[...] = jnp.zeros_like(mix)
    flow[...] = jnp.zeros_like(flow)

    def inside(index):
        columns = pl.ds(pl.multiple_of(index * width, width), width)
        pair_slices = pl.ds(index * 2, 2)
        lanes = head_lanes(index * 4, heads, width, HEAD)
        broad = head_lanes(index * 4, heads, 4 * BLOCK, BLOCK)
        in_first = iota((BLOCK, PAIR), 1) < HEAD
        for block in range(count):
            rows = blocks[block]
            xs, gs = conv[rows, columns], grad[rows, columns]
            te, fs = widen(to_end[block], lanes), widen(from_start[block], lanes)
            wide[0, rows, columns] = fs
            wide[1, rows, columns] = te
            xw = (te * xs.astype(F32)).astype(BF16)
            gw = (fs * gs.astype(F32)).astype(BF16)
            weighed[0, rows, columns] = gw
            weighed[1, rows, columns] = xw
            finals[block, pair_slices] = dot(xw, maps[rows, :STATE], TN).reshape(2, PAIR, STATE)
            if block:
                backs[block - 1, pair_slices] = dot(gw, maps[rows, STATE:], TN).reshape(2, PAIR, STATE)
            column = sum(dot(piece, broad) for piece in cum_parts[block])
            y_parts, d_parts, mixed = [], [], None
            for pair in range(2):
                lane = slice(pair * PAIR, (pair + 1) * PAIR)
                x_pair, g_pair = xs[:, lane], gs[:, lane]
                zero = jnp.zeros_like(x_pair)
                x_own = [jnp.where(in_first, x_pair, zero), jnp.where(in_first, zero, x_pair)]
                g_own = [jnp.where(in_first, g_pair, zero), jnp.where(in_first, zero, g_pair)]
                weights = []
                for one in range(2):
                    head = 2 * pair + one
                    col = column[:, head * BLOCK : (head + 1) * BLOCK].reshape(16, 8, BLOCK)
                    gap = (col - cum_rows[block, index * 4 + head][None]).reshape(square)
                    falls = jnp.exp(jnp.where(causal, gap, -1e30))
                    term = falls * dot(g_own[one], x_pair, NT)
                    weights.append((falls * scores[block]).astype(BF16))
                    mixed = term if mixed is None else mixed + term
                y_parts.append(dot(jnp.concatenate(weights, axis=1), jnp.concatenate(x_own, axis=0)))
                d_parts.append(dot(jnp.concatenate(weights, axis=0), jnp.concatenate(g_own, axis=0), TN))
            mix[block] += mixed
            inner_out[0, rows, columns] = jnp.concatenate(y_parts, axis=1)
            inner_out[1, rows, columns] = jnp.concatenate(d_parts, axis=1)


    def join(way, step):
        k = order(step)
        first = x == way
        x_copy(way, k).wait_recv()
        piece = (z + k) % Z_SIZE
        mine = own[way, x * Z_SIZE + piece]
        theirs = x_in[way, piece]
        early = jnp.where(first, mine, theirs)
        late = jnp.where(first, theirs, mine)
        t_out[way, k, :PAIR] = per_head(late[PAIR:], early[:PAIR]) + late[:PAIR]
        t_out[way, k, PAIR:] = early[PAIR:] * late[PAIR:]

        @pl.when(step < Z_SIZE - 1)
        def _():
            z_copy(way, k).start()

    def scan(way):
        for step in range(Z_SIZE - 1):
            z_copy(way, order(step)).wait_recv()
        z_in[way, 0] = t_out[way, 0]
        state = jnp.zeros((PAIR, STATE), F32)
        fade = jnp.ones((8, STATE), F32)
        for step in range(Z_SIZE):
            at = Z_SIZE - 1 - step if way else step
            slot = (z + Z_SIZE - at) % Z_SIZE
            out = (at + Z_SIZE - z) % Z_SIZE
            before[way, out, :PAIR] = state
            before[way, out, PAIR:] = fade
            tile = z_in[way, slot, PAIR:]
            state = per_head(tile, state) + z_in[way, slot, :PAIR]
            fade = fade * tile
        y_in[way, 0, :PAIR] = state
        y_in[way, 0, PAIR:] = fade
        for m in (2, 1, 3):
            y_copy(way, m).start()

    def spread(way):
        for m in range(1, Y_SIZE):
            y_copy(way, m).wait_recv()
        state = jnp.zeros((PAIR, STATE), F32)
        for step in range(Y_SIZE):
            at = Y_SIZE - 1 - step if way else step
            slot = (y + Y_SIZE - at) % Y_SIZE
            counts = (at > y) if way else (at < y)
            new = per_head(y_in[way, slot, PAIR:], state) + y_in[way, slot, :PAIR]
            state = jnp.where(counts, new, state)
        for step in range(Z_SIZE):
            k = order(step)
            target = back_out.at[way, k] if k else back_in.at[way, 0]
            target[...] = before[way, k, :PAIR] + per_head(before[way, k, PAIR:], state)
            if k:
                b_copy(way, k).start()

    def hand_on(way, step):
        k = order(Z_SIZE - 1 - step)
        first = x == way

        @pl.when(step > 0)
        def _():
            b_copy(way, k).wait_recv()

        piece = (z + Z_SIZE - k) % Z_SIZE
        early = back_in[way, k]
        left = jnp.where(first, own[way, x * Z_SIZE + piece], x_in[way, piece])
        late = per_head(left[PAIR:], early) + left[:PAIR]
        x_out[way, k] = jnp.where(first, late, early)
        result[way, x * Z_SIZE + piece] = jnp.where(first, early, late)
        r_copy(way, k).start()


    def fade_rows(block, index, state):
        tiles = total_rows[block, pl.ds(index * 2, 2)][:, None]
        return (state.reshape(2, 8, 8, STATE) * tiles).reshape(PAIR, STATE)

    def add_change(block, index, product):
        lanes = head_lanes(index * 2, heads, PAIR, HEAD)
        high, low = two_parts(product)
        change[block] += dot(lanes, high, NT) + dot(lanes, low, NT)

    def with_start(index):
        columns = pl.ds(pl.multiple_of(index * PAIR, PAIR), PAIR)
        state = result[0, index]
        for block in range(count):
            rows = blocks[block]
            low = state.astype(BF16)
            flow[0, block] += dot(weighed[0, rows, columns], low)
            outputs = inner_out[0, rows, columns] + wide[0, rows, columns] * dot(maps[rows, STATE:], low, NT)
            add_change(block, index, grad[rows, columns].astype(F32) * outputs)
            state = fade_rows(block, index, state) + finals[block, index]
            states[block, index] = state

    def with_finish(index):
        columns = pl.ds(pl.multiple_of(index * PAIR, PAIR), PAIR)
        state = result[1, index]
        for block in reversed(range(count)):
            rows = blocks[block]
            ends[block, pl.ds(index * 2, 2)] = jnp.sum(
                (state * states[block, index]).reshape(2, 8, 8, STATE), axis=1
            )
            low = state.astype(BF16)
            flow[1, block] += dot(weighed[1, rows, columns], low)
            inputs = inner_out[1, rows, columns] + wide[1, rows, columns] * dot(maps[rows, :STATE], low, NT)
            grad_conv[rows, columns] = inputs.astype(BF16)
            add_change(block, index, conv[rows, columns].astype(F32) * -inputs)
            if block:
                state = fade_rows(block, index, state) + backs[block - 1, index]


    share = toks // 4
    mine = pl.ds(pl.multiple_of(dp * share, share), share)

    def p_copy(half, m):
        rows = pl.ds(pl.multiple_of((dp + m) % 4 * share, share), share)
        return remote(
            part.at[half, rows], gathered.at[half, m], p_send.at[half, m], p_recv.at[half, m], p_at(m)
        )

    def g_copy(half, m):
        return remote(
            total.at[half, mine], total.at[half, mine], g_send.at[half, m], g_recv.at[half, m], p_at(m)
        )

    def sum_begin(half):
        for block in range(count):
            rows = blocks[block]
            if half:
                made = dot(mix[block], maps[rows, STATE:].astype(F32), TN, HIGHEST)
            else:
                made = dot(mix[block], maps[rows, :STATE].astype(F32), NN, HIGHEST)
            part[half, rows] = made + flow[half, block]
        for m in range(1, 4):
            p_copy(half, m).start()

    def sum_middle(half):
        for m in range(1, 4):
            p_copy(half, m).wait_recv()
        total[half, mine] = part[half, mine] + gathered[half, 1] + gathered[half, 2] + gathered[half, 3]
        for m in range(1, 4):
            g_copy(half, m).start()

    def sum_end(half):
        for m in range(1, 4):
            g_copy(half, m).wait_recv()
        made = total[half]
        grad_maps[:, (1 - half) * STATE : (2 - half) * STATE] = made
        return made.astype(BF16)


    by_y, ry_in, ry_sum, rz_late = (by_y0, by_y1), (ry_in0, ry_in1), (ry_sum0, ry_sum1), (rz_late0, rz_late1)
    splits = (0, z_rows)

    def ry_copy(half, m):
        return remote(
            by_y[half].at[(y + m) % Y_SIZE], ry_in[half].at[m], ry_send.at[half, m], ry_recv.at[half, m], y_at(m)
        )

    def rzl_copy(half, k):
        return remote(
            ry_sum[half].at[(z + k) % Z_SIZE], rz_late[half].at[k],
            rzl_send.at[half, k], rzl_recv.at[half, k], z_at(k),
        )

    def rz_copy(k):
        return remote(by_z.at[(z + k) % Z_SIZE], rz_in.at[k], rz_send.at[k], rz_recv.at[k], z_at(k))

    def ryl_copy(m):
        return remote(
            rz_sum.at[(y + m) % Y_SIZE], ry_late.at[m], ryl_send.at[m], ryl_recv.at[m], y_at(m)
        )

    def rx_copy(half):
        return remote(
            rx_own.at[half, 1 - x], rx_in.at[half], rx_send.at[half], rx_recv.at[half], other
        )

    def weigh(half, low):
        cut = splits[half]
        for piece in range(Y_SIZE):
            made = dot(flipped[piece], low) * scale
            made = made.reshape(Z_SIZE, 2, -1, STATE)
            by_y[half][piece] = made[:, :, cut:]
            if cut:
                by_z[:, piece] = made[:, :, :cut]
        if cut:
            for step in range(3):
                rz_copy(order(step)).start()
        for m in (2, 1, 3):
            ry_copy(half, m).start()
        if cut:
            for step in range(3, Z_SIZE - 1):
                rz_copy(order(step)).start()

    def weigh_middle(half):
        for m in range(1, Y_SIZE):
            ry_copy(half, m).wait_recv()
        ry_sum[half][...] = by_y[half][y] + ry_in[half][1] + ry_in[half][2] + ry_in[half][3]
        for step in range(Z_SIZE - 1):
            rzl_copy(half, order(step)).start()

    def weigh_middle_z():
        for k in range(1, Z_SIZE):
            rz_copy(k).wait_recv()
        rz_sum[...] = by_z[z] + sum(rz_in[k] for k in range(1, Z_SIZE))
        for m in (2, 1, 3):
            ryl_copy(m).start()

    def weigh_late(half):
        cut = splits[half]
        if cut:
            for m in range(1, Y_SIZE):
                ryl_copy(m).wait_recv()
            rx_own[half, :, :cut] = rz_sum[y] + sum(ry_late[m] for m in range(1, Y_SIZE))
        for k in range(1, Z_SIZE):
            rzl_copy(half, k).wait_recv()
        rx_own[half, :, cut:] = ry_sum[half][z] + sum(rz_late[half][k] for k in range(1, Z_SIZE))
        rx_copy(half).start()

    def weigh_end(half):
        rx_copy(half).wait_recv()
        weight[:, (1 - half) * STATE : (2 - half) * STATE] = rx_own[half, x] + rx_in[half]


    span = layer.shape[1] // Y_SIZE
    for piece in range(Y_SIZE):
        flipped[piece] = layer[:, piece * span : (piece + 1) * span].T

    def joins(turn, _):
        way, step = turn // 4, turn % 4 * 2
        join(way, step)
        join(way, step + 1)
        inside(turn)

        @pl.when(turn == 5)
        def _():
            scan(0)

        return 0

    lax.fori_loop(0, Z_SIZE, joins, 0)
    spread(0)

    def starts(turn, _):
        way, step = turn // Z_SIZE, turn % Z_SIZE
        hand_on(way, step)

        @pl.when(turn >= Z_SIZE)
        def _():
            r_copy(0, order(Z_SIZE - 1 - step)).wait_recv()

        piece = (z + Z_SIZE - order(Z_SIZE - 1 - step)) % Z_SIZE
        half = x + way * (1 - 2 * x)
        with_start(half * Z_SIZE + piece)

        @pl.when(turn == 2)
        def _():
            scan(1)

        @pl.when(turn == 4)
        def _():
            spread(1)

        return 0

    lax.fori_loop(0, 2 * Z_SIZE, starts, 0)
    sum_begin(0)

    def finishes(turn, _):
        way, step = turn // Z_SIZE, turn % Z_SIZE

        @pl.when(turn >= Z_SIZE)
        def _():
            r_copy(1, order(Z_SIZE - 1 - step)).wait_recv()

        piece = (z + Z_SIZE - order(Z_SIZE - 1 - step)) % Z_SIZE
        half = x + way * (1 - 2 * x)
        with_finish(half * Z_SIZE + piece)

        @pl.when(turn == Z_SIZE - 1)
        def _():
            sum_middle(0)

        return 0

    lax.fori_loop(0, 2 * Z_SIZE, finishes, 0)
    sum_begin(1)
    low = sum_end(0)
    weigh(0, low)
    sum_middle(1)
    low = sum_end(1)
    weigh(1, low)
    for block in range(count):
        end_term = jnp.sum(jnp.sum(ends[block], axis=1), axis=1, keepdims=True)
        at_last = iota((heads, BLOCK), 1) == BLOCK - 1
        changes = change[block] + jnp.where(at_last, end_term, 0.0)
        grad_decay[:, blocks[block]] = dot(changes, lower, NN, HIGHEST)
    weigh_middle(0)
    weigh_middle_z()
    weigh_middle(1)
    weigh_late(0)
    weigh_late(1)
    weigh_end(0)
    weigh_end(1)

    for way in range(2):
        for k in range(Z_SIZE):
            x_copy(way, k).wait_send()
            r_copy(way, k).wait_send()
            if k:
                z_copy(way, k).wait_send()
                b_copy(way, k).wait_send()
                rzl_copy(way, k).wait_send()
                if way:
                    rz_copy(k).wait_send()
        for m in range(1, 4):
            y_copy(way, m).wait_send()
            p_copy(way, m).wait_send()
            g_copy(way, m).wait_send()
            ry_copy(way, m).wait_send()
            if way:
                ryl_copy(m).wait_send()
        rx_copy(way).wait_send()


def dma(*shape):
    return pltpu.SemaphoreType.DMA(shape)


def on_device(layer_input, conv_output, state_maps, log_decay, out_grad):
    toks, columns = conv_output.shape
    heads = log_decay.shape[0]
    slices = heads // 2
    count = toks // BLOCK
    tile = columns // (Y_SIZE * Z_SIZE * 2)
    z_rows = 8
    late = tile - z_rows

    def floats(*shape):
        return pltpu.VMEM(shape, F32)

    grad_conv, grad_maps, grad_decay, grad_weight = pl.pallas_call(
        functools.partial(kernel, 1.0 / math.sqrt(toks * lax.axis_size("ctx")), z_rows),
        out_shape=(
            jax.ShapeDtypeStruct((toks, columns), BF16),
            jax.ShapeDtypeStruct((toks, 2 * STATE), F32),
            jax.ShapeDtypeStruct((heads, toks), F32),
            jax.ShapeDtypeStruct((tile, 2 * STATE), F32),
        ),
        in_specs=[VMEM] * 5,
        out_specs=(VMEM,) * 4,
        scratch_shapes=[
            floats(2, slices, ROWS, STATE),
            floats(2, Z_SIZE, ROWS, STATE),
            floats(2, Z_SIZE, ROWS, STATE),
            floats(2, Z_SIZE, ROWS, STATE),
            floats(2, Y_SIZE, ROWS, STATE),
            floats(2, Z_SIZE, ROWS, STATE),
            floats(2, Z_SIZE, PAIR, STATE),
            floats(2, Z_SIZE, PAIR, STATE),
            floats(2, Z_SIZE, PAIR, STATE),
            floats(2, slices, PAIR, STATE),
            floats(count, heads, 8, BLOCK),
            floats(count, heads, 8, STATE),
            floats(count, heads, BLOCK),
            floats(count, heads, 8, STATE),
            floats(count, BLOCK, BLOCK),
            floats(2, count, BLOCK, STATE),
            floats(2, toks, columns),
            pltpu.VMEM((2, toks, columns), BF16),
            floats(2, toks, columns),
            floats(count, slices, PAIR, STATE),
            floats(max(count - 1, 1), slices, PAIR, STATE),
            floats(count, slices, PAIR, STATE),
            floats(2, toks, STATE),
            floats(2, 4, toks // 4, STATE),
            floats(2, toks, STATE),
            pltpu.VMEM((Y_SIZE, columns // Y_SIZE, toks), BF16),
            floats(Y_SIZE, Z_SIZE, 2, tile, STATE),
            floats(Y_SIZE, Z_SIZE, 2, late, STATE),
            floats(Z_SIZE, Y_SIZE, 2, z_rows, STATE),
            floats(Y_SIZE, Z_SIZE, 2, tile, STATE),
            floats(Y_SIZE, Z_SIZE, 2, late, STATE),
            floats(Z_SIZE, Y_SIZE, 2, z_rows, STATE),
            floats(Z_SIZE, 2, tile, STATE),
            floats(Z_SIZE, 2, late, STATE),
            floats(Y_SIZE, 2, z_rows, STATE),
            floats(Z_SIZE, 2, tile, STATE),
            floats(Z_SIZE, 2, late, STATE),
            floats(Y_SIZE, 2, z_rows, STATE),
            floats(2, 2, tile, STATE),
            floats(2, tile, STATE),
            dma(2, Z_SIZE), dma(2, Z_SIZE), dma(2, Z_SIZE), dma(2, Z_SIZE),
            dma(2, Y_SIZE), dma(2, Y_SIZE), dma(2, Z_SIZE), dma(2, Z_SIZE),
            dma(2, Z_SIZE), dma(2, Z_SIZE),
            dma(2, 4), dma(2, 4), dma(2, 4), dma(2, 4),
            dma(2, Y_SIZE), dma(2, Y_SIZE), dma(Z_SIZE), dma(Z_SIZE),
            dma(2, Z_SIZE), dma(2, Z_SIZE), dma(Y_SIZE), dma(Y_SIZE),
            dma(2), dma(2),
        ],
        compiler_params=pltpu.CompilerParams(
            collective_id=0, has_side_effects=True, vmem_limit_bytes=LIMIT
        ),
        name="backward",
    )(conv_output, out_grad, state_maps, log_decay, layer_input)
    return (grad_conv, grad_maps, grad_decay, grad_weight)


def solution(mesh):
    placed = (P("ctx", "dp"), P("ctx", "dp"), P("ctx", None), P("dp", "ctx"), P("ctx", "dp"))
    return jax.shard_map(
        on_device,
        mesh=mesh,
        in_specs=placed,
        out_specs=(P("ctx", "dp"), P("ctx", None), P("dp", "ctx"), P(("dp", "ctx"), None)),
        check_vma=False,
    )
```

```python
import functools
import math

import jax
import jax.numpy as jnp
from jax import lax
from jax.experimental import pallas as pl
from jax.experimental.pallas import tpu as pltpu
from jax.sharding import PartitionSpec as P

BLOCK = 128
HEAD = 64
STATE = 128
PAIR = 2 * HEAD
CHUNKS = 4
Z_SIZE = 8
Y_SIZE = 4
MESH = pl.DeviceIdType.MESH
F32 = jnp.float32
BF16 = jnp.bfloat16
HIGHEST = lax.Precision.HIGHEST
NT = (((1,), (1,)), ((), ()))
TN = (((0,), (0,)), ((), ()))
NN = (((1,), (0,)), ((), ()))
VMEM = pl.BlockSpec(memory_space=pltpu.VMEM)
LIMIT = 56 * 1024 * 1024


def dot(a, b, dims=NN, precision=None):
    return lax.dot_general(a, b, dims, precision=precision, preferred_element_type=F32)


def iota(shape, axis):
    return lax.broadcasted_iota(jnp.int32, shape, axis)


def two_parts(values):
    high = values.astype(BF16)
    return high, (values - high.astype(F32)).astype(BF16)


def head_lanes(first_head, head_count, columns, width):
    shape = (head_count, columns)
    return (iota(shape, 0) == first_head + iota(shape, 1) // width).astype(BF16)


def widen(parts, lanes):
    return dot(parts[0], lanes) + dot(parts[1], lanes)


def place():
    dp, ctx = lax.axis_index("dp"), lax.axis_index("ctx")
    return dp, ctx // (2 * Z_SIZE), (ctx // 2) % Z_SIZE, ctx % 2


def device(dp, y, z, x):
    return (dp, (y * Z_SIZE + z) * 2 + x)


def remote(src, dst, send, recv, target):
    return pltpu.make_async_remote_copy(
        src_ref=src, dst_ref=dst, send_sem=send, recv_sem=recv, device_id=target, device_id_type=MESH
    )


def pick(tile, part):
    return jnp.where(part == 0, tile[0:1], tile[4:5])


def order(step):
    odd = step % 2
    return Z_SIZE // 2 + (step // 2) * (1 - odd) - ((step + 1) // 2) * odd


def kernel(
    scale, z_rows,
    conv, grad, maps, decay, layer, grad_conv, grad_maps, grad_decay, weight,
    own, x_in, t_out, z_in, y_in, before, back_out, back_in, x_out, result,
    d_own, d_x, d_t, d_z, d_y, d_before,
    cum_rows, total_rows, change, ends, mix, flow, wide, weighed, inner_out, finals, backs, states,
    part, gathered, total, flipped, by_y0, by_y1, by_z,
    ry_in0, ry_in1, rz_in, ry_sum0, ry_sum1, rz_sum, rz_late0, rz_late1, ry_late, rx_own, rx_in,
    x_send, x_recv, z_send, z_recv, y_send, y_recv, b_send, b_recv, r_send, r_recv,
    dx_send, dx_recv, dz_send, dz_recv, dy_send, dy_recv,
    p_send, p_recv, g_send, g_recv, ry_send, ry_recv, rz_send, rz_recv,
    rzl_send, rzl_recv, ryl_send, ryl_recv, rx_send, rx_recv,
):
    dp, y, z, x = place()
    other = device(dp, y, z, 1 - x)

    def z_at(k):
        return device(dp, y, (z + k) % Z_SIZE, x)

    def y_at(m):
        return device(dp, (y + m) % Y_SIZE, z, x)

    def p_at(m):
        return device((dp + m) % 4, y, z, x)

    partners = [other] + [z_at(k) for k in range(1, Z_SIZE)]
    partners += [y_at(m) for m in range(1, Y_SIZE)] + [p_at(m) for m in range(1, 4)]
    barrier = pltpu.get_barrier_semaphore()
    for partner in partners:
        pl.semaphore_signal(barrier, inc=1, device_id=partner, device_id_type=MESH)

    heads, toks = decay.shape
    count = toks // BLOCK
    width = 4 * HEAD
    square = (BLOCK, BLOCK)
    blocks = [slice(block * BLOCK, (block + 1) * BLOCK) for block in range(count)]


    def head_rows(chunk):
        return pl.ds(pl.multiple_of(chunk % 2 * HEAD, HEAD), HEAD)

    def x_copy(chunk, k):
        piece, rows = (z + k) % Z_SIZE, head_rows(chunk)
        return remote(
            own.at[chunk // 2, (1 - x) * Z_SIZE + piece, rows], x_in.at[chunk // 2, piece, rows],
            x_send.at[chunk, k], x_recv.at[chunk, k], other,
        )

    def z_copy(chunk, k):
        return remote(
            t_out.at[chunk, k], z_in.at[chunk, k], z_send.at[chunk, k], z_recv.at[chunk, k], z_at(k)
        )

    def y_copy(chunk, m):
        return remote(
            y_in.at[chunk, 0], y_in.at[chunk, m], y_send.at[chunk, m], y_recv.at[chunk, m], y_at(m)
        )

    def b_copy(chunk, k):
        return remote(
            back_out.at[chunk, k], back_in.at[chunk, k], b_send.at[chunk, k], b_recv.at[chunk, k], z_at(k)
        )

    def r_copy(chunk, k):
        piece = x * Z_SIZE + (z + Z_SIZE - k) % Z_SIZE
        return remote(
            x_out.at[chunk, k], result.at[chunk // 2, piece, head_rows(chunk)],
            r_send.at[chunk, k], r_recv.at[chunk, k], other,
        )

    def dx_copy():
        rows = pl.ds((1 - x) * Z_SIZE, Z_SIZE)
        return remote(d_own.at[rows], d_x, dx_send.at[0], dx_recv.at[0], other)

    def dz_copy(k):
        return remote(d_t.at[k], d_z.at[k], dz_send.at[k], dz_recv.at[k], z_at(k))

    def dy_copy(m):
        return remote(d_y.at[0], d_y.at[m], dy_send.at[m], dy_recv.at[m], y_at(m))


    decays = decay[...]
    lower_all = (iota((toks, toks), 1) <= iota((toks, toks), 0)).astype(F32)
    cum_all = dot(lower_all, decays, NT, HIGHEST)
    factors = (two_parts(jnp.exp(cum_all[toks - 1 : toks, :] - cum_all)), two_parts(jnp.exp(cum_all)))
    sources = (conv, grad)
    total_all = jnp.exp(dot(decays, jnp.ones((toks, STATE), F32), NN, HIGHEST))
    expand = (iota((heads * 4, heads), 0) // 4 == iota((heads * 4, heads), 1)).astype(F32)
    d_own[...] = dot(expand, total_all, NN, HIGHEST).reshape(heads // 2, 8, STATE)

    def summarize(way, half):
        chunk = 8 * HEAD
        for piece in range(heads // 2 * HEAD // chunk):
            first = half * (heads // 2 * HEAD) + piece * chunk
            columns = pl.ds(pl.multiple_of(first, chunk), chunk)
            lanes = head_lanes(half * (heads // 2) + piece * 8, heads, chunk, HEAD)
            weighted = (widen(factors[way], lanes) * sources[way][:, columns].astype(F32)).astype(BF16)
            made = dot(weighted, maps[:, way * STATE : (way + 1) * STATE], TN)
            own[way, pl.ds(half * Z_SIZE + piece * 4, 4)] = made.reshape(4, PAIR, STATE)

    summarize(0, 1 - x)
    pl.semaphore_wait(barrier, len(partners))
    dx_copy().start()
    for chunk in range(2):
        for step in range(Z_SIZE):
            x_copy(chunk, order(step)).start()
    summarize(1, 1 - x)
    for chunk in range(2, CHUNKS):
        for step in range(Z_SIZE):
            x_copy(chunk, order(step)).start()
    summarize(0, x)
    summarize(1, x)


    causal = iota(square, 1) <= iota(square, 0)
    lower = causal.astype(F32)
    cum_parts, to_end, from_start, scores = [], [], [], []
    for block in range(count):
        rows = blocks[block]
        local = decay[:, rows]
        cum = dot(lower, local, NT, HIGHEST)
        high, middle = two_parts(cum)
        low = (cum - high.astype(F32) - middle.astype(F32)).astype(BF16)
        cum_parts.append((high, middle, low))
        to_end.append(two_parts(jnp.exp(cum[BLOCK - 1 : BLOCK, :] - cum)))
        from_start.append(two_parts(jnp.exp(cum)))
        cum_rows[block] = jnp.broadcast_to(dot(local, lower, NT, HIGHEST)[:, None, :], (heads, 8, BLOCK))
        whole = jnp.exp(dot(local, jnp.ones((BLOCK, STATE), F32), NN, HIGHEST))
        total_rows[block] = jnp.broadcast_to(whole[:, None, :], (heads, 8, STATE))
        scores.append(dot(maps[rows, STATE:], maps[rows, :STATE], NT))
    change[...] = jnp.zeros_like(change)
    mix[...] = jnp.zeros_like(mix)
    flow[...] = jnp.zeros_like(flow)

    def inside(index):
        columns = pl.ds(pl.multiple_of(index * width, width), width)
        pair_slices = pl.ds(index * 2, 2)
        lanes = head_lanes(index * 4, heads, width, HEAD)
        broad = head_lanes(index * 4, heads, 4 * BLOCK, BLOCK)
        in_first = iota((BLOCK, PAIR), 1) < HEAD
        for block in range(count):
            rows = blocks[block]
            xs, gs = conv[rows, columns], grad[rows, columns]
            te, fs = widen(to_end[block], lanes), widen(from_start[block], lanes)
            wide[0, rows, columns] = fs
            wide[1, rows, columns] = te
            xw = (te * xs.astype(F32)).astype(BF16)
            gw = (fs * gs.astype(F32)).astype(BF16)
            weighed[0, rows, columns] = gw
            weighed[1, rows, columns] = xw
            finals[block, pair_slices] = dot(xw, maps[rows, :STATE], TN).reshape(2, PAIR, STATE)
            if block:
                backs[block - 1, pair_slices] = dot(gw, maps[rows, STATE:], TN).reshape(2, PAIR, STATE)
            column = sum(dot(piece, broad) for piece in cum_parts[block])
            y_parts, d_parts, mixed = [], [], None
            for pair in range(2):
                lane = slice(pair * PAIR, (pair + 1) * PAIR)
                x_pair, g_pair = xs[:, lane], gs[:, lane]
                zero = jnp.zeros_like(x_pair)
                x_own = [jnp.where(in_first, x_pair, zero), jnp.where(in_first, zero, x_pair)]
                g_own = [jnp.where(in_first, g_pair, zero), jnp.where(in_first, zero, g_pair)]
                weights = []
                for one in range(2):
                    head = 2 * pair + one
                    col = column[:, head * BLOCK : (head + 1) * BLOCK].reshape(16, 8, BLOCK)
                    gap = (col - cum_rows[block, index * 4 + head][None]).reshape(square)
                    falls = jnp.exp(jnp.where(causal, gap, -1e30))
                    term = falls * dot(g_own[one], x_pair, NT)
                    weights.append((falls * scores[block]).astype(BF16))
                    mixed = term if mixed is None else mixed + term
                y_parts.append(dot(jnp.concatenate(weights, axis=1), jnp.concatenate(x_own, axis=0)))
                d_parts.append(dot(jnp.concatenate(weights, axis=0), jnp.concatenate(g_own, axis=0), TN))
            mix[block] += mixed
            inner_out[0, rows, columns] = jnp.concatenate(y_parts, axis=1)
            inner_out[1, rows, columns] = jnp.concatenate(d_parts, axis=1)


    def pass_decays():
        dx_copy().wait_recv()
        for step in range(Z_SIZE):
            k = order(step)
            piece = (z + k) % Z_SIZE
            target = d_t.at[k] if k else d_z.at[0]
            target[...] = d_own[x * Z_SIZE + piece] * d_x[piece]
            if k:
                dz_copy(k).start()

    def scan_decays():
        for k in range(1, Z_SIZE):
            dz_copy(k).wait_recv()
        for way in range(2):
            fade = jnp.ones((8, STATE), F32)
            for step in range(Z_SIZE):
                at = Z_SIZE - 1 - step if way else step
                d_before[way, (at + Z_SIZE - z) % Z_SIZE] = fade
                fade = fade * d_z[(z + Z_SIZE - at) % Z_SIZE]
        d_y[0] = fade
        for m in (2, 1, 3):
            dy_copy(m).start()

    def join(chunk, step):
        way, part, rows = chunk // 2, chunk % 2, head_rows(chunk)
        k = order(step)
        first = x == way
        x_copy(chunk, k).wait_recv()
        piece = (z + k) % Z_SIZE
        mine = own[way, x * Z_SIZE + piece, rows]
        theirs = x_in[way, piece, rows]
        early = jnp.where(first, mine, theirs)
        late = jnp.where(first, theirs, mine)
        fade = pick(jnp.where(first, d_x[piece], d_own[x * Z_SIZE + piece]), part)
        t_out[chunk, k] = fade * early + late

        @pl.when(step < Z_SIZE - 1)
        def _():
            z_copy(chunk, k).start()

    def scan(chunk):
        way, part = chunk // 2, chunk % 2
        for step in range(Z_SIZE - 1):
            z_copy(chunk, order(step)).wait_recv()
        z_in[chunk, 0] = t_out[chunk, 0]
        state = jnp.zeros((HEAD, STATE), F32)
        for step in range(Z_SIZE):
            at = step + way * (Z_SIZE - 1 - 2 * step)
            slot = (z + Z_SIZE - at) % Z_SIZE
            before[chunk, (at + Z_SIZE - z) % Z_SIZE] = state
            state = pick(d_z[slot], part) * state + z_in[chunk, slot]
        y_in[chunk, 0] = state
        for m in (2, 1, 3):
            y_copy(chunk, m).start()

    def spread(chunk):
        way, part = chunk // 2, chunk % 2
        for m in range(1, Y_SIZE):
            y_copy(chunk, m).wait_recv()
        state = jnp.zeros((HEAD, STATE), F32)
        for step in range(Y_SIZE):
            at = step + way * (Y_SIZE - 1 - 2 * step)
            slot = (y + Y_SIZE - at) % Y_SIZE
            counts = (at - y) * (1 - 2 * way) < 0
            state = jnp.where(counts, pick(d_y[slot], part) * state + y_in[chunk, slot], state)
        for step in range(Z_SIZE):
            k = order(step)
            target = back_out.at[chunk, k] if k else back_in.at[chunk, 0]
            target[...] = before[chunk, k] + pick(d_before[way, k], part) * state
            if k:
                b_copy(chunk, k).start()

    def hand_on(chunk, step):
        way, part, rows = chunk // 2, chunk % 2, head_rows(chunk)
        k = order(Z_SIZE - 1 - step)
        first = x == way

        @pl.when(step > 0)
        def _():
            b_copy(chunk, k).wait_recv()

        piece = (z + Z_SIZE - k) % Z_SIZE
        early = back_in[chunk, k]
        left = jnp.where(first, own[way, x * Z_SIZE + piece, rows], x_in[way, piece, rows])
        fade = pick(jnp.where(first, d_own[x * Z_SIZE + piece], d_x[piece]), part)
        late = fade * early + left
        x_out[chunk, k] = jnp.where(first, late, early)
        result[way, x * Z_SIZE + piece, rows] = jnp.where(first, early, late)
        r_copy(chunk, k).start()


    def fade_rows(block, index, state):
        tiles = total_rows[block, pl.ds(index * 2, 2)][:, None]
        return (state.reshape(2, 8, 8, STATE) * tiles).reshape(PAIR, STATE)

    def add_change(block, index, product):
        lanes = head_lanes(index * 2, heads, PAIR, HEAD)
        high, low = two_parts(product)
        change[block] += dot(lanes, high, NT) + dot(lanes, low, NT)

    def with_start(index):
        columns = pl.ds(pl.multiple_of(index * PAIR, PAIR), PAIR)
        state = result[0, index]
        for block in range(count):
            rows = blocks[block]
            low = state.astype(BF16)
            flow[0, block] += dot(weighed[0, rows, columns], low)
            outputs = inner_out[0, rows, columns] + wide[0, rows, columns] * dot(maps[rows, STATE:], low, NT)
            add_change(block, index, grad[rows, columns].astype(F32) * outputs)
            state = fade_rows(block, index, state) + finals[block, index]
            states[block, index] = state

    def with_finish(index):
        columns = pl.ds(pl.multiple_of(index * PAIR, PAIR), PAIR)
        state = result[1, index]
        for block in reversed(range(count)):
            rows = blocks[block]
            ends[block, pl.ds(index * 2, 2)] = jnp.sum(
                (state * states[block, index]).reshape(2, 8, 8, STATE), axis=1
            )
            low = state.astype(BF16)
            flow[1, block] += dot(weighed[1, rows, columns], low)
            inputs = inner_out[1, rows, columns] + wide[1, rows, columns] * dot(maps[rows, :STATE], low, NT)
            grad_conv[rows, columns] = inputs.astype(BF16)
            add_change(block, index, conv[rows, columns].astype(F32) * -inputs)
            if block:
                state = fade_rows(block, index, state) + backs[block - 1, index]


    share = toks // 4
    mine = pl.ds(pl.multiple_of(dp * share, share), share)

    def p_copy(half, m):
        rows = pl.ds(pl.multiple_of((dp + m) % 4 * share, share), share)
        return remote(
            part.at[half, rows], gathered.at[half, m], p_send.at[half, m], p_recv.at[half, m], p_at(m)
        )

    def g_copy(half, m):
        return remote(
            total.at[half, mine], total.at[half, mine], g_send.at[half, m], g_recv.at[half, m], p_at(m)
        )

    def sum_begin(half):
        for block in range(count):
            rows = blocks[block]
            if half:
                made = dot(mix[block], maps[rows, STATE:].astype(F32), TN, HIGHEST)
            else:
                made = dot(mix[block], maps[rows, :STATE].astype(F32), NN, HIGHEST)
            part[half, rows] = made + flow[half, block]
        for m in range(1, 4):
            p_copy(half, m).start()

    def sum_middle(half):
        for m in range(1, 4):
            p_copy(half, m).wait_recv()
        total[half, mine] = part[half, mine] + gathered[half, 1] + gathered[half, 2] + gathered[half, 3]
        for m in range(1, 4):
            g_copy(half, m).start()

    def sum_end(half):
        for m in range(1, 4):
            g_copy(half, m).wait_recv()
        made = total[half]
        grad_maps[:, (1 - half) * STATE : (2 - half) * STATE] = made
        return made.astype(BF16)


    by_y, ry_in, ry_sum, rz_late = (by_y0, by_y1), (ry_in0, ry_in1), (ry_sum0, ry_sum1), (rz_late0, rz_late1)
    splits = (0, z_rows)

    def ry_copy(half, m):
        return remote(
            by_y[half].at[(y + m) % Y_SIZE], ry_in[half].at[m], ry_send.at[half, m], ry_recv.at[half, m], y_at(m)
        )

    def rzl_copy(half, k):
        return remote(
            ry_sum[half].at[(z + k) % Z_SIZE], rz_late[half].at[k],
            rzl_send.at[half, k], rzl_recv.at[half, k], z_at(k),
        )

    def rz_copy(k):
        return remote(by_z.at[(z + k) % Z_SIZE], rz_in.at[k], rz_send.at[k], rz_recv.at[k], z_at(k))

    def ryl_copy(m):
        return remote(
            rz_sum.at[(y + m) % Y_SIZE], ry_late.at[m], ryl_send.at[m], ryl_recv.at[m], y_at(m)
        )

    def rx_copy(half):
        return remote(
            rx_own.at[half, 1 - x], rx_in.at[half], rx_send.at[half], rx_recv.at[half], other
        )

    def weigh(half, low):
        cut = splits[half]
        for piece in range(Y_SIZE):
            made = dot(flipped[piece], low) * scale
            made = made.reshape(Z_SIZE, 2, -1, STATE)
            by_y[half][piece] = made[:, :, cut:]
            if cut:
                by_z[:, piece] = made[:, :, :cut]
        if cut:
            for step in range(3):
                rz_copy(order(step)).start()
        for m in (2, 1, 3):
            ry_copy(half, m).start()
        if cut:
            for step in range(3, Z_SIZE - 1):
                rz_copy(order(step)).start()

    def weigh_middle(half):
        for m in range(1, Y_SIZE):
            ry_copy(half, m).wait_recv()
        ry_sum[half][...] = by_y[half][y] + ry_in[half][1] + ry_in[half][2] + ry_in[half][3]
        for step in range(Z_SIZE - 1):
            rzl_copy(half, order(step)).start()

    def weigh_middle_z():
        for k in range(1, Z_SIZE):
            rz_copy(k).wait_recv()
        rz_sum[...] = by_z[z] + sum(rz_in[k] for k in range(1, Z_SIZE))
        for m in (2, 1, 3):
            ryl_copy(m).start()

    def weigh_late(half):
        cut = splits[half]
        if cut:
            for m in range(1, Y_SIZE):
                ryl_copy(m).wait_recv()
            rx_own[half, :, :cut] = rz_sum[y] + sum(ry_late[m] for m in range(1, Y_SIZE))
        for k in range(1, Z_SIZE):
            rzl_copy(half, k).wait_recv()
        rx_own[half, :, cut:] = ry_sum[half][z] + sum(rz_late[half][k] for k in range(1, Z_SIZE))
        rx_copy(half).start()

    def weigh_end(half):
        rx_copy(half).wait_recv()
        weight[:, (1 - half) * STATE : (2 - half) * STATE] = rx_own[half, x] + rx_in[half]


    def done(turn):
        return jnp.where(turn == 0, 0, jnp.minimum(turn + 1, heads * HEAD // width))

    def joins(turn, _):
        chunk = turn // 2

        def one_join(step, _):
            join(chunk, step)
            return 0

        def one_group(index, _):
            inside(index)
            return 0

        lax.fori_loop(turn % 2 * 4, turn % 2 * 4 + 4, one_join, 0)
        lax.fori_loop(done(turn), done(turn + 1), one_group, 0)

        @pl.when(turn == 1)
        def _():
            scan_decays()

        @pl.when(turn == 3)
        def _():
            for m in range(1, Y_SIZE):
                dy_copy(m).wait_recv()

        @pl.when(jnp.logical_and(turn >= 2, turn % 2 == 0))
        def _():
            scan(chunk - 1)

        @pl.when(jnp.logical_and(turn >= 3, turn % 2 == 1))
        def _():
            spread(chunk - 1)

        return 0

    def nearest(step):
        return order(Z_SIZE - 1 - step)

    def piece_of(half, step):
        return half * Z_SIZE + (z + Z_SIZE - nearest(step)) % Z_SIZE

    def first_chunk(step, _):
        hand_on(0, step)
        return 0

    def second_chunk(step, _):
        hand_on(1, step)
        with_start(piece_of(x, step))

        @pl.when(step == 3)
        def _():
            spread(3)

        return 0

    def third_chunk(step, _):
        hand_on(2, step)
        r_copy(0, nearest(step)).wait_recv()
        r_copy(1, nearest(step)).wait_recv()
        with_start(piece_of(1 - x, step))
        return 0

    def last_chunk(step, _):
        hand_on(3, step)
        with_finish(piece_of(x, step))

        @pl.when(step == 3)
        def _():
            sum_middle(0)

        return 0

    def others_last(step, _):
        r_copy(2, nearest(step)).wait_recv()
        r_copy(3, nearest(step)).wait_recv()
        with_finish(piece_of(1 - x, step))
        return 0

    pass_decays()
    lax.fori_loop(0, Z_SIZE, joins, 0)
    lax.fori_loop(0, Z_SIZE, first_chunk, 0)
    span = layer.shape[1] // Y_SIZE
    for piece in range(Y_SIZE):
        flipped[piece] = layer[:, piece * span : (piece + 1) * span].T
    scan(3)
    lax.fori_loop(0, Z_SIZE, second_chunk, 0)
    lax.fori_loop(0, Z_SIZE, third_chunk, 0)
    sum_begin(0)
    lax.fori_loop(0, Z_SIZE, last_chunk, 0)
    low = sum_end(0)
    weigh(0, low)
    lax.fori_loop(0, Z_SIZE, others_last, 0)
    sum_begin(1)
    sum_middle(1)
    low = sum_end(1)
    weigh(1, low)
    for block in range(count):
        end_term = jnp.sum(jnp.sum(ends[block], axis=1), axis=1, keepdims=True)
        at_last = iota((heads, BLOCK), 1) == BLOCK - 1
        changes = change[block] + jnp.where(at_last, end_term, 0.0)
        grad_decay[:, blocks[block]] = dot(changes, lower, NN, HIGHEST)
    weigh_middle(0)
    weigh_middle_z()
    weigh_middle(1)
    weigh_late(0)
    weigh_late(1)
    weigh_end(0)
    weigh_end(1)

    dx_copy().wait_send()
    for chunk in range(CHUNKS):
        for k in range(Z_SIZE):
            x_copy(chunk, k).wait_send()
            r_copy(chunk, k).wait_send()
            if k:
                z_copy(chunk, k).wait_send()
                b_copy(chunk, k).wait_send()
        for m in range(1, Y_SIZE):
            y_copy(chunk, m).wait_send()
    for k in range(1, Z_SIZE):
        dz_copy(k).wait_send()
        rz_copy(k).wait_send()
        for half in range(2):
            rzl_copy(half, k).wait_send()
    for m in range(1, 4):
        dy_copy(m).wait_send()
        ryl_copy(m).wait_send()
        for half in range(2):
            p_copy(half, m).wait_send()
            g_copy(half, m).wait_send()
            ry_copy(half, m).wait_send()
    for half in range(2):
        rx_copy(half).wait_send()


def dma(*shape):
    return pltpu.SemaphoreType.DMA(shape)


def hand_out_kernel(a, b, c, d, a_out, b_out, c_out, d_out, sems):
    pairs = ((a, a_out), (b, b_out), (c, c_out), (d, d_out))
    copies = [pltpu.make_async_copy(one, out, sems.at[i]) for i, (one, out) in enumerate(pairs)]
    for copy in copies:
        copy.start()
    for copy in copies:
        copy.wait()


def on_device(layer_input, conv_output, state_maps, log_decay, out_grad):
    toks, columns = conv_output.shape
    heads = log_decay.shape[0]
    slices = heads // 2
    count = toks // BLOCK
    tile = columns // (Y_SIZE * Z_SIZE * 2)
    z_rows = 8
    late = tile - z_rows

    def floats(*shape):
        return pltpu.VMEM(shape, F32)

    grad_conv, grad_maps, grad_decay, grad_weight = pl.pallas_call(
        functools.partial(kernel, 1.0 / math.sqrt(toks * lax.axis_size("ctx")), z_rows),
        out_shape=(
            jax.ShapeDtypeStruct((toks, columns), BF16),
            jax.ShapeDtypeStruct((toks, 2 * STATE), F32),
            jax.ShapeDtypeStruct((heads, toks), F32),
            jax.ShapeDtypeStruct((tile, 2 * STATE), F32),
        ),
        in_specs=[VMEM] * 5,
        out_specs=(VMEM,) * 4,
        scratch_shapes=[
            floats(2, slices, PAIR, STATE),
            floats(2, Z_SIZE, PAIR, STATE),
            floats(CHUNKS, Z_SIZE, HEAD, STATE),
            floats(CHUNKS, Z_SIZE, HEAD, STATE),
            floats(CHUNKS, Y_SIZE, HEAD, STATE),
            floats(CHUNKS, Z_SIZE, HEAD, STATE),
            floats(CHUNKS, Z_SIZE, HEAD, STATE),
            floats(CHUNKS, Z_SIZE, HEAD, STATE),
            floats(CHUNKS, Z_SIZE, HEAD, STATE),
            floats(2, slices, PAIR, STATE),
            floats(slices, 8, STATE),
            floats(Z_SIZE, 8, STATE),
            floats(Z_SIZE, 8, STATE),
            floats(Z_SIZE, 8, STATE),
            floats(Y_SIZE, 8, STATE),
            floats(2, Z_SIZE, 8, STATE),
            floats(count, heads, 8, BLOCK),
            floats(count, heads, 8, STATE),
            floats(count, heads, BLOCK),
            floats(count, heads, 8, STATE),
            floats(count, BLOCK, BLOCK),
            floats(2, count, BLOCK, STATE),
            floats(2, toks, columns),
            pltpu.VMEM((2, toks, columns), BF16),
            floats(2, toks, columns),
            floats(count, slices, PAIR, STATE),
            floats(max(count - 1, 1), slices, PAIR, STATE),
            floats(count, slices, PAIR, STATE),
            floats(2, toks, STATE),
            floats(2, 4, toks // 4, STATE),
            floats(2, toks, STATE),
            pltpu.VMEM((Y_SIZE, columns // Y_SIZE, toks), BF16),
            floats(Y_SIZE, Z_SIZE, 2, tile, STATE),
            floats(Y_SIZE, Z_SIZE, 2, late, STATE),
            floats(Z_SIZE, Y_SIZE, 2, z_rows, STATE),
            floats(Y_SIZE, Z_SIZE, 2, tile, STATE),
            floats(Y_SIZE, Z_SIZE, 2, late, STATE),
            floats(Z_SIZE, Y_SIZE, 2, z_rows, STATE),
            floats(Z_SIZE, 2, tile, STATE),
            floats(Z_SIZE, 2, late, STATE),
            floats(Y_SIZE, 2, z_rows, STATE),
            floats(Z_SIZE, 2, tile, STATE),
            floats(Z_SIZE, 2, late, STATE),
            floats(Y_SIZE, 2, z_rows, STATE),
            floats(2, 2, tile, STATE),
            floats(2, tile, STATE),
            dma(CHUNKS, Z_SIZE), dma(CHUNKS, Z_SIZE), dma(CHUNKS, Z_SIZE), dma(CHUNKS, Z_SIZE),
            dma(CHUNKS, Y_SIZE), dma(CHUNKS, Y_SIZE), dma(CHUNKS, Z_SIZE), dma(CHUNKS, Z_SIZE),
            dma(CHUNKS, Z_SIZE), dma(CHUNKS, Z_SIZE),
            dma(1), dma(1), dma(Z_SIZE), dma(Z_SIZE), dma(Y_SIZE), dma(Y_SIZE),
            dma(2, 4), dma(2, 4), dma(2, 4), dma(2, 4),
            dma(2, Y_SIZE), dma(2, Y_SIZE), dma(Z_SIZE), dma(Z_SIZE),
            dma(2, Z_SIZE), dma(2, Z_SIZE), dma(Y_SIZE), dma(Y_SIZE),
            dma(2), dma(2),
        ],
        compiler_params=pltpu.CompilerParams(
            collective_id=0, has_side_effects=True, vmem_limit_bytes=LIMIT
        ),
        name="backward",
    )(conv_output, out_grad, state_maps, log_decay, layer_input)
    results = (grad_conv, grad_maps, grad_decay, grad_weight)
    return pl.pallas_call(
        hand_out_kernel,
        out_shape=tuple(jax.ShapeDtypeStruct(one.shape, one.dtype) for one in results),
        in_specs=[VMEM] * 4,
        out_specs=(pl.BlockSpec(memory_space=pl.ANY),) * 4,
        scratch_shapes=[dma(4)],
        name="hand_out",
    )(*results)


def solution(mesh):
    placed = (P("ctx", "dp"), P("ctx", "dp"), P("ctx", None), P("dp", "ctx"), P("ctx", "dp"))
    return jax.shard_map(
        on_device,
        mesh=mesh,
        in_specs=placed,
        out_specs=(P("ctx", "dp"), P("ctx", None), P("dp", "ctx"), P(("dp", "ctx"), None)),
        check_vma=False,
    )
```

```python
import functools
import math

import jax
import jax.numpy as jnp
from jax import lax
from jax.experimental import pallas as pl
from jax.experimental.pallas import tpu as pltpu
from jax.sharding import PartitionSpec as P

BLOCK = 128
HEAD = 64
STATE = 128
PAIR = 2 * HEAD
CHUNKS = 4
Z_SIZE = 8
Y_SIZE = 4
MESH = pl.DeviceIdType.MESH
F32 = jnp.float32
BF16 = jnp.bfloat16
HIGHEST = lax.Precision.HIGHEST
NT = (((1,), (1,)), ((), ()))
TN = (((0,), (0,)), ((), ()))
NN = (((1,), (0,)), ((), ()))
VMEM = pl.BlockSpec(memory_space=pltpu.VMEM)
LIMIT = 56 * 1024 * 1024


def dot(a, b, dims=NN, precision=None):
    return lax.dot_general(a, b, dims, precision=precision, preferred_element_type=F32)


def iota(shape, axis):
    return lax.broadcasted_iota(jnp.int32, shape, axis)


def two_parts(values):
    high = values.astype(BF16)
    return high, (values - high.astype(F32)).astype(BF16)


def head_lanes(first_head, head_count, columns, width):
    shape = (head_count, columns)
    return (iota(shape, 0) == first_head + iota(shape, 1) // width).astype(BF16)


def widen(parts, lanes):
    return dot(parts[0], lanes) + dot(parts[1], lanes)


def place():
    dp, ctx = lax.axis_index("dp"), lax.axis_index("ctx")
    return dp, ctx // (2 * Z_SIZE), (ctx // 2) % Z_SIZE, ctx % 2


def device(dp, y, z, x):
    return (dp, (y * Z_SIZE + z) * 2 + x)


def remote(src, dst, send, recv, target):
    return pltpu.make_async_remote_copy(
        src_ref=src, dst_ref=dst, send_sem=send, recv_sem=recv, device_id=target, device_id_type=MESH
    )


def pick(tile, part):
    return jnp.where(part == 0, tile[0:1], tile[4:5])


def order(step):
    odd = step % 2
    return Z_SIZE // 2 + (step // 2) * (1 - odd) - ((step + 1) // 2) * odd


def kernel(
    scale, splits,
    conv, grad, maps, decay, layer, grad_conv, grad_maps, grad_decay, weight,
    own, x_in, t_out, z_in, y_in, before, back_out, back_in, x_out, result,
    d_own, d_x, d_t, d_z, d_y, d_before,
    cum_rows, total_rows, change, ends, mix, flow, wide, weighed, inner_out, finals, backs, states,
    part, gathered, total, flipped, by_y, by_x, by_z,
    ry_in, rx_in, rz_in, ry_sum, rx_sum, rz_sum, rz_late, ry_late, ry_next, ry_total, rz_next,
    rl_own, rl_in,
    x_send, x_recv, z_send, z_recv, y_send, y_recv, b_send, b_recv, r_send, r_recv,
    dx_send, dx_recv, dz_send, dz_recv, dy_send, dy_recv,
    p_send, p_recv, g_send, g_recv, ry_send, ry_recv, rz_send, rz_recv,
    rx_send, rx_recv, rzl_send, rzl_recv, ryl_send, ryl_recv, ryn_send, ryn_recv, rzn_send, rzn_recv,
    rl_send, rl_recv,
):
    dp, y, z, x = place()
    other = device(dp, y, z, 1 - x)

    def z_at(k):
        return device(dp, y, (z + k) % Z_SIZE, x)

    def y_at(m):
        return device(dp, (y + m) % Y_SIZE, z, x)

    def p_at(m):
        return device((dp + m) % 4, y, z, x)

    partners = [other] + [z_at(k) for k in range(1, Z_SIZE)]
    partners += [y_at(m) for m in range(1, Y_SIZE)] + [p_at(m) for m in range(1, 4)]
    barrier = pltpu.get_barrier_semaphore()
    for partner in partners:
        pl.semaphore_signal(barrier, inc=1, device_id=partner, device_id_type=MESH)

    heads, toks = decay.shape
    count = toks // BLOCK
    width = 4 * HEAD
    square = (BLOCK, BLOCK)
    blocks = [slice(block * BLOCK, (block + 1) * BLOCK) for block in range(count)]


    def head_rows(chunk):
        return pl.ds(pl.multiple_of(chunk % 2 * HEAD, HEAD), HEAD)

    def x_copy(chunk, k):
        piece, rows = (z + k) % Z_SIZE, head_rows(chunk)
        return remote(
            own.at[chunk // 2, (1 - x) * Z_SIZE + piece, rows], x_in.at[chunk // 2, piece, rows],
            x_send.at[chunk, k], x_recv.at[chunk, k], other,
        )

    def z_copy(chunk, k):
        return remote(
            t_out.at[chunk, k], z_in.at[chunk, k], z_send.at[chunk, k], z_recv.at[chunk, k], z_at(k)
        )

    def y_copy(chunk, m):
        return remote(
            y_in.at[chunk, 0], y_in.at[chunk, m], y_send.at[chunk, m], y_recv.at[chunk, m], y_at(m)
        )

    def b_copy(chunk, k):
        return remote(
            back_out.at[chunk, k], back_in.at[chunk, k], b_send.at[chunk, k], b_recv.at[chunk, k], z_at(k)
        )

    def r_copy(chunk, k):
        piece = x * Z_SIZE + (z + Z_SIZE - k) % Z_SIZE
        return remote(
            x_out.at[chunk, k], result.at[chunk // 2, piece, head_rows(chunk)],
            r_send.at[chunk, k], r_recv.at[chunk, k], other,
        )

    def dx_copy():
        rows = pl.ds((1 - x) * Z_SIZE, Z_SIZE)
        return remote(d_own.at[rows], d_x, dx_send.at[0], dx_recv.at[0], other)

    def dz_copy(k):
        return remote(d_t.at[k], d_z.at[k], dz_send.at[k], dz_recv.at[k], z_at(k))

    def dy_copy(m):
        return remote(d_y.at[0], d_y.at[m], dy_send.at[m], dy_recv.at[m], y_at(m))


    decays = decay[...]
    lower_all = (iota((toks, toks), 1) <= iota((toks, toks), 0)).astype(F32)
    cum_all = dot(lower_all, decays, NT, HIGHEST)
    factors = (two_parts(jnp.exp(cum_all[toks - 1 : toks, :] - cum_all)), two_parts(jnp.exp(cum_all)))
    sources = (conv, grad)
    total_all = jnp.exp(dot(decays, jnp.ones((toks, STATE), F32), NN, HIGHEST))
    expand = (iota((heads * 4, heads), 0) // 4 == iota((heads * 4, heads), 1)).astype(F32)
    d_own[...] = dot(expand, total_all, NN, HIGHEST).reshape(heads // 2, 8, STATE)

    def summarize(way, half):
        chunk = 8 * HEAD
        for piece in range(heads // 2 * HEAD // chunk):
            first = half * (heads // 2 * HEAD) + piece * chunk
            columns = pl.ds(pl.multiple_of(first, chunk), chunk)
            lanes = head_lanes(half * (heads // 2) + piece * 8, heads, chunk, HEAD)
            weighted = (widen(factors[way], lanes) * sources[way][:, columns].astype(F32)).astype(BF16)
            made = dot(weighted, maps[:, way * STATE : (way + 1) * STATE], TN)
            own[way, pl.ds(half * Z_SIZE + piece * 4, 4)] = made.reshape(4, PAIR, STATE)

    summarize(0, 1 - x)
    pl.semaphore_wait(barrier, len(partners))
    dx_copy().start()
    for chunk in range(2):
        for step in range(Z_SIZE):
            x_copy(chunk, order(step)).start()
    summarize(1, 1 - x)
    for chunk in range(2, CHUNKS):
        for step in range(Z_SIZE):
            x_copy(chunk, order(step)).start()
    summarize(0, x)
    summarize(1, x)


    causal = iota(square, 1) <= iota(square, 0)
    lower = causal.astype(F32)
    cum_parts, to_end, from_start, scores = [], [], [], []
    for block in range(count):
        rows = blocks[block]
        local = decay[:, rows]
        cum = dot(lower, local, NT, HIGHEST)
        high, middle = two_parts(cum)
        low = (cum - high.astype(F32) - middle.astype(F32)).astype(BF16)
        cum_parts.append((high, middle, low))
        to_end.append(two_parts(jnp.exp(cum[BLOCK - 1 : BLOCK, :] - cum)))
        from_start.append(two_parts(jnp.exp(cum)))
        cum_rows[block] = jnp.broadcast_to(dot(local, lower, NT, HIGHEST)[:, None, :], (heads, 8, BLOCK))
        whole = jnp.exp(dot(local, jnp.ones((BLOCK, STATE), F32), NN, HIGHEST))
        total_rows[block] = jnp.broadcast_to(whole[:, None, :], (heads, 8, STATE))
        scores.append(dot(maps[rows, STATE:], maps[rows, :STATE], NT))
    change[...] = jnp.zeros_like(change)
    mix[...] = jnp.zeros_like(mix)
    flow[...] = jnp.zeros_like(flow)

    def inside(index):
        columns = pl.ds(pl.multiple_of(index * width, width), width)
        pair_slices = pl.ds(index * 2, 2)
        lanes = head_lanes(index * 4, heads, width, HEAD)
        broad = head_lanes(index * 4, heads, 4 * BLOCK, BLOCK)
        in_first = iota((BLOCK, PAIR), 1) < HEAD
        for block in range(count):
            rows = blocks[block]
            xs, gs = conv[rows, columns], grad[rows, columns]
            te, fs = widen(to_end[block], lanes), widen(from_start[block], lanes)
            wide[0, rows, columns] = fs
            wide[1, rows, columns] = te
            xw = (te * xs.astype(F32)).astype(BF16)
            gw = (fs * gs.astype(F32)).astype(BF16)
            weighed[0, rows, columns] = gw
            weighed[1, rows, columns] = xw
            finals[block, pair_slices] = dot(xw, maps[rows, :STATE], TN).reshape(2, PAIR, STATE)
            if block:
                backs[block - 1, pair_slices] = dot(gw, maps[rows, STATE:], TN).reshape(2, PAIR, STATE)
            column = sum(dot(piece, broad) for piece in cum_parts[block])
            y_parts, d_parts, mixed = [], [], None
            for pair in range(2):
                lane = slice(pair * PAIR, (pair + 1) * PAIR)
                x_pair, g_pair = xs[:, lane], gs[:, lane]
                zero = jnp.zeros_like(x_pair)
                x_own = [jnp.where(in_first, x_pair, zero), jnp.where(in_first, zero, x_pair)]
                g_own = [jnp.where(in_first, g_pair, zero), jnp.where(in_first, zero, g_pair)]
                weights = []
                for one in range(2):
                    head = 2 * pair + one
                    col = column[:, head * BLOCK : (head + 1) * BLOCK].reshape(16, 8, BLOCK)
                    gap = (col - cum_rows[block, index * 4 + head][None]).reshape(square)
                    falls = jnp.exp(jnp.where(causal, gap, -1e30))
                    term = falls * dot(g_own[one], x_pair, NT)
                    weights.append((falls * scores[block]).astype(BF16))
                    mixed = term if mixed is None else mixed + term
                y_parts.append(dot(jnp.concatenate(weights, axis=1), jnp.concatenate(x_own, axis=0)))
                d_parts.append(dot(jnp.concatenate(weights, axis=0), jnp.concatenate(g_own, axis=0), TN))
            mix[block] += mixed
            inner_out[0, rows, columns] = jnp.concatenate(y_parts, axis=1)
            inner_out[1, rows, columns] = jnp.concatenate(d_parts, axis=1)


    def pass_decays():
        dx_copy().wait_recv()
        for step in range(Z_SIZE):
            k = order(step)
            piece = (z + k) % Z_SIZE
            target = d_t.at[k] if k else d_z.at[0]
            target[...] = d_own[x * Z_SIZE + piece] * d_x[piece]
            if k:
                dz_copy(k).start()

    def scan_decays():
        for k in range(1, Z_SIZE):
            dz_copy(k).wait_recv()
        for way in range(2):
            fade = jnp.ones((8, STATE), F32)
            for step in range(Z_SIZE):
                at = Z_SIZE - 1 - step if way else step
                d_before[way, (at + Z_SIZE - z) % Z_SIZE] = fade
                fade = fade * d_z[(z + Z_SIZE - at) % Z_SIZE]
        d_y[0] = fade
        for m in (2, 1, 3):
            dy_copy(m).start()

    def join(chunk, step):
        way, part, rows = chunk // 2, chunk % 2, head_rows(chunk)
        k = order(step)
        first = x == way
        x_copy(chunk, k).wait_recv()
        piece = (z + k) % Z_SIZE
        mine = own[way, x * Z_SIZE + piece, rows]
        theirs = x_in[way, piece, rows]
        early = jnp.where(first, mine, theirs)
        late = jnp.where(first, theirs, mine)
        fade = pick(jnp.where(first, d_x[piece], d_own[x * Z_SIZE + piece]), part)
        t_out[chunk, k] = fade * early + late

        @pl.when(step < Z_SIZE - 1)
        def _():
            z_copy(chunk, k).start()

    def scan(chunk):
        way, part = chunk // 2, chunk % 2
        for step in range(Z_SIZE - 1):
            z_copy(chunk, order(step)).wait_recv()
        z_in[chunk, 0] = t_out[chunk, 0]
        state = jnp.zeros((HEAD, STATE), F32)
        for step in range(Z_SIZE):
            at = step + way * (Z_SIZE - 1 - 2 * step)
            slot = (z + Z_SIZE - at) % Z_SIZE
            before[chunk, (at + Z_SIZE - z) % Z_SIZE] = state
            state = pick(d_z[slot], part) * state + z_in[chunk, slot]
        y_in[chunk, 0] = state
        for m in (2, 1, 3):
            y_copy(chunk, m).start()

    def spread(chunk):
        way, part = chunk // 2, chunk % 2
        for m in range(1, Y_SIZE):
            y_copy(chunk, m).wait_recv()
        state = jnp.zeros((HEAD, STATE), F32)
        for step in range(Y_SIZE):
            at = step + way * (Y_SIZE - 1 - 2 * step)
            slot = (y + Y_SIZE - at) % Y_SIZE
            counts = (at - y) * (1 - 2 * way) < 0
            state = jnp.where(counts, pick(d_y[slot], part) * state + y_in[chunk, slot], state)
        for step in range(Z_SIZE):
            k = order(step)
            target = back_out.at[chunk, k] if k else back_in.at[chunk, 0]
            target[...] = before[chunk, k] + pick(d_before[way, k], part) * state
            if k:
                b_copy(chunk, k).start()

    def hand_on(chunk, k):
        way, part, rows = chunk // 2, chunk % 2, head_rows(chunk)
        first = x == way

        @pl.when(k > 0)
        def _():
            b_copy(chunk, k).wait_recv()

        piece = (z + Z_SIZE - k) % Z_SIZE
        early = back_in[chunk, k]
        left = jnp.where(first, own[way, x * Z_SIZE + piece, rows], x_in[way, piece, rows])
        fade = pick(jnp.where(first, d_own[x * Z_SIZE + piece], d_x[piece]), part)
        late = fade * early + left
        x_out[chunk, k] = jnp.where(first, late, early)
        result[way, x * Z_SIZE + piece, rows] = jnp.where(first, early, late)
        r_copy(chunk, k).start()


    def fade_rows(block, index, state):
        tiles = total_rows[block, pl.ds(index * 2, 2)][:, None]
        return (state.reshape(2, 8, 8, STATE) * tiles).reshape(PAIR, STATE)

    def add_change(block, index, product):
        lanes = head_lanes(index * 2, heads, PAIR, HEAD)
        high, low = two_parts(product)
        change[block] += dot(lanes, high, NT) + dot(lanes, low, NT)

    def with_start(index):
        columns = pl.ds(pl.multiple_of(index * PAIR, PAIR), PAIR)
        state = result[0, index]
        for block in range(count):
            rows = blocks[block]
            low = state.astype(BF16)
            flow[0, block] += dot(weighed[0, rows, columns], low)
            outputs = inner_out[0, rows, columns] + wide[0, rows, columns] * dot(maps[rows, STATE:], low, NT)
            add_change(block, index, grad[rows, columns].astype(F32) * outputs)
            state = fade_rows(block, index, state) + finals[block, index]
            states[block, index] = state

    def with_finish(index):
        columns = pl.ds(pl.multiple_of(index * PAIR, PAIR), PAIR)
        state = result[1, index]
        for block in reversed(range(count)):
            rows = blocks[block]
            ends[block, pl.ds(index * 2, 2)] = jnp.sum(
                (state * states[block, index]).reshape(2, 8, 8, STATE), axis=1
            )
            low = state.astype(BF16)
            flow[1, block] += dot(weighed[1, rows, columns], low)
            inputs = inner_out[1, rows, columns] + wide[1, rows, columns] * dot(maps[rows, :STATE], low, NT)
            grad_conv[rows, columns] = inputs.astype(BF16)
            add_change(block, index, conv[rows, columns].astype(F32) * -inputs)
            if block:
                state = fade_rows(block, index, state) + backs[block - 1, index]


    share = toks // 4
    mine = pl.ds(pl.multiple_of(dp * share, share), share)

    def p_copy(half, m):
        rows = pl.ds(pl.multiple_of((dp + m) % 4 * share, share), share)
        return remote(
            part.at[half, rows], gathered.at[half, m], p_send.at[half, m], p_recv.at[half, m], p_at(m)
        )

    def g_copy(half, m):
        return remote(
            total.at[half, mine], total.at[half, mine], g_send.at[half, m], g_recv.at[half, m], p_at(m)
        )

    def sum_begin(half):
        for block in range(count):
            rows = blocks[block]
            if half:
                made = dot(mix[block], maps[rows, STATE:].astype(F32), TN, HIGHEST)
            else:
                made = dot(mix[block], maps[rows, :STATE].astype(F32), NN, HIGHEST)
            part[half, rows] = made + flow[half, block]
        for m in range(1, 4):
            p_copy(half, m).start()

    def sum_middle(half):
        for m in range(1, 4):
            p_copy(half, m).wait_recv()
        total[half, mine] = part[half, mine] + gathered[half, 1] + gathered[half, 2] + gathered[half, 3]
        for m in range(1, 4):
            g_copy(half, m).start()

    def sum_end(half):
        for m in range(1, 4):
            g_copy(half, m).wait_recv()
        made = total[half]
        grad_maps[:, (1 - half) * STATE : (2 - half) * STATE] = made
        return made.astype(BF16)


    def ry_copy(half, m):
        return remote(
            by_y[half].at[(y + m) % Y_SIZE], ry_in[half].at[m], ry_send.at[half, m], ry_recv.at[half, m], y_at(m)
        )

    def rx_copy():
        return remote(by_x.at[1 - x], rx_in, rx_send.at[0], rx_recv.at[0], other)

    def rz_copy(half, k):
        return remote(
            by_z[half].at[(z + k) % Z_SIZE], rz_in[half].at[k], rz_send.at[half, k], rz_recv.at[half, k], z_at(k)
        )

    def rzl_copy(half, k):
        return remote(
            ry_sum[half].at[(z + k) % Z_SIZE], rz_late[half].at[k],
            rzl_send.at[half, k], rzl_recv.at[half, k], z_at(k),
        )

    def ryl_copy(half, m):
        return remote(
            rz_sum[half].at[(y + m) % Y_SIZE], ry_late[half].at[m],
            ryl_send.at[half, m], ryl_recv.at[half, m], y_at(m),
        )

    def ryn_copy(m):
        return remote(
            rx_sum.at[(y + m) % Y_SIZE], ry_next.at[m], ryn_send.at[m], ryn_recv.at[m], y_at(m)
        )

    def rzn_copy(k):
        return remote(
            ry_total.at[(z + k) % Z_SIZE], rz_next.at[k], rzn_send.at[k], rzn_recv.at[k], z_at(k)
        )

    def rl_copy(half):
        return remote(
            rl_own[half].at[1 - x], rl_in[half], rl_send.at[half], rl_recv.at[half], other
        )

    def weigh(half, low):
        first, second, third = splits[half]
        for piece in range(Y_SIZE):
            made = dot(flipped[piece], low) * scale
            made = made.reshape(Z_SIZE, 2, -1, STATE)
            by_z[half][:, piece] = made[:, :, :first]
            by_y[half][piece] = made[:, :, first : first + second]
            for side in range(2 if third else 0):
                by_x[side, piece] = made[:, side, first + second :]
        for step in range(3):
            rz_copy(half, order(step)).start()
        for m in (2, 1, 3):
            ry_copy(half, m).start()
        if third:
            rx_copy().start()
        for step in range(3, Z_SIZE - 1):
            rz_copy(half, order(step)).start()

    def weigh_middle_x():
        rx_copy().wait_recv()
        rx_sum[...] = by_x[x] + rx_in[...]
        for m in (2, 1, 3):
            ryn_copy(m).start()

    def weigh_middle_y(half):
        for m in range(1, Y_SIZE):
            ry_copy(half, m).wait_recv()
        ry_sum[half][...] = by_y[half][y] + ry_in[half][1] + ry_in[half][2] + ry_in[half][3]
        for step in range(Z_SIZE - 1):
            rzl_copy(half, order(step)).start()

    def weigh_middle_z(half):
        for k in range(1, Z_SIZE):
            rz_copy(half, k).wait_recv()
        rz_sum[half][...] = by_z[half][z] + sum(rz_in[half][k] for k in range(1, Z_SIZE))
        for m in (2, 1, 3):
            ryl_copy(half, m).start()

    def weigh_next():
        for m in range(1, Y_SIZE):
            ryn_copy(m).wait_recv()
        ry_total[...] = rx_sum[y] + sum(ry_next[m] for m in range(1, Y_SIZE))
        for step in range(Z_SIZE - 1):
            rzn_copy(order(step)).start()

    def weigh_late(half):
        first = splits[half][0]
        for m in range(1, Y_SIZE):
            ryl_copy(half, m).wait_recv()
        rl_own[half][:, :first] = rz_sum[half][y] + sum(ry_late[half][m] for m in range(1, Y_SIZE))
        for k in range(1, Z_SIZE):
            rzl_copy(half, k).wait_recv()
        rl_own[half][:, first:] = ry_sum[half][z] + sum(rz_late[half][k] for k in range(1, Z_SIZE))
        rl_copy(half).start()

    def weigh_end(half):
        first, second, third = splits[half]
        columns = slice((1 - half) * STATE, (2 - half) * STATE)
        if third:
            for k in range(1, Z_SIZE):
                rzn_copy(k).wait_recv()
            weight[first + second :, columns] = ry_total[z] + sum(rz_next[k] for k in range(1, Z_SIZE))
        rl_copy(half).wait_recv()
        weight[: first + second, columns] = rl_own[half][x] + rl_in[half][...]


    def done(turn):
        return jnp.where(turn == 0, 0, jnp.minimum(turn + 1, heads * HEAD // width))

    def joins(turn, _):
        chunk = turn // 2

        def one_join(step, _):
            join(chunk, step)
            return 0

        def one_group(index, _):
            inside(index)
            return 0

        lax.fori_loop(turn % 2 * 4, turn % 2 * 4 + 4, one_join, 0)
        lax.fori_loop(done(turn), done(turn + 1), one_group, 0)

        @pl.when(turn == 1)
        def _():
            scan_decays()

        @pl.when(turn == 3)
        def _():
            for m in range(1, Y_SIZE):
                dy_copy(m).wait_recv()

        @pl.when(jnp.logical_and(turn >= 2, turn % 2 == 0))
        def _():
            scan(chunk - 1)

        @pl.when(jnp.logical_and(turn >= 3, turn % 2 == 1))
        def _():
            spread(chunk - 1)

        return 0

    def nearest(step):
        return order(Z_SIZE - 1 - step)

    def own_then_far(step):
        return order((step + Z_SIZE - 1) % Z_SIZE)

    def piece_of(half, k):
        return half * Z_SIZE + (z + Z_SIZE - k) % Z_SIZE

    def first_chunk(step, _):
        hand_on(0, nearest(step))
        return 0

    def second_chunk(step, _):
        hand_on(1, nearest(step))
        return 0

    def own_first(step, _):
        with_start(piece_of(x, nearest(step)))
        return 0

    def others_first(step, _):
        k = nearest(step)
        r_copy(0, k).wait_recv()
        r_copy(1, k).wait_recv()
        with_start(piece_of(1 - x, k))
        return 0

    def third_chunk(step, _):
        hand_on(2, nearest(step))
        return 0

    def last_chunk(step, _):
        hand_on(3, own_then_far(step))
        return 0

    def own_last(step, _):
        with_finish(piece_of(x, own_then_far(step)))
        return 0

    def others_last(step, _):
        k = own_then_far(step)
        r_copy(2, k).wait_recv()
        r_copy(3, k).wait_recv()
        with_finish(piece_of(1 - x, k))
        return 0

    pass_decays()
    lax.fori_loop(0, Z_SIZE, joins, 0)
    lax.fori_loop(0, Z_SIZE, first_chunk, 0)
    lax.fori_loop(0, Z_SIZE, second_chunk, 0)
    span = layer.shape[1] // Y_SIZE
    for piece in range(Y_SIZE):
        flipped[piece] = layer[:, piece * span : (piece + 1) * span].T
    scan(3)
    lax.fori_loop(0, Z_SIZE, own_first, 0)
    spread(3)
    lax.fori_loop(0, Z_SIZE // 2, others_first, 0)
    lax.fori_loop(0, Z_SIZE, third_chunk, 0)
    lax.fori_loop(Z_SIZE // 2, Z_SIZE, others_first, 0)
    sum_begin(0)
    sum_middle(0)
    lax.fori_loop(0, Z_SIZE, last_chunk, 0)
    low = sum_end(0)
    weigh(0, low)
    lax.fori_loop(0, Z_SIZE, own_last, 0)
    lax.fori_loop(0, Z_SIZE, others_last, 0)
    sum_begin(1)
    weigh_middle_y(0)
    weigh_middle_z(0)
    sum_middle(1)
    low = sum_end(1)
    weigh(1, low)
    weigh_late(0)
    for block in range(count):
        end_term = jnp.sum(jnp.sum(ends[block], axis=1), axis=1, keepdims=True)
        at_last = iota((heads, BLOCK), 1) == BLOCK - 1
        changes = change[block] + jnp.where(at_last, end_term, 0.0)
        grad_decay[:, blocks[block]] = dot(changes, lower, NN, HIGHEST)
    weigh_middle_x()
    weigh_end(0)
    weigh_middle_y(1)
    weigh_next()
    weigh_middle_z(1)
    weigh_late(1)
    weigh_end(1)

    dx_copy().wait_send()
    for chunk in range(CHUNKS):
        for k in range(Z_SIZE):
            x_copy(chunk, k).wait_send()
            r_copy(chunk, k).wait_send()
            if k:
                z_copy(chunk, k).wait_send()
                b_copy(chunk, k).wait_send()
        for m in range(1, Y_SIZE):
            y_copy(chunk, m).wait_send()
    for k in range(1, Z_SIZE):
        dz_copy(k).wait_send()
        rzn_copy(k).wait_send()
        for half in range(2):
            rz_copy(half, k).wait_send()
            rzl_copy(half, k).wait_send()
    for m in range(1, 4):
        dy_copy(m).wait_send()
        ryn_copy(m).wait_send()
        for half in range(2):
            p_copy(half, m).wait_send()
            g_copy(half, m).wait_send()
            ry_copy(half, m).wait_send()
            ryl_copy(half, m).wait_send()
    rx_copy().wait_send()
    for half in range(2):
        rl_copy(half).wait_send()


def dma(*shape):
    return pltpu.SemaphoreType.DMA(shape)


def hand_out_kernel(a, b, c, d, a_out, b_out, c_out, d_out, sems):
    pairs = ((a, a_out), (b, b_out), (c, c_out), (d, d_out))
    copies = [pltpu.make_async_copy(one, out, sems.at[i]) for i, (one, out) in enumerate(pairs)]
    for copy in copies:
        copy.start()
    for copy in copies:
        copy.wait()


def on_device(layer_input, conv_output, state_maps, log_decay, out_grad):
    toks, columns = conv_output.shape
    heads = log_decay.shape[0]
    slices = heads // 2
    count = toks // BLOCK
    tile = columns // (Y_SIZE * Z_SIZE * 2)
    splits = ((tile // 4, tile // 4 * 3, 0), (tile // 4, tile // 2, tile // 4))
    third = splits[1][2]

    def floats(*shape):
        return pltpu.VMEM(shape, F32)

    def both(which, *shape):
        return [floats(*shape, splits[half][which], STATE) for half in range(2)]

    grad_conv, grad_maps, grad_decay, grad_weight = pl.pallas_call(
        functools.partial(kernel, 1.0 / math.sqrt(toks * lax.axis_size("ctx")), splits),
        out_shape=(
            jax.ShapeDtypeStruct((toks, columns), BF16),
            jax.ShapeDtypeStruct((toks, 2 * STATE), F32),
            jax.ShapeDtypeStruct((heads, toks), F32),
            jax.ShapeDtypeStruct((tile, 2 * STATE), F32),
        ),
        in_specs=[VMEM] * 5,
        out_specs=(VMEM,) * 4,
        scratch_shapes=[
            floats(2, slices, PAIR, STATE),
            floats(2, Z_SIZE, PAIR, STATE),
            floats(CHUNKS, Z_SIZE, HEAD, STATE),
            floats(CHUNKS, Z_SIZE, HEAD, STATE),
            floats(CHUNKS, Y_SIZE, HEAD, STATE),
            floats(CHUNKS, Z_SIZE, HEAD, STATE),
            floats(CHUNKS, Z_SIZE, HEAD, STATE),
            floats(CHUNKS, Z_SIZE, HEAD, STATE),
            floats(CHUNKS, Z_SIZE, HEAD, STATE),
            floats(2, slices, PAIR, STATE),
            floats(slices, 8, STATE),
            floats(Z_SIZE, 8, STATE),
            floats(Z_SIZE, 8, STATE),
            floats(Z_SIZE, 8, STATE),
            floats(Y_SIZE, 8, STATE),
            floats(2, Z_SIZE, 8, STATE),
            floats(count, heads, 8, BLOCK),
            floats(count, heads, 8, STATE),
            floats(count, heads, BLOCK),
            floats(count, heads, 8, STATE),
            floats(count, BLOCK, BLOCK),
            floats(2, count, BLOCK, STATE),
            floats(2, toks, columns),
            pltpu.VMEM((2, toks, columns), BF16),
            floats(2, toks, columns),
            floats(count, slices, PAIR, STATE),
            floats(max(count - 1, 1), slices, PAIR, STATE),
            floats(count, slices, PAIR, STATE),
            floats(2, toks, STATE),
            floats(2, 4, toks // 4, STATE),
            floats(2, toks, STATE),
            pltpu.VMEM((Y_SIZE, columns // Y_SIZE, toks), BF16),
            both(1, Y_SIZE, Z_SIZE, 2),
            floats(2, Y_SIZE, Z_SIZE, third, STATE),
            both(0, Z_SIZE, Y_SIZE, 2),
            both(1, Y_SIZE, Z_SIZE, 2),
            floats(Y_SIZE, Z_SIZE, third, STATE),
            both(0, Z_SIZE, Y_SIZE, 2),
            both(1, Z_SIZE, 2),
            floats(Y_SIZE, Z_SIZE, third, STATE),
            both(0, Y_SIZE, 2),
            both(1, Z_SIZE, 2),
            both(0, Y_SIZE, 2),
            floats(Y_SIZE, Z_SIZE, third, STATE),
            floats(Z_SIZE, third, STATE),
            floats(Z_SIZE, third, STATE),
            [floats(2, sum(split[:2]), STATE) for split in splits],
            [floats(sum(split[:2]), STATE) for split in splits],
            dma(CHUNKS, Z_SIZE), dma(CHUNKS, Z_SIZE), dma(CHUNKS, Z_SIZE), dma(CHUNKS, Z_SIZE),
            dma(CHUNKS, Y_SIZE), dma(CHUNKS, Y_SIZE), dma(CHUNKS, Z_SIZE), dma(CHUNKS, Z_SIZE),
            dma(CHUNKS, Z_SIZE), dma(CHUNKS, Z_SIZE),
            dma(1), dma(1), dma(Z_SIZE), dma(Z_SIZE), dma(Y_SIZE), dma(Y_SIZE),
            dma(2, 4), dma(2, 4), dma(2, 4), dma(2, 4),
            dma(2, Y_SIZE), dma(2, Y_SIZE), dma(2, Z_SIZE), dma(2, Z_SIZE),
            dma(1), dma(1), dma(2, Z_SIZE), dma(2, Z_SIZE), dma(2, Y_SIZE), dma(2, Y_SIZE),
            dma(Y_SIZE), dma(Y_SIZE), dma(Z_SIZE), dma(Z_SIZE),
            dma(2), dma(2),
        ],
        compiler_params=pltpu.CompilerParams(
            collective_id=0, has_side_effects=True, vmem_limit_bytes=LIMIT
        ),
        name="backward",
    )(conv_output, out_grad, state_maps, log_decay, layer_input)
    results = (grad_conv, grad_maps, grad_decay, grad_weight)
    return pl.pallas_call(
        hand_out_kernel,
        out_shape=tuple(jax.ShapeDtypeStruct(one.shape, one.dtype) for one in results),
        in_specs=[VMEM] * 4,
        out_specs=(pl.BlockSpec(memory_space=pl.ANY),) * 4,
        scratch_shapes=[dma(4)],
        name="hand_out",
    )(*results)


def solution(mesh):
    placed = (P("ctx", "dp"), P("ctx", "dp"), P("ctx", None), P("dp", "ctx"), P("ctx", "dp"))
    return jax.shard_map(
        on_device,
        mesh=mesh,
        in_specs=placed,
        out_specs=(P("ctx", "dp"), P("ctx", None), P("dp", "ctx"), P(("dp", "ctx"), None)),
        check_vma=False,
    )
```

```python
import functools
import math

import jax
import jax.numpy as jnp
from jax import lax
from jax.experimental import pallas as pl
from jax.experimental.pallas import tpu as pltpu
from jax.sharding import PartitionSpec as P

BLOCK = 128
HEAD = 64
STATE = 128
PAIR = 2 * HEAD
CHUNKS = 4
Z_SIZE = 8
Y_SIZE = 4
MESH = pl.DeviceIdType.MESH
F32 = jnp.float32
BF16 = jnp.bfloat16
HIGHEST = lax.Precision.HIGHEST
NT = (((1,), (1,)), ((), ()))
TN = (((0,), (0,)), ((), ()))
NN = (((1,), (0,)), ((), ()))
VMEM = pl.BlockSpec(memory_space=pltpu.VMEM)
LIMIT = 48 * 1024 * 1024


def dot(a, b, dims=NN, precision=None):
    return lax.dot_general(a, b, dims, precision=precision, preferred_element_type=F32)


def iota(shape, axis):
    return lax.broadcasted_iota(jnp.int32, shape, axis)


def two_parts(values):
    high = values.astype(BF16)
    return high, (values - high.astype(F32)).astype(BF16)


def head_lanes(first_head, head_count, columns, width):
    shape = (head_count, columns)
    return (iota(shape, 0) == first_head + iota(shape, 1) // width).astype(BF16)


def widen(parts, lanes):
    return dot(parts[0], lanes) + dot(parts[1], lanes)


def place():
    dp, ctx = lax.axis_index("dp"), lax.axis_index("ctx")
    return dp, ctx // (2 * Z_SIZE), (ctx // 2) % Z_SIZE, ctx % 2


def device(dp, y, z, x):
    return (dp, (y * Z_SIZE + z) * 2 + x)


def remote(src, dst, send, recv, target):
    return pltpu.make_async_remote_copy(
        src_ref=src, dst_ref=dst, send_sem=send, recv_sem=recv, device_id=target, device_id_type=MESH
    )


def pick(tile, part):
    return jnp.where(part == 0, tile[0:1], tile[4:5])


def order(step):
    odd = step % 2
    return Z_SIZE // 2 + (step // 2) * (1 - odd) - ((step + 1) // 2) * odd


def kernel(
    scale, splits,
    conv, grad, maps, decay, layer, grad_conv, grad_maps, grad_decay, weight,
    own, x_in, t_out, z_in, y_in, before, back_out, back_in, x_out, result,
    d_own, d_x, d_t, d_z, d_y, d_before,
    cum_rows, total_rows, change, ends, mix, flow, wide, weighed, inner_out, finals, backs, states,
    part, beside, total, across, flipped, by_y, by_x, by_z,
    ry_in, rx_in, rz_in, ry_sum, rx_sum, rz_sum, rz_late, ry_late, ry_next, ry_total, rz_next,
    rl_own, rl_in,
    x_send, x_recv, z_send, z_recv, y_send, y_recv, b_send, b_recv, r_send, r_recv,
    dx_send, dx_recv, dz_send, dz_recv, dy_send, dy_recv,
    p_send, p_recv, g_send, g_recv, ry_send, ry_recv, rz_send, rz_recv,
    rx_send, rx_recv, rzl_send, rzl_recv, ryl_send, ryl_recv, ryn_send, ryn_recv, rzn_send, rzn_recv,
    rl_send, rl_recv,
):
    dp, y, z, x = place()
    other = device(dp, y, z, 1 - x)

    def z_at(k):
        return device(dp, y, (z + k) % Z_SIZE, x)

    def y_at(m):
        return device(dp, (y + m) % Y_SIZE, z, x)

    def p_at(m):
        return device((dp + m) % 4, y, z, x)

    partners = [other] + [z_at(k) for k in range(1, Z_SIZE)]
    partners += [y_at(m) for m in range(1, Y_SIZE)] + [p_at(m) for m in range(1, 4)]
    barrier = pltpu.get_barrier_semaphore()
    for partner in partners:
        pl.semaphore_signal(barrier, inc=1, device_id=partner, device_id_type=MESH)

    heads, toks = decay.shape
    count = toks // BLOCK
    width = 4 * HEAD
    square = (BLOCK, BLOCK)
    blocks = [slice(block * BLOCK, (block + 1) * BLOCK) for block in range(count)]


    def head_rows(chunk):
        return pl.ds(pl.multiple_of(chunk % 2 * HEAD, HEAD), HEAD)

    def x_copy(chunk, k):
        piece, rows = (z + k) % Z_SIZE, head_rows(chunk)
        return remote(
            own.at[chunk // 2, (1 - x) * Z_SIZE + piece, rows], x_in.at[chunk // 2, piece, rows],
            x_send.at[chunk, k], x_recv.at[chunk, k], other,
        )

    def z_copy(chunk, k):
        return remote(
            t_out.at[chunk, k], z_in.at[chunk, k], z_send.at[chunk, k], z_recv.at[chunk, k], z_at(k)
        )

    def y_copy(chunk, m):
        return remote(
            y_in.at[chunk, 0], y_in.at[chunk, m], y_send.at[chunk, m], y_recv.at[chunk, m], y_at(m)
        )

    def b_copy(chunk, k):
        return remote(
            back_out.at[chunk, k], back_in.at[chunk, k], b_send.at[chunk, k], b_recv.at[chunk, k], z_at(k)
        )

    def r_copy(chunk, k):
        piece = x * Z_SIZE + (z + Z_SIZE - k) % Z_SIZE
        return remote(
            x_out.at[chunk, k], result.at[chunk // 2, piece, head_rows(chunk)],
            r_send.at[chunk, k], r_recv.at[chunk, k], other,
        )

    def dx_copy():
        rows = pl.ds((1 - x) * Z_SIZE, Z_SIZE)
        return remote(d_own.at[rows], d_x, dx_send.at[0], dx_recv.at[0], other)

    def dz_copy(k):
        return remote(d_t.at[k], d_z.at[k], dz_send.at[k], dz_recv.at[k], z_at(k))

    def dy_copy(m):
        return remote(d_y.at[0], d_y.at[m], dy_send.at[m], dy_recv.at[m], y_at(m))


    decays = decay[...]
    lower_all = (iota((toks, toks), 1) <= iota((toks, toks), 0)).astype(F32)
    cum_all = dot(lower_all, decays, NT, HIGHEST)
    factors = (two_parts(jnp.exp(cum_all[toks - 1 : toks, :] - cum_all)), two_parts(jnp.exp(cum_all)))
    sources = (conv, grad)
    total_all = jnp.exp(dot(decays, jnp.ones((toks, STATE), F32), NN, HIGHEST))
    expand = (iota((heads * 4, heads), 0) // 4 == iota((heads * 4, heads), 1)).astype(F32)
    d_own[...] = dot(expand, total_all, NN, HIGHEST).reshape(heads // 2, 8, STATE)

    def summarize(way, half):
        chunk = 8 * HEAD
        for piece in range(heads // 2 * HEAD // chunk):
            first = half * (heads // 2 * HEAD) + piece * chunk
            columns = pl.ds(pl.multiple_of(first, chunk), chunk)
            lanes = head_lanes(half * (heads // 2) + piece * 8, heads, chunk, HEAD)
            weighted = (widen(factors[way], lanes) * sources[way][:, columns].astype(F32)).astype(BF16)
            made = dot(weighted, maps[:, way * STATE : (way + 1) * STATE], TN)
            own[way, pl.ds(half * Z_SIZE + piece * 4, 4)] = made.reshape(4, PAIR, STATE)

    summarize(0, 1 - x)
    pl.semaphore_wait(barrier, len(partners))
    dx_copy().start()
    for chunk in range(2):
        for step in range(Z_SIZE):
            x_copy(chunk, order(step)).start()
    summarize(1, 1 - x)
    for chunk in range(2, CHUNKS):
        for step in range(Z_SIZE):
            x_copy(chunk, order(step)).start()
    summarize(0, x)
    summarize(1, x)


    causal = iota(square, 1) <= iota(square, 0)
    lower = causal.astype(F32)
    cum_parts, to_end, from_start, scores = [], [], [], []
    for block in range(count):
        rows = blocks[block]
        local = decay[:, rows]
        cum = dot(lower, local, NT, HIGHEST)
        high, middle = two_parts(cum)
        low = (cum - high.astype(F32) - middle.astype(F32)).astype(BF16)
        cum_parts.append((high, middle, low))
        to_end.append(two_parts(jnp.exp(cum[BLOCK - 1 : BLOCK, :] - cum)))
        from_start.append(two_parts(jnp.exp(cum)))
        cum_rows[block] = jnp.broadcast_to(dot(local, lower, NT, HIGHEST)[:, None, :], (heads, 8, BLOCK))
        whole = jnp.exp(dot(local, jnp.ones((BLOCK, STATE), F32), NN, HIGHEST))
        total_rows[block] = jnp.broadcast_to(whole[:, None, :], (heads, 8, STATE))
        scores.append(dot(maps[rows, STATE:], maps[rows, :STATE], NT))
    change[...] = jnp.zeros_like(change)
    mix[...] = jnp.zeros_like(mix)
    flow[...] = jnp.zeros_like(flow)

    def inside(index):
        columns = pl.ds(pl.multiple_of(index * width, width), width)
        pair_slices = pl.ds(index * 2, 2)
        lanes = head_lanes(index * 4, heads, width, HEAD)
        broad = head_lanes(index * 4, heads, 4 * BLOCK, BLOCK)
        in_first = iota((BLOCK, PAIR), 1) < HEAD
        for block in range(count):
            rows = blocks[block]
            xs, gs = conv[rows, columns], grad[rows, columns]
            te, fs = widen(to_end[block], lanes), widen(from_start[block], lanes)
            wide[0, rows, columns] = fs
            wide[1, rows, columns] = te
            xw = (te * xs.astype(F32)).astype(BF16)
            gw = (fs * gs.astype(F32)).astype(BF16)
            weighed[0, rows, columns] = gw
            weighed[1, rows, columns] = xw
            finals[block, pair_slices] = dot(xw, maps[rows, :STATE], TN).reshape(2, PAIR, STATE)
            if block:
                backs[block - 1, pair_slices] = dot(gw, maps[rows, STATE:], TN).reshape(2, PAIR, STATE)
            column = sum(dot(piece, broad) for piece in cum_parts[block])
            y_parts, d_parts, mixed = [], [], None
            for pair in range(2):
                lane = slice(pair * PAIR, (pair + 1) * PAIR)
                x_pair, g_pair = xs[:, lane], gs[:, lane]
                zero = jnp.zeros_like(x_pair)
                x_own = [jnp.where(in_first, x_pair, zero), jnp.where(in_first, zero, x_pair)]
                g_own = [jnp.where(in_first, g_pair, zero), jnp.where(in_first, zero, g_pair)]
                weights = []
                for one in range(2):
                    head = 2 * pair + one
                    col = column[:, head * BLOCK : (head + 1) * BLOCK].reshape(16, 8, BLOCK)
                    gap = (col - cum_rows[block, index * 4 + head][None]).reshape(square)
                    falls = jnp.exp(jnp.where(causal, gap, -1e30))
                    term = falls * dot(g_own[one], x_pair, NT)
                    weights.append((falls * scores[block]).astype(BF16))
                    mixed = term if mixed is None else mixed + term
                y_parts.append(dot(jnp.concatenate(weights, axis=1), jnp.concatenate(x_own, axis=0)))
                d_parts.append(dot(jnp.concatenate(weights, axis=0), jnp.concatenate(g_own, axis=0), TN))
            mix[block] += mixed
            inner_out[0, rows, columns] = jnp.concatenate(y_parts, axis=1)
            inner_out[1, rows, columns] = jnp.concatenate(d_parts, axis=1)


    def pass_decays():
        dx_copy().wait_recv()
        for step in range(Z_SIZE):
            k = order(step)
            piece = (z + k) % Z_SIZE
            target = d_t.at[k] if k else d_z.at[0]
            target[...] = d_own[x * Z_SIZE + piece] * d_x[piece]
            if k:
                dz_copy(k).start()

    def scan_decays():
        for k in range(1, Z_SIZE):
            dz_copy(k).wait_recv()
        for way in range(2):
            fade = jnp.ones((8, STATE), F32)
            for step in range(Z_SIZE):
                at = Z_SIZE - 1 - step if way else step
                d_before[way, (at + Z_SIZE - z) % Z_SIZE] = fade
                fade = fade * d_z[(z + Z_SIZE - at) % Z_SIZE]
        d_y[0] = fade
        for m in (2, 1, 3):
            dy_copy(m).start()

    def join(chunk, step):
        way, part, rows = chunk // 2, chunk % 2, head_rows(chunk)
        k = order(step)
        first = x == way
        x_copy(chunk, k).wait_recv()
        piece = (z + k) % Z_SIZE
        mine = own[way, x * Z_SIZE + piece, rows]
        theirs = x_in[way, piece, rows]
        early = jnp.where(first, mine, theirs)
        late = jnp.where(first, theirs, mine)
        fade = pick(jnp.where(first, d_x[piece], d_own[x * Z_SIZE + piece]), part)
        t_out[chunk, k] = fade * early + late

        @pl.when(step < Z_SIZE - 1)
        def _():
            z_copy(chunk, k).start()

    def scan(chunk):
        way, part = chunk // 2, chunk % 2
        for step in range(Z_SIZE - 1):
            z_copy(chunk, order(step)).wait_recv()
        z_in[chunk, 0] = t_out[chunk, 0]
        state = jnp.zeros((HEAD, STATE), F32)
        for step in range(Z_SIZE):
            at = step + way * (Z_SIZE - 1 - 2 * step)
            slot = (z + Z_SIZE - at) % Z_SIZE
            before[chunk, (at + Z_SIZE - z) % Z_SIZE] = state
            state = pick(d_z[slot], part) * state + z_in[chunk, slot]
        y_in[chunk, 0] = state
        for m in (2, 1, 3):
            y_copy(chunk, m).start()

    def spread(chunk):
        way, part = chunk // 2, chunk % 2
        for m in range(1, Y_SIZE):
            y_copy(chunk, m).wait_recv()
        state = jnp.zeros((HEAD, STATE), F32)
        for step in range(Y_SIZE):
            at = step + way * (Y_SIZE - 1 - 2 * step)
            slot = (y + Y_SIZE - at) % Y_SIZE
            counts = (at - y) * (1 - 2 * way) < 0
            state = jnp.where(counts, pick(d_y[slot], part) * state + y_in[chunk, slot], state)
        for step in range(Z_SIZE):
            k = order(step)
            target = back_out.at[chunk, k] if k else back_in.at[chunk, 0]
            target[...] = before[chunk, k] + pick(d_before[way, k], part) * state
            if k:
                b_copy(chunk, k).start()

    def hand_on(chunk, k):
        way, part, rows = chunk // 2, chunk % 2, head_rows(chunk)
        first = x == way

        @pl.when(k > 0)
        def _():
            b_copy(chunk, k).wait_recv()

        piece = (z + Z_SIZE - k) % Z_SIZE
        early = back_in[chunk, k]
        left = jnp.where(first, own[way, x * Z_SIZE + piece, rows], x_in[way, piece, rows])
        fade = pick(jnp.where(first, d_own[x * Z_SIZE + piece], d_x[piece]), part)
        late = fade * early + left
        x_out[chunk, k] = jnp.where(first, late, early)
        result[way, x * Z_SIZE + piece, rows] = jnp.where(first, early, late)
        r_copy(chunk, k).start()


    def fade_rows(block, index, state):
        tiles = total_rows[block, pl.ds(index * 2, 2)][:, None]
        return (state.reshape(2, 8, 8, STATE) * tiles).reshape(PAIR, STATE)

    def add_change(block, index, product):
        lanes = head_lanes(index * 2, heads, PAIR, HEAD)
        high, low = two_parts(product)
        change[block] += dot(lanes, high, NT) + dot(lanes, low, NT)

    def with_start(index):
        columns = pl.ds(pl.multiple_of(index * PAIR, PAIR), PAIR)
        state = result[0, index]
        for block in range(count):
            rows = blocks[block]
            low = state.astype(BF16)
            flow[0, block] += dot(weighed[0, rows, columns], low)
            outputs = inner_out[0, rows, columns] + wide[0, rows, columns] * dot(maps[rows, STATE:], low, NT)
            add_change(block, index, grad[rows, columns].astype(F32) * outputs)
            state = fade_rows(block, index, state) + finals[block, index]
            states[block, index] = state

    def with_finish(index):
        columns = pl.ds(pl.multiple_of(index * PAIR, PAIR), PAIR)
        state = result[1, index]
        for block in reversed(range(count)):
            rows = blocks[block]
            ends[block, pl.ds(index * 2, 2)] = jnp.sum(
                (state * states[block, index]).reshape(2, 8, 8, STATE), axis=1
            )
            low = state.astype(BF16)
            flow[1, block] += dot(weighed[1, rows, columns], low)
            inputs = inner_out[1, rows, columns] + wide[1, rows, columns] * dot(maps[rows, :STATE], low, NT)
            grad_conv[rows, columns] = inputs.astype(BF16)
            add_change(block, index, conv[rows, columns].astype(F32) * -inputs)
            if block:
                state = fade_rows(block, index, state) + backs[block - 1, index]


    core, chip = dp % 2, dp // 2
    share = toks // 2

    def p_copy(half):
        return remote(
            part.at[half], beside.at[half], p_send.at[half], p_recv.at[half],
            device(dp + 1 - 2 * core, y, z, x),
        )

    def g_copy(half, source, target):
        rows = pl.ds(pl.multiple_of(source * share, share), share)
        return remote(
            total.at[half, rows], across.at[half, rows], g_send.at[half, target], g_recv.at[half, source],
            device((1 - chip) * 2 + target, y, z, x),
        )

    def mix_maps():
        for block in range(count):
            rows = blocks[block]
            part[0, rows] = dot(mix[block], maps[rows, :STATE].astype(F32), NN, HIGHEST)
            part[1, rows] = dot(mix[block], maps[rows, STATE:].astype(F32), TN, HIGHEST)

    def sum_begin(half):
        for block in range(count):
            part[half, blocks[block]] += flow[half, block]
        p_copy(half).start()

    def sum_middle(half):
        p_copy(half).wait_recv()
        total[half] = part[half] + beside[half]
        for target in range(2):
            g_copy(half, core, target).start()

    def sum_end(half):
        for source in range(2):
            g_copy(half, source, 0).wait_recv()
        made = total[half] + across[half]
        grad_maps[:, (1 - half) * STATE : (2 - half) * STATE] = made
        return made.astype(BF16)


    def ry_copy(half, m):
        return remote(
            by_y[half].at[(y + m) % Y_SIZE], ry_in[half].at[m], ry_send.at[half, m], ry_recv.at[half, m], y_at(m)
        )

    def rx_copy():
        return remote(by_x.at[1 - x], rx_in, rx_send.at[0], rx_recv.at[0], other)

    def rz_copy(half, k):
        return remote(
            by_z[half].at[(z + k) % Z_SIZE], rz_in[half].at[k], rz_send.at[half, k], rz_recv.at[half, k], z_at(k)
        )

    def rzl_copy(half, k):
        return remote(
            ry_sum[half].at[(z + k) % Z_SIZE], rz_late[half].at[k],
            rzl_send.at[half, k], rzl_recv.at[half, k], z_at(k),
        )

    def ryl_copy(half, m):
        return remote(
            rz_sum[half].at[(y + m) % Y_SIZE], ry_late[half].at[m],
            ryl_send.at[half, m], ryl_recv.at[half, m], y_at(m),
        )

    def ryn_copy(m):
        return remote(
            rx_sum.at[(y + m) % Y_SIZE], ry_next.at[m], ryn_send.at[m], ryn_recv.at[m], y_at(m)
        )

    def rzn_copy(k):
        return remote(
            ry_total.at[(z + k) % Z_SIZE], rz_next.at[k], rzn_send.at[k], rzn_recv.at[k], z_at(k)
        )

    def rl_copy(half):
        return remote(
            rl_own[half].at[1 - x], rl_in[half], rl_send.at[half], rl_recv.at[half], other
        )

    def weigh(half, low):
        first, second, third = splits[half]
        for piece in range(Y_SIZE):
            made = dot(flipped[piece], low) * scale
            made = made.reshape(Z_SIZE, 2, -1, STATE)
            by_z[half][:, piece] = made[:, :, :first]
            by_y[half][piece] = made[:, :, first : first + second]
            for side in range(2 if third else 0):
                by_x[side, piece] = made[:, side, first + second :]
        for step in range(3):
            rz_copy(half, order(step)).start()
        for m in (2, 1, 3):
            ry_copy(half, m).start()
        if third:
            rx_copy().start()
        for step in range(3, Z_SIZE - 1):
            rz_copy(half, order(step)).start()

    def weigh_middle_x():
        rx_copy().wait_recv()
        rx_sum[...] = by_x[x] + rx_in[...]
        for m in (2, 1, 3):
            ryn_copy(m).start()

    def weigh_middle_y(half):
        for m in range(1, Y_SIZE):
            ry_copy(half, m).wait_recv()
        ry_sum[half][...] = by_y[half][y] + ry_in[half][1] + ry_in[half][2] + ry_in[half][3]
        for step in range(Z_SIZE - 1):
            rzl_copy(half, order(step)).start()

    def weigh_middle_z(half):
        for k in range(1, Z_SIZE):
            rz_copy(half, k).wait_recv()
        rz_sum[half][...] = by_z[half][z] + sum(rz_in[half][k] for k in range(1, Z_SIZE))
        for m in (2, 1, 3):
            ryl_copy(half, m).start()

    def weigh_next():
        for m in range(1, Y_SIZE):
            ryn_copy(m).wait_recv()
        ry_total[...] = rx_sum[y] + sum(ry_next[m] for m in range(1, Y_SIZE))
        for step in range(Z_SIZE - 1):
            rzn_copy(order(step)).start()

    def weigh_late(half):
        first = splits[half][0]
        for m in range(1, Y_SIZE):
            ryl_copy(half, m).wait_recv()
        rl_own[half][:, :first] = rz_sum[half][y] + sum(ry_late[half][m] for m in range(1, Y_SIZE))
        for k in range(1, Z_SIZE):
            rzl_copy(half, k).wait_recv()
        rl_own[half][:, first:] = ry_sum[half][z] + sum(rz_late[half][k] for k in range(1, Z_SIZE))
        rl_copy(half).start()

    def weigh_end(half):
        first, second, third = splits[half]
        columns = slice((1 - half) * STATE, (2 - half) * STATE)
        if third:
            for k in range(1, Z_SIZE):
                rzn_copy(k).wait_recv()
            weight[first + second :, columns] = ry_total[z] + sum(rz_next[k] for k in range(1, Z_SIZE))
        rl_copy(half).wait_recv()
        weight[: first + second, columns] = rl_own[half][x] + rl_in[half][...]


    def done(turn):
        return jnp.where(turn == 0, 0, jnp.minimum(turn + 1, heads * HEAD // width))

    def joins(turn, _):
        chunk = turn // 2

        def one_join(step, _):
            join(chunk, step)
            return 0

        def one_group(index, _):
            inside(index)
            return 0

        lax.fori_loop(turn % 2 * 4, turn % 2 * 4 + 4, one_join, 0)
        lax.fori_loop(done(turn), done(turn + 1), one_group, 0)

        @pl.when(turn == 1)
        def _():
            scan_decays()

        @pl.when(turn == 3)
        def _():
            for m in range(1, Y_SIZE):
                dy_copy(m).wait_recv()

        @pl.when(jnp.logical_and(turn >= 2, turn % 2 == 0))
        def _():
            scan(chunk - 1)

        @pl.when(jnp.logical_and(turn >= 3, turn % 2 == 1))
        def _():
            spread(chunk - 1)

        return 0

    def nearest(step):
        return order(Z_SIZE - 1 - step)

    def own_then_far(step):
        return order((step + Z_SIZE - 1) % Z_SIZE)

    def piece_of(half, k):
        return half * Z_SIZE + (z + Z_SIZE - k) % Z_SIZE

    def first_chunk(step, _):
        hand_on(0, nearest(step))
        return 0

    def second_chunk(step, _):
        hand_on(1, nearest(step))
        return 0

    def own_first(step, _):
        with_start(piece_of(x, nearest(step)))
        return 0

    def others_first(step, _):
        k = nearest(step)
        r_copy(0, k).wait_recv()
        r_copy(1, k).wait_recv()
        with_start(piece_of(1 - x, k))
        return 0

    def third_chunk(step, _):
        hand_on(2, nearest(step))
        return 0

    def last_chunk(step, _):
        hand_on(3, own_then_far(step))
        return 0

    def own_last(step, _):
        with_finish(piece_of(x, own_then_far(step)))
        return 0

    def others_last(step, _):
        k = own_then_far(step)
        r_copy(2, k).wait_recv()
        r_copy(3, k).wait_recv()
        with_finish(piece_of(1 - x, k))
        return 0

    pass_decays()
    lax.fori_loop(0, Z_SIZE, joins, 0)
    lax.fori_loop(0, Z_SIZE, first_chunk, 0)
    lax.fori_loop(0, Z_SIZE, second_chunk, 0)
    span = layer.shape[1] // Y_SIZE
    for piece in range(Y_SIZE):
        flipped[piece] = layer[:, piece * span : (piece + 1) * span].T
    mix_maps()
    scan(3)
    lax.fori_loop(0, Z_SIZE, own_first, 0)
    spread(3)
    lax.fori_loop(0, Z_SIZE // 2, others_first, 0)
    lax.fori_loop(0, Z_SIZE, third_chunk, 0)
    lax.fori_loop(Z_SIZE // 2, Z_SIZE, others_first, 0)
    sum_begin(0)
    sum_middle(0)
    lax.fori_loop(0, Z_SIZE, last_chunk, 0)
    low = sum_end(0)
    weigh(0, low)
    lax.fori_loop(0, Z_SIZE, own_last, 0)
    lax.fori_loop(0, Z_SIZE, others_last, 0)
    sum_begin(1)
    weigh_middle_y(0)
    weigh_middle_z(0)
    sum_middle(1)
    low = sum_end(1)
    weigh(1, low)
    weigh_late(0)
    for block in range(count):
        end_term = jnp.sum(jnp.sum(ends[block], axis=1), axis=1, keepdims=True)
        at_last = iota((heads, BLOCK), 1) == BLOCK - 1
        changes = change[block] + jnp.where(at_last, end_term, 0.0)
        grad_decay[:, blocks[block]] = dot(changes, lower, NN, HIGHEST)
    weigh_middle_x()
    weigh_end(0)
    weigh_middle_y(1)
    weigh_next()
    weigh_middle_z(1)
    weigh_late(1)
    weigh_end(1)

    dx_copy().wait_send()
    for chunk in range(CHUNKS):
        for k in range(Z_SIZE):
            x_copy(chunk, k).wait_send()
            r_copy(chunk, k).wait_send()
            if k:
                z_copy(chunk, k).wait_send()
                b_copy(chunk, k).wait_send()
        for m in range(1, Y_SIZE):
            y_copy(chunk, m).wait_send()
    for k in range(1, Z_SIZE):
        dz_copy(k).wait_send()
        rzn_copy(k).wait_send()
        for half in range(2):
            rz_copy(half, k).wait_send()
            rzl_copy(half, k).wait_send()
    for m in range(1, 4):
        dy_copy(m).wait_send()
        ryn_copy(m).wait_send()
        for half in range(2):
            ry_copy(half, m).wait_send()
            ryl_copy(half, m).wait_send()
    rx_copy().wait_send()
    for half in range(2):
        rl_copy(half).wait_send()
        p_copy(half).wait_send()
        for target in range(2):
            g_copy(half, core, target).wait_send()


def dma(*shape):
    return pltpu.SemaphoreType.DMA(shape)


def hand_out_kernel(a, b, c, d, a_out, b_out, c_out, d_out, sems):
    pairs = ((a, a_out), (b, b_out), (c, c_out), (d, d_out))
    copies = [pltpu.make_async_copy(one, out, sems.at[i]) for i, (one, out) in enumerate(pairs)]
    for copy in copies:
        copy.start()
    for copy in copies:
        copy.wait()


def on_device(layer_input, conv_output, state_maps, log_decay, out_grad):
    toks, columns = conv_output.shape
    heads = log_decay.shape[0]
    slices = heads // 2
    count = toks // BLOCK
    tile = columns // (Y_SIZE * Z_SIZE * 2)
    splits = ((tile // 4, tile // 4 * 3, 0), (tile // 4, tile // 2, tile // 4))
    third = splits[1][2]

    def floats(*shape):
        return pltpu.VMEM(shape, F32)

    def both(which, *shape):
        return [floats(*shape, splits[half][which], STATE) for half in range(2)]

    grad_conv, grad_maps, grad_decay, grad_weight = pl.pallas_call(
        functools.partial(kernel, 1.0 / math.sqrt(toks * lax.axis_size("ctx")), splits),
        out_shape=(
            pltpu.VMEM((toks, columns), BF16),
            pltpu.VMEM((toks, 2 * STATE), F32),
            pltpu.VMEM((heads, toks), F32),
            pltpu.VMEM((tile, 2 * STATE), F32),
        ),
        in_specs=[VMEM] * 5,
        out_specs=(VMEM,) * 4,
        scratch_shapes=[
            floats(2, slices, PAIR, STATE),
            floats(2, Z_SIZE, PAIR, STATE),
            floats(CHUNKS, Z_SIZE, HEAD, STATE),
            floats(CHUNKS, Z_SIZE, HEAD, STATE),
            floats(CHUNKS, Y_SIZE, HEAD, STATE),
            floats(CHUNKS, Z_SIZE, HEAD, STATE),
            floats(CHUNKS, Z_SIZE, HEAD, STATE),
            floats(CHUNKS, Z_SIZE, HEAD, STATE),
            floats(CHUNKS, Z_SIZE, HEAD, STATE),
            floats(2, slices, PAIR, STATE),
            floats(slices, 8, STATE),
            floats(Z_SIZE, 8, STATE),
            floats(Z_SIZE, 8, STATE),
            floats(Z_SIZE, 8, STATE),
            floats(Y_SIZE, 8, STATE),
            floats(2, Z_SIZE, 8, STATE),
            floats(count, heads, 8, BLOCK),
            floats(count, heads, 8, STATE),
            floats(count, heads, BLOCK),
            floats(count, heads, 8, STATE),
            floats(count, BLOCK, BLOCK),
            floats(2, count, BLOCK, STATE),
            floats(2, toks, columns),
            pltpu.VMEM((2, toks, columns), BF16),
            floats(2, toks, columns),
            floats(count, slices, PAIR, STATE),
            floats(max(count - 1, 1), slices, PAIR, STATE),
            floats(count, slices, PAIR, STATE),
            floats(2, toks, STATE),
            floats(2, toks, STATE),
            floats(2, toks, STATE),
            floats(2, toks, STATE),
            pltpu.VMEM((Y_SIZE, columns // Y_SIZE, toks), BF16),
            both(1, Y_SIZE, Z_SIZE, 2),
            floats(2, Y_SIZE, Z_SIZE, third, STATE),
            both(0, Z_SIZE, Y_SIZE, 2),
            both(1, Y_SIZE, Z_SIZE, 2),
            floats(Y_SIZE, Z_SIZE, third, STATE),
            both(0, Z_SIZE, Y_SIZE, 2),
            both(1, Z_SIZE, 2),
            floats(Y_SIZE, Z_SIZE, third, STATE),
            both(0, Y_SIZE, 2),
            both(1, Z_SIZE, 2),
            both(0, Y_SIZE, 2),
            floats(Y_SIZE, Z_SIZE, third, STATE),
            floats(Z_SIZE, third, STATE),
            floats(Z_SIZE, third, STATE),
            [floats(2, sum(split[:2]), STATE) for split in splits],
            [floats(sum(split[:2]), STATE) for split in splits],
            dma(CHUNKS, Z_SIZE), dma(CHUNKS, Z_SIZE), dma(CHUNKS, Z_SIZE), dma(CHUNKS, Z_SIZE),
            dma(CHUNKS, Y_SIZE), dma(CHUNKS, Y_SIZE), dma(CHUNKS, Z_SIZE), dma(CHUNKS, Z_SIZE),
            dma(CHUNKS, Z_SIZE), dma(CHUNKS, Z_SIZE),
            dma(1), dma(1), dma(Z_SIZE), dma(Z_SIZE), dma(Y_SIZE), dma(Y_SIZE),
            dma(2), dma(2), dma(2, 2), dma(2, 2),
            dma(2, Y_SIZE), dma(2, Y_SIZE), dma(2, Z_SIZE), dma(2, Z_SIZE),
            dma(1), dma(1), dma(2, Z_SIZE), dma(2, Z_SIZE), dma(2, Y_SIZE), dma(2, Y_SIZE),
            dma(Y_SIZE), dma(Y_SIZE), dma(Z_SIZE), dma(Z_SIZE),
            dma(2), dma(2),
        ],
        compiler_params=pltpu.CompilerParams(
            collective_id=0, has_side_effects=True, vmem_limit_bytes=LIMIT
        ),
        name="backward",
    )(
        *(
            pltpu.with_memory_space_constraint(one, pltpu.HBM)
            for one in (conv_output, out_grad, state_maps, log_decay, layer_input)
        )
    )
    results = [
        pltpu.with_memory_space_constraint(one, pltpu.VMEM)
        for one in (grad_conv, grad_maps, grad_decay, grad_weight)
    ]
    return pl.pallas_call(
        hand_out_kernel,
        out_shape=tuple(jax.ShapeDtypeStruct(one.shape, one.dtype) for one in results),
        in_specs=[pl.BlockSpec(memory_space=pl.ANY)] * 4,
        out_specs=(pl.BlockSpec(memory_space=pl.ANY),) * 4,
        scratch_shapes=[dma(4)],
        name="hand_out",
    )(*results)


def solution(mesh):
    placed = (P("ctx", "dp"), P("ctx", "dp"), P("ctx", None), P("dp", "ctx"), P("ctx", "dp"))
    return jax.shard_map(
        on_device,
        mesh=mesh,
        in_specs=placed,
        out_specs=(P("ctx", "dp"), P("ctx", None), P("dp", "ctx"), P(("dp", "ctx"), None)),
        check_vma=False,
    )
```

```python
import functools
import math

import jax
import jax.numpy as jnp
from jax import lax
from jax.experimental import pallas as pl
from jax.experimental.pallas import tpu as pltpu
from jax.sharding import PartitionSpec as P

BLOCK = 128
HEAD = 64
STATE = 128
PAIR = 2 * HEAD
CHUNKS = 4
Z_SIZE = 8
Y_SIZE = 4
MESH = pl.DeviceIdType.MESH
F32 = jnp.float32
BF16 = jnp.bfloat16
HIGHEST = lax.Precision.HIGHEST
NT = (((1,), (1,)), ((), ()))
TN = (((0,), (0,)), ((), ()))
NN = (((1,), (0,)), ((), ()))
VMEM = pl.BlockSpec(memory_space=pltpu.VMEM)
LIMIT = 48 * 1024 * 1024


def dot(a, b, dims=NN, precision=None):
    return lax.dot_general(a, b, dims, precision=precision, preferred_element_type=F32)


def iota(shape, axis):
    return lax.broadcasted_iota(jnp.int32, shape, axis)


def two_parts(values):
    high = values.astype(BF16)
    return high, (values - high.astype(F32)).astype(BF16)


def head_lanes(first_head, head_count, columns, width):
    shape = (head_count, columns)
    return (iota(shape, 0) == first_head + iota(shape, 1) // width).astype(BF16)


def widen(parts, lanes):
    return dot(parts[0], lanes) + dot(parts[1], lanes)


def place():
    dp, ctx = lax.axis_index("dp"), lax.axis_index("ctx")
    return dp, ctx // (2 * Z_SIZE), (ctx // 2) % Z_SIZE, ctx % 2


def device(dp, y, z, x):
    return (dp, (y * Z_SIZE + z) * 2 + x)


def remote(src, dst, send, recv, target):
    return pltpu.make_async_remote_copy(
        src_ref=src, dst_ref=dst, send_sem=send, recv_sem=recv, device_id=target, device_id_type=MESH
    )


def pick(tile, part):
    return jnp.where(part == 0, tile[0:1], tile[4:5])


def order(step):
    odd = step % 2
    return Z_SIZE // 2 + (step // 2) * (1 - odd) - ((step + 1) // 2) * odd


def kernel(
    scale, splits,
    conv, grad, maps, decay, layer, grad_conv, grad_maps, grad_decay, weight,
    own, x_in, t_out, z_in, y_in, before, back_out, back_in, x_out, result,
    d_own, d_x, d_t, d_z, d_y, d_before,
    cum_rows, total_rows, change, ends, mix, flow, wide, weighed, inner_out, finals, backs, states,
    part, beside, total, across, flipped, by_y, by_x, by_z,
    ry_in, rx_in, rz_in, ry_sum, rx_sum, rz_sum, rz_late, ry_late, ry_next, ry_total, rz_next,
    rl_own, rl_in,
    x_send, x_recv, z_send, z_recv, y_send, y_recv, b_send, b_recv, r_send, r_recv,
    dx_send, dx_recv, dz_send, dz_recv, dy_send, dy_recv,
    p_send, p_recv, g_send, g_recv, ry_send, ry_recv, rz_send, rz_recv,
    rx_send, rx_recv, rzl_send, rzl_recv, ryl_send, ryl_recv, ryn_send, ryn_recv, rzn_send, rzn_recv,
    rl_send, rl_recv,
):
    dp, y, z, x = place()
    other = device(dp, y, z, 1 - x)

    def z_at(k):
        return device(dp, y, (z + k) % Z_SIZE, x)

    def y_at(m):
        return device(dp, (y + m) % Y_SIZE, z, x)

    def p_at(m):
        return device((dp + m) % 4, y, z, x)

    partners = [other] + [z_at(k) for k in range(1, Z_SIZE)]
    partners += [y_at(m) for m in range(1, Y_SIZE)] + [p_at(m) for m in range(1, 4)]
    barrier = pltpu.get_barrier_semaphore()
    for partner in partners:
        pl.semaphore_signal(barrier, inc=1, device_id=partner, device_id_type=MESH)

    heads, toks = decay.shape
    count = toks // BLOCK
    width = 4 * HEAD
    square = (BLOCK, BLOCK)
    blocks = [slice(block * BLOCK, (block + 1) * BLOCK) for block in range(count)]


    def head_rows(chunk):
        return pl.ds(pl.multiple_of(chunk % 2 * HEAD, HEAD), HEAD)

    def x_copy(chunk, k):
        piece, rows = (z + k) % Z_SIZE, head_rows(chunk)
        return remote(
            own.at[chunk // 2, (1 - x) * Z_SIZE + piece, rows], x_in.at[chunk // 2, piece, rows],
            x_send.at[chunk, k], x_recv.at[chunk, k], other,
        )

    def z_copy(chunk, k):
        return remote(
            t_out.at[chunk, k], z_in.at[chunk, k], z_send.at[chunk, k], z_recv.at[chunk, k], z_at(k)
        )

    def y_copy(chunk, m):
        return remote(
            y_in.at[chunk, 0], y_in.at[chunk, m], y_send.at[chunk, m], y_recv.at[chunk, m], y_at(m)
        )

    def b_copy(chunk, k):
        return remote(
            back_out.at[chunk, k], back_in.at[chunk, k], b_send.at[chunk, k], b_recv.at[chunk, k], z_at(k)
        )

    def r_copy(chunk, k):
        piece = x * Z_SIZE + (z + Z_SIZE - k) % Z_SIZE
        return remote(
            x_out.at[chunk, k], result.at[chunk // 2, piece, head_rows(chunk)],
            r_send.at[chunk, k], r_recv.at[chunk, k], other,
        )

    def dx_copy():
        rows = pl.ds((1 - x) * Z_SIZE, Z_SIZE)
        return remote(d_own.at[rows], d_x, dx_send.at[0], dx_recv.at[0], other)

    def dz_copy(k):
        return remote(d_t.at[k], d_z.at[k], dz_send.at[k], dz_recv.at[k], z_at(k))

    def dy_copy(m):
        return remote(d_y.at[0], d_y.at[m], dy_send.at[m], dy_recv.at[m], y_at(m))


    decays = decay[...]
    lower_all = (iota((toks, toks), 1) <= iota((toks, toks), 0)).astype(F32)
    cum_all = dot(lower_all, decays, NT, HIGHEST)
    factors = (two_parts(jnp.exp(cum_all[toks - 1 : toks, :] - cum_all)), two_parts(jnp.exp(cum_all)))
    sources = (conv, grad)
    total_all = jnp.exp(dot(decays, jnp.ones((toks, STATE), F32), NN, HIGHEST))
    expand = (iota((heads * 4, heads), 0) // 4 == iota((heads * 4, heads), 1)).astype(F32)
    d_own[...] = dot(expand, total_all, NN, HIGHEST).reshape(heads // 2, 8, STATE)

    def summarize(way, half):
        chunk = 8 * HEAD
        for piece in range(heads // 2 * HEAD // chunk):
            first = half * (heads // 2 * HEAD) + piece * chunk
            columns = pl.ds(pl.multiple_of(first, chunk), chunk)
            lanes = head_lanes(half * (heads // 2) + piece * 8, heads, chunk, HEAD)
            weighted = (widen(factors[way], lanes) * sources[way][:, columns].astype(F32)).astype(BF16)
            made = dot(weighted, maps[:, way * STATE : (way + 1) * STATE], TN)
            own[way, pl.ds(half * Z_SIZE + piece * 4, 4)] = made.reshape(4, PAIR, STATE)

    summarize(0, 1 - x)
    pl.semaphore_wait(barrier, len(partners))
    dx_copy().start()
    for chunk in range(2):
        for step in range(Z_SIZE):
            x_copy(chunk, order(step)).start()
    summarize(1, 1 - x)
    for chunk in range(2, CHUNKS):
        for step in range(Z_SIZE):
            x_copy(chunk, order(step)).start()
    summarize(0, x)
    summarize(1, x)


    causal = iota(square, 1) <= iota(square, 0)
    lower = causal.astype(F32)
    cum_parts, to_end, from_start, scores = [], [], [], []
    for block in range(count):
        rows = blocks[block]
        local = decay[:, rows]
        cum = dot(lower, local, NT, HIGHEST)
        high, middle = two_parts(cum)
        low = (cum - high.astype(F32) - middle.astype(F32)).astype(BF16)
        cum_parts.append((high, middle, low))
        to_end.append(two_parts(jnp.exp(cum[BLOCK - 1 : BLOCK, :] - cum)))
        from_start.append(two_parts(jnp.exp(cum)))
        cum_rows[block] = jnp.broadcast_to(dot(local, lower, NT, HIGHEST)[:, None, :], (heads, 8, BLOCK))
        whole = jnp.exp(dot(local, jnp.ones((BLOCK, STATE), F32), NN, HIGHEST))
        total_rows[block] = jnp.broadcast_to(whole[:, None, :], (heads, 8, STATE))
        scores.append(dot(maps[rows, STATE:], maps[rows, :STATE], NT))
    change[...] = jnp.zeros_like(change)
    mix[...] = jnp.zeros_like(mix)
    flow[...] = jnp.zeros_like(flow)

    def inside(index):
        columns = pl.ds(pl.multiple_of(index * width, width), width)
        pair_slices = pl.ds(index * 2, 2)
        lanes = head_lanes(index * 4, heads, width, HEAD)
        broad = head_lanes(index * 4, heads, 4 * BLOCK, BLOCK)
        in_first = iota((BLOCK, PAIR), 1) < HEAD
        for block in range(count):
            rows = blocks[block]
            xs, gs = conv[rows, columns], grad[rows, columns]
            te, fs = widen(to_end[block], lanes), widen(from_start[block], lanes)
            wide[0, rows, columns] = fs
            wide[1, rows, columns] = te
            xw = (te * xs.astype(F32)).astype(BF16)
            gw = (fs * gs.astype(F32)).astype(BF16)
            weighed[0, rows, columns] = gw
            weighed[1, rows, columns] = xw
            finals[block, pair_slices] = dot(xw, maps[rows, :STATE], TN).reshape(2, PAIR, STATE)
            if block:
                backs[block - 1, pair_slices] = dot(gw, maps[rows, STATE:], TN).reshape(2, PAIR, STATE)
            column = sum(dot(piece, broad) for piece in cum_parts[block])
            y_parts, d_parts, mixed = [], [], None
            for pair in range(2):
                lane = slice(pair * PAIR, (pair + 1) * PAIR)
                x_pair, g_pair = xs[:, lane], gs[:, lane]
                zero = jnp.zeros_like(x_pair)
                x_own = [jnp.where(in_first, x_pair, zero), jnp.where(in_first, zero, x_pair)]
                g_own = [jnp.where(in_first, g_pair, zero), jnp.where(in_first, zero, g_pair)]
                weights = []
                for one in range(2):
                    head = 2 * pair + one
                    col = column[:, head * BLOCK : (head + 1) * BLOCK].reshape(16, 8, BLOCK)
                    gap = (col - cum_rows[block, index * 4 + head][None]).reshape(square)
                    falls = jnp.exp(jnp.where(causal, gap, -1e30))
                    term = falls * dot(g_own[one], x_pair, NT)
                    weights.append((falls * scores[block]).astype(BF16))
                    mixed = term if mixed is None else mixed + term
                y_parts.append(dot(jnp.concatenate(weights, axis=1), jnp.concatenate(x_own, axis=0)))
                d_parts.append(dot(jnp.concatenate(weights, axis=0), jnp.concatenate(g_own, axis=0), TN))
            mix[block] += mixed
            inner_out[0, rows, columns] = jnp.concatenate(y_parts, axis=1)
            inner_out[1, rows, columns] = jnp.concatenate(d_parts, axis=1)


    def pass_decays():
        dx_copy().wait_recv()
        for step in range(Z_SIZE):
            k = order(step)
            piece = (z + k) % Z_SIZE
            target = d_t.at[k] if k else d_z.at[0]
            target[...] = d_own[x * Z_SIZE + piece] * d_x[piece]
            if k:
                dz_copy(k).start()

    def scan_decays():
        for k in range(1, Z_SIZE):
            dz_copy(k).wait_recv()
        for way in range(2):
            fade = jnp.ones((8, STATE), F32)
            for step in range(Z_SIZE):
                at = Z_SIZE - 1 - step if way else step
                d_before[way, (at + Z_SIZE - z) % Z_SIZE] = fade
                fade = fade * d_z[(z + Z_SIZE - at) % Z_SIZE]
        d_y[0] = fade
        for m in (2, 1, 3):
            dy_copy(m).start()

    def join(chunk, step):
        way, part, rows = chunk // 2, chunk % 2, head_rows(chunk)
        k = order(step)
        first = x == way
        x_copy(chunk, k).wait_recv()
        piece = (z + k) % Z_SIZE
        mine = own[way, x * Z_SIZE + piece, rows]
        theirs = x_in[way, piece, rows]
        early = jnp.where(first, mine, theirs)
        late = jnp.where(first, theirs, mine)
        fade = pick(jnp.where(first, d_x[piece], d_own[x * Z_SIZE + piece]), part)
        t_out[chunk, k] = fade * early + late

        @pl.when(step < Z_SIZE - 1)
        def _():
            z_copy(chunk, k).start()

    def scan(chunk):
        way, part = chunk // 2, chunk % 2
        for step in range(Z_SIZE - 1):
            z_copy(chunk, order(step)).wait_recv()
        z_in[chunk, 0] = t_out[chunk, 0]
        state = jnp.zeros((HEAD, STATE), F32)
        for step in range(Z_SIZE):
            at = step + way * (Z_SIZE - 1 - 2 * step)
            slot = (z + Z_SIZE - at) % Z_SIZE
            before[chunk, (at + Z_SIZE - z) % Z_SIZE] = state
            state = pick(d_z[slot], part) * state + z_in[chunk, slot]
        y_in[chunk, 0] = state
        for m in (2, 1, 3):
            y_copy(chunk, m).start()

    def spread(chunk):
        way, part = chunk // 2, chunk % 2
        for m in range(1, Y_SIZE):
            y_copy(chunk, m).wait_recv()
        state = jnp.zeros((HEAD, STATE), F32)
        for step in range(Y_SIZE):
            at = step + way * (Y_SIZE - 1 - 2 * step)
            slot = (y + Y_SIZE - at) % Y_SIZE
            counts = (at - y) * (1 - 2 * way) < 0
            state = jnp.where(counts, pick(d_y[slot], part) * state + y_in[chunk, slot], state)
        for step in range(Z_SIZE):
            k = order(step)
            target = back_out.at[chunk, k] if k else back_in.at[chunk, 0]
            target[...] = before[chunk, k] + pick(d_before[way, k], part) * state
            if k:
                b_copy(chunk, k).start()

    def hand_on(chunk, k):
        way, part, rows = chunk // 2, chunk % 2, head_rows(chunk)
        first = x == way

        @pl.when(k > 0)
        def _():
            b_copy(chunk, k).wait_recv()

        piece = (z + Z_SIZE - k) % Z_SIZE
        early = back_in[chunk, k]
        left = jnp.where(first, own[way, x * Z_SIZE + piece, rows], x_in[way, piece, rows])
        fade = pick(jnp.where(first, d_own[x * Z_SIZE + piece], d_x[piece]), part)
        late = fade * early + left
        x_out[chunk, k] = jnp.where(first, late, early)
        result[way, x * Z_SIZE + piece, rows] = jnp.where(first, early, late)
        r_copy(chunk, k).start()


    def fade_rows(block, index, state):
        tiles = total_rows[block, pl.ds(index * 2, 2)][:, None]
        return (state.reshape(2, 8, 8, STATE) * tiles).reshape(PAIR, STATE)

    def add_change(block, index, product):
        lanes = head_lanes(index * 2, heads, PAIR, HEAD)
        high, low = two_parts(product)
        change[block] += dot(lanes, high, NT) + dot(lanes, low, NT)

    def with_start(index):
        columns = pl.ds(pl.multiple_of(index * PAIR, PAIR), PAIR)
        state = result[0, index]
        for block in range(count):
            rows = blocks[block]
            low = state.astype(BF16)
            flow[0, block] += dot(weighed[0, rows, columns], low)
            outputs = inner_out[0, rows, columns] + wide[0, rows, columns] * dot(maps[rows, STATE:], low, NT)
            add_change(block, index, grad[rows, columns].astype(F32) * outputs)
            state = fade_rows(block, index, state) + finals[block, index]
            states[block, index] = state

    def with_finish(index):
        columns = pl.ds(pl.multiple_of(index * PAIR, PAIR), PAIR)
        state = result[1, index]
        for block in reversed(range(count)):
            rows = blocks[block]
            ends[block, pl.ds(index * 2, 2)] = jnp.sum(
                (state * states[block, index]).reshape(2, 8, 8, STATE), axis=1
            )
            low = state.astype(BF16)
            flow[1, block] += dot(weighed[1, rows, columns], low)
            inputs = inner_out[1, rows, columns] + wide[1, rows, columns] * dot(maps[rows, :STATE], low, NT)
            grad_conv[rows, columns] = inputs.astype(BF16)
            add_change(block, index, conv[rows, columns].astype(F32) * -inputs)
            if block:
                state = fade_rows(block, index, state) + backs[block - 1, index]


    core, chip = dp % 2, dp // 2
    share = toks // 2

    def p_copy(half):
        return remote(
            part.at[half], beside.at[half], p_send.at[half], p_recv.at[half],
            device(dp + 1 - 2 * core, y, z, x),
        )

    def g_copy(half, source, target):
        rows = pl.ds(pl.multiple_of(source * share, share), share)
        return remote(
            total.at[half, rows], across.at[half, rows], g_send.at[half, target], g_recv.at[half, source],
            device((1 - chip) * 2 + target, y, z, x),
        )

    def mix_maps():
        for block in range(count):
            rows = blocks[block]
            part[0, rows] = dot(mix[block], maps[rows, :STATE].astype(F32), NN, HIGHEST)
            part[1, rows] = dot(mix[block], maps[rows, STATE:].astype(F32), TN, HIGHEST)

    def sum_begin(half):
        for block in range(count):
            part[half, blocks[block]] += flow[half, block]
        p_copy(half).start()

    def sum_middle(half):
        p_copy(half).wait_recv()
        total[half] = part[half] + beside[half]
        for target in range(2):
            g_copy(half, core, target).start()

    def sum_end(half):
        for source in range(2):
            g_copy(half, source, 0).wait_recv()
        made = total[half] + across[half]
        grad_maps[:, (1 - half) * STATE : (2 - half) * STATE] = made
        return made.astype(BF16)


    def ry_copy(half, m):
        return remote(
            by_y[half].at[(y + m) % Y_SIZE], ry_in[half].at[m], ry_send.at[half, m], ry_recv.at[half, m], y_at(m)
        )

    def rx_copy():
        return remote(by_x.at[1 - x], rx_in, rx_send.at[0], rx_recv.at[0], other)

    def rz_copy(half, k):
        return remote(
            by_z[half].at[(z + k) % Z_SIZE], rz_in[half].at[k], rz_send.at[half, k], rz_recv.at[half, k], z_at(k)
        )

    def rzl_copy(half, k):
        return remote(
            ry_sum[half].at[(z + k) % Z_SIZE], rz_late[half].at[k],
            rzl_send.at[half, k], rzl_recv.at[half, k], z_at(k),
        )

    def ryl_copy(half, m):
        return remote(
            rz_sum[half].at[(y + m) % Y_SIZE], ry_late[half].at[m],
            ryl_send.at[half, m], ryl_recv.at[half, m], y_at(m),
        )

    def ryn_copy(m):
        return remote(
            rx_sum.at[(y + m) % Y_SIZE], ry_next.at[m], ryn_send.at[m], ryn_recv.at[m], y_at(m)
        )

    def rzn_copy(k):
        return remote(
            ry_total.at[(z + k) % Z_SIZE], rz_next.at[k], rzn_send.at[k], rzn_recv.at[k], z_at(k)
        )

    def rl_copy(half):
        return remote(
            rl_own[half].at[1 - x], rl_in[half], rl_send.at[half], rl_recv.at[half], other
        )

    def weigh(half, low):
        first, second, third = splits[half]
        for piece in range(Y_SIZE):
            made = dot(flipped[piece], low) * scale
            made = made.reshape(Z_SIZE, 2, -1, STATE)
            by_z[half][:, piece] = made[:, :, :first]
            by_y[half][piece] = made[:, :, first : first + second]
            for side in range(2 if third else 0):
                by_x[side, piece] = made[:, side, first + second :]
        for step in range(3):
            rz_copy(half, order(step)).start()
        for m in (2, 1, 3):
            ry_copy(half, m).start()
        if third:
            rx_copy().start()
        for step in range(3, Z_SIZE - 1):
            rz_copy(half, order(step)).start()

    def weigh_middle_x():
        rx_copy().wait_recv()
        rx_sum[...] = by_x[x] + rx_in[...]
        for m in (2, 1, 3):
            ryn_copy(m).start()

    def weigh_middle_y(half):
        for m in range(1, Y_SIZE):
            ry_copy(half, m).wait_recv()
        ry_sum[half][...] = by_y[half][y] + ry_in[half][1] + ry_in[half][2] + ry_in[half][3]
        for step in range(Z_SIZE - 1):
            rzl_copy(half, order(step)).start()

    def weigh_middle_z(half):
        for k in range(1, Z_SIZE):
            rz_copy(half, k).wait_recv()
        rz_sum[half][...] = by_z[half][z] + sum(rz_in[half][k] for k in range(1, Z_SIZE))
        for m in (2, 1, 3):
            ryl_copy(half, m).start()

    def weigh_next():
        for m in range(1, Y_SIZE):
            ryn_copy(m).wait_recv()
        ry_total[...] = rx_sum[y] + sum(ry_next[m] for m in range(1, Y_SIZE))
        for step in range(Z_SIZE - 1):
            rzn_copy(order(step)).start()

    def weigh_late(half):
        first = splits[half][0]
        for m in range(1, Y_SIZE):
            ryl_copy(half, m).wait_recv()
        rl_own[half][:, :first] = rz_sum[half][y] + sum(ry_late[half][m] for m in range(1, Y_SIZE))
        for k in range(1, Z_SIZE):
            rzl_copy(half, k).wait_recv()
        rl_own[half][:, first:] = ry_sum[half][z] + sum(rz_late[half][k] for k in range(1, Z_SIZE))
        rl_copy(half).start()

    def weigh_end(half):
        first, second, third = splits[half]
        columns = slice((1 - half) * STATE, (2 - half) * STATE)
        if third:
            for k in range(1, Z_SIZE):
                rzn_copy(k).wait_recv()
            weight[first + second :, columns] = ry_total[z] + sum(rz_next[k] for k in range(1, Z_SIZE))
        rl_copy(half).wait_recv()
        weight[: first + second, columns] = rl_own[half][x] + rl_in[half][...]


    def done(turn):
        return jnp.where(turn == 0, 0, jnp.minimum(turn + 1, heads * HEAD // width))

    def joins(turn, _):
        chunk = turn // 2

        def one_join(step, _):
            join(chunk, step)
            return 0

        def one_group(index, _):
            inside(index)
            return 0

        lax.fori_loop(turn % 2 * 4, turn % 2 * 4 + 4, one_join, 0)
        lax.fori_loop(done(turn), done(turn + 1), one_group, 0)

        @pl.when(turn == 1)
        def _():
            scan_decays()

        @pl.when(turn == 3)
        def _():
            for m in range(1, Y_SIZE):
                dy_copy(m).wait_recv()

        @pl.when(jnp.logical_and(turn >= 2, turn % 2 == 0))
        def _():
            scan(chunk - 1)

        @pl.when(jnp.logical_and(turn >= 3, turn % 2 == 1))
        def _():
            spread(chunk - 1)

        return 0

    def nearest(step):
        return order(Z_SIZE - 1 - step)

    def own_then_far(step):
        return order((step + Z_SIZE - 1) % Z_SIZE)

    def piece_of(half, k):
        return half * Z_SIZE + (z + Z_SIZE - k) % Z_SIZE

    def first_chunk(step, _):
        hand_on(0, nearest(step))
        return 0

    def second_chunk(step, _):
        hand_on(1, nearest(step))
        return 0

    def own_first(step, _):
        with_start(piece_of(x, nearest(step)))
        return 0

    def others_first(step, _):
        k = nearest(step)
        r_copy(0, k).wait_recv()
        r_copy(1, k).wait_recv()
        with_start(piece_of(1 - x, k))
        return 0

    def third_chunk(step, _):
        hand_on(2, nearest(step))
        return 0

    def last_chunk(step, _):
        hand_on(3, own_then_far(step))
        return 0

    def own_last(step, _):
        with_finish(piece_of(x, own_then_far(step)))
        return 0

    def others_last(step, _):
        k = own_then_far(step)
        r_copy(2, k).wait_recv()
        r_copy(3, k).wait_recv()
        with_finish(piece_of(1 - x, k))
        return 0

    pass_decays()
    lax.fori_loop(0, Z_SIZE, joins, 0)
    lax.fori_loop(0, Z_SIZE, first_chunk, 0)
    lax.fori_loop(0, Z_SIZE, second_chunk, 0)
    span = layer.shape[1] // Y_SIZE
    for piece in range(Y_SIZE):
        flipped[piece] = layer[:, piece * span : (piece + 1) * span].T
    mix_maps()
    scan(3)
    lax.fori_loop(0, Z_SIZE, own_first, 0)
    spread(3)
    lax.fori_loop(0, Z_SIZE // 2, others_first, 0)
    lax.fori_loop(0, Z_SIZE, third_chunk, 0)
    lax.fori_loop(Z_SIZE // 2, Z_SIZE, others_first, 0)
    sum_begin(0)
    sum_middle(0)
    lax.fori_loop(0, Z_SIZE, last_chunk, 0)
    low = sum_end(0)
    weigh(0, low)
    lax.fori_loop(0, Z_SIZE, own_last, 0)
    lax.fori_loop(0, Z_SIZE, others_last, 0)
    sum_begin(1)
    sum_middle(1)
    weigh_middle_y(0)
    weigh_middle_z(0)
    low = sum_end(1)
    weigh(1, low)
    for block in range(count):
        end_term = jnp.sum(jnp.sum(ends[block], axis=1), axis=1, keepdims=True)
        at_last = iota((heads, BLOCK), 1) == BLOCK - 1
        changes = change[block] + jnp.where(at_last, end_term, 0.0)
        grad_decay[:, blocks[block]] = dot(changes, lower, NN, HIGHEST)
    weigh_middle_x()
    weigh_middle_y(1)
    weigh_next()
    weigh_middle_z(1)
    weigh_late(0)
    weigh_late(1)
    weigh_end(0)
    weigh_end(1)

    dx_copy().wait_send()
    for chunk in range(CHUNKS):
        for k in range(Z_SIZE):
            x_copy(chunk, k).wait_send()
            r_copy(chunk, k).wait_send()
            if k:
                z_copy(chunk, k).wait_send()
                b_copy(chunk, k).wait_send()
        for m in range(1, Y_SIZE):
            y_copy(chunk, m).wait_send()
    for k in range(1, Z_SIZE):
        dz_copy(k).wait_send()
        rzn_copy(k).wait_send()
        for half in range(2):
            rz_copy(half, k).wait_send()
            rzl_copy(half, k).wait_send()
    for m in range(1, 4):
        dy_copy(m).wait_send()
        ryn_copy(m).wait_send()
        for half in range(2):
            ry_copy(half, m).wait_send()
            ryl_copy(half, m).wait_send()
    rx_copy().wait_send()
    for half in range(2):
        rl_copy(half).wait_send()
        p_copy(half).wait_send()
        for target in range(2):
            g_copy(half, core, target).wait_send()


def dma(*shape):
    return pltpu.SemaphoreType.DMA(shape)


def hand_out_kernel(a, b, c, d, a_out, b_out, c_out, d_out, sems):
    pairs = ((a, a_out), (b, b_out), (c, c_out), (d, d_out))
    copies = [pltpu.make_async_copy(one, out, sems.at[i]) for i, (one, out) in enumerate(pairs)]
    for copy in copies:
        copy.start()
    for copy in copies:
        copy.wait()


def on_device(layer_input, conv_output, state_maps, log_decay, out_grad):
    toks, columns = conv_output.shape
    heads = log_decay.shape[0]
    slices = heads // 2
    count = toks // BLOCK
    tile = columns // (Y_SIZE * Z_SIZE * 2)
    splits = ((tile // 4, tile // 4 * 3, 0), (tile // 4, tile // 2, tile // 4))
    third = splits[1][2]

    def floats(*shape):
        return pltpu.VMEM(shape, F32)

    def both(which, *shape):
        return [floats(*shape, splits[half][which], STATE) for half in range(2)]

    grad_conv, grad_maps, grad_decay, grad_weight = pl.pallas_call(
        functools.partial(kernel, 1.0 / math.sqrt(toks * lax.axis_size("ctx")), splits),
        out_shape=(
            pltpu.VMEM((toks, columns), BF16),
            pltpu.VMEM((toks, 2 * STATE), F32),
            pltpu.VMEM((heads, toks), F32),
            pltpu.VMEM((tile, 2 * STATE), F32),
        ),
        in_specs=[VMEM] * 5,
        out_specs=(VMEM,) * 4,
        scratch_shapes=[
            floats(2, slices, PAIR, STATE),
            floats(2, Z_SIZE, PAIR, STATE),
            floats(CHUNKS, Z_SIZE, HEAD, STATE),
            floats(CHUNKS, Z_SIZE, HEAD, STATE),
            floats(CHUNKS, Y_SIZE, HEAD, STATE),
            floats(CHUNKS, Z_SIZE, HEAD, STATE),
            floats(CHUNKS, Z_SIZE, HEAD, STATE),
            floats(CHUNKS, Z_SIZE, HEAD, STATE),
            floats(CHUNKS, Z_SIZE, HEAD, STATE),
            floats(2, slices, PAIR, STATE),
            floats(slices, 8, STATE),
            floats(Z_SIZE, 8, STATE),
            floats(Z_SIZE, 8, STATE),
            floats(Z_SIZE, 8, STATE),
            floats(Y_SIZE, 8, STATE),
            floats(2, Z_SIZE, 8, STATE),
            floats(count, heads, 8, BLOCK),
            floats(count, heads, 8, STATE),
            floats(count, heads, BLOCK),
            floats(count, heads, 8, STATE),
            floats(count, BLOCK, BLOCK),
            floats(2, count, BLOCK, STATE),
            floats(2, toks, columns),
            pltpu.VMEM((2, toks, columns), BF16),
            floats(2, toks, columns),
            floats(count, slices, PAIR, STATE),
            floats(max(count - 1, 1), slices, PAIR, STATE),
            floats(count, slices, PAIR, STATE),
            floats(2, toks, STATE),
            floats(2, toks, STATE),
            floats(2, toks, STATE),
            floats(2, toks, STATE),
            pltpu.VMEM((Y_SIZE, columns // Y_SIZE, toks), BF16),
            both(1, Y_SIZE, Z_SIZE, 2),
            floats(2, Y_SIZE, Z_SIZE, third, STATE),
            both(0, Z_SIZE, Y_SIZE, 2),
            both(1, Y_SIZE, Z_SIZE, 2),
            floats(Y_SIZE, Z_SIZE, third, STATE),
            both(0, Z_SIZE, Y_SIZE, 2),
            both(1, Z_SIZE, 2),
            floats(Y_SIZE, Z_SIZE, third, STATE),
            both(0, Y_SIZE, 2),
            both(1, Z_SIZE, 2),
            both(0, Y_SIZE, 2),
            floats(Y_SIZE, Z_SIZE, third, STATE),
            floats(Z_SIZE, third, STATE),
            floats(Z_SIZE, third, STATE),
            [floats(2, sum(split[:2]), STATE) for split in splits],
            [floats(sum(split[:2]), STATE) for split in splits],
            dma(CHUNKS, Z_SIZE), dma(CHUNKS, Z_SIZE), dma(CHUNKS, Z_SIZE), dma(CHUNKS, Z_SIZE),
            dma(CHUNKS, Y_SIZE), dma(CHUNKS, Y_SIZE), dma(CHUNKS, Z_SIZE), dma(CHUNKS, Z_SIZE),
            dma(CHUNKS, Z_SIZE), dma(CHUNKS, Z_SIZE),
            dma(1), dma(1), dma(Z_SIZE), dma(Z_SIZE), dma(Y_SIZE), dma(Y_SIZE),
            dma(2), dma(2), dma(2, 2), dma(2, 2),
            dma(2, Y_SIZE), dma(2, Y_SIZE), dma(2, Z_SIZE), dma(2, Z_SIZE),
            dma(1), dma(1), dma(2, Z_SIZE), dma(2, Z_SIZE), dma(2, Y_SIZE), dma(2, Y_SIZE),
            dma(Y_SIZE), dma(Y_SIZE), dma(Z_SIZE), dma(Z_SIZE),
            dma(2), dma(2),
        ],
        compiler_params=pltpu.CompilerParams(
            collective_id=0, has_side_effects=True, vmem_limit_bytes=LIMIT
        ),
        name="backward",
    )(
        *(
            pltpu.with_memory_space_constraint(one, pltpu.HBM)
            for one in (conv_output, out_grad, state_maps, log_decay, layer_input)
        )
    )
    results = [
        pltpu.with_memory_space_constraint(one, pltpu.VMEM)
        for one in (grad_conv, grad_maps, grad_decay, grad_weight)
    ]
    return pl.pallas_call(
        hand_out_kernel,
        out_shape=tuple(jax.ShapeDtypeStruct(one.shape, one.dtype) for one in results),
        in_specs=[pl.BlockSpec(memory_space=pl.ANY)] * 4,
        out_specs=(pl.BlockSpec(memory_space=pl.ANY),) * 4,
        scratch_shapes=[dma(4)],
        name="hand_out",
    )(*results)


def solution(mesh):
    placed = (P("ctx", "dp"), P("ctx", "dp"), P("ctx", None), P("dp", "ctx"), P("ctx", "dp"))
    return jax.shard_map(
        on_device,
        mesh=mesh,
        in_specs=placed,
        out_specs=(P("ctx", "dp"), P("ctx", None), P("dp", "ctx"), P(("dp", "ctx"), None)),
        check_vma=False,
    )
```

```python
import functools
import math

import jax
import jax.numpy as jnp
from jax import lax
from jax.experimental import pallas as pl
from jax.experimental.pallas import tpu as pltpu
from jax.sharding import PartitionSpec as P

BLOCK = 128
HEAD = 64
STATE = 128
PAIR = 2 * HEAD
CHUNKS = 4
Z_SIZE = 8
Y_SIZE = 4
MESH = pl.DeviceIdType.MESH
F32 = jnp.float32
BF16 = jnp.bfloat16
HIGHEST = lax.Precision.HIGHEST
NT = (((1,), (1,)), ((), ()))
TN = (((0,), (0,)), ((), ()))
NN = (((1,), (0,)), ((), ()))
VMEM = pl.BlockSpec(memory_space=pltpu.VMEM)
FAR = pl.BlockSpec(memory_space=pl.ANY)
LIMIT = 48 * 1024 * 1024


def dot(a, b, dims=NN, precision=None):
    return lax.dot_general(a, b, dims, precision=precision, preferred_element_type=F32)


def iota(shape, axis):
    return lax.broadcasted_iota(jnp.int32, shape, axis)


def two_parts(values):
    high = values.astype(BF16)
    return high, (values - high.astype(F32)).astype(BF16)


def three_parts(values):
    high, rest = two_parts(values)
    return high, rest, (values - high.astype(F32) - rest.astype(F32)).astype(BF16)


def head_lanes(first_head, head_count, columns, width):
    shape = (head_count, columns)
    return (iota(shape, 0) == first_head + iota(shape, 1) // width).astype(BF16)


def widen(parts, lanes):
    return dot(parts[0], lanes) + dot(parts[1], lanes)


def place():
    dp, ctx = lax.axis_index("dp"), lax.axis_index("ctx")
    return dp, ctx // (2 * Z_SIZE), (ctx // 2) % Z_SIZE, ctx % 2


def device(dp, y, z, x):
    return (dp, (y * Z_SIZE + z) * 2 + x)


def remote(src, dst, send, recv, target):
    return pltpu.make_async_remote_copy(
        src_ref=src, dst_ref=dst, send_sem=send, recv_sem=recv, device_id=target, device_id_type=MESH
    )


def pick(tile, part):
    return jnp.where(part == 0, tile[0:1], tile[4:5])


def order(step):
    odd = step % 2
    return Z_SIZE // 2 + (step // 2) * (1 - odd) - ((step + 1) // 2) * odd


def kernel(
    scale, splits,
    conv, grad_far, maps, decay, layer_far, grad_conv, grad_maps, grad_decay, weight,
    own, x_in, t_out, z_in, y_in, before, back_out, back_in, x_out, result,
    d_own, d_x, d_t, d_z, d_y, d_before,
    cum_rows, total_rows, change, ends, mix, flow, wide, weighed, inner_out, finals, backs, states,
    part, beside, total, across, flipped, by_y, by_x, by_z,
    ry_in, rx_in, rz_in, ry_sum, rx_sum, rz_sum, rz_late, ry_late, ry_next, ry_total, rz_next,
    rl_own, rl_in,
    x_send, x_recv, z_send, z_recv, y_send, y_recv, b_send, b_recv, r_send, r_recv,
    dx_send, dx_recv, dz_send, dz_recv, dy_send, dy_recv,
    p_send, p_recv, g_send, g_recv, ry_send, ry_recv, rz_send, rz_recv,
    rx_send, rx_recv, rzl_send, rzl_recv, ryl_send, ryl_recv, ryn_send, ryn_recv, rzn_send, rzn_recv,
    rl_send, rl_recv, grad, layer, load_sems,
):
    loads = [
        pltpu.make_async_copy(far, near, load_sems.at[one])
        for one, (far, near) in enumerate(((grad_far, grad), (layer_far, layer)))
    ]
    for load in loads:
        load.start()
    dp, y, z, x = place()
    other = device(dp, y, z, 1 - x)

    def z_at(k):
        return device(dp, y, (z + k) % Z_SIZE, x)

    def y_at(m):
        return device(dp, (y + m) % Y_SIZE, z, x)

    def p_at(m):
        return device((dp + m) % 4, y, z, x)

    partners = [other] + [z_at(k) for k in range(1, Z_SIZE)]
    partners += [y_at(m) for m in range(1, Y_SIZE)] + [p_at(m) for m in range(1, 4)]
    barrier = pltpu.get_barrier_semaphore()
    for partner in partners:
        pl.semaphore_signal(barrier, inc=1, device_id=partner, device_id_type=MESH)

    heads, toks = decay.shape
    count = toks // BLOCK
    width = 4 * HEAD
    square = (BLOCK, BLOCK)
    blocks = [slice(block * BLOCK, (block + 1) * BLOCK) for block in range(count)]


    def head_rows(chunk):
        return pl.ds(pl.multiple_of(chunk % 2 * HEAD, HEAD), HEAD)

    def x_copy(chunk, k):
        piece, rows = (z + k) % Z_SIZE, head_rows(chunk)
        return remote(
            own.at[chunk // 2, (1 - x) * Z_SIZE + piece, rows], x_in.at[chunk // 2, piece, rows],
            x_send.at[chunk, k], x_recv.at[chunk, k], other,
        )

    def z_copy(chunk, k):
        return remote(
            t_out.at[chunk, k], z_in.at[chunk, k], z_send.at[chunk, k], z_recv.at[chunk, k], z_at(k)
        )

    def y_copy(chunk, m):
        return remote(
            y_in.at[chunk, 0], y_in.at[chunk, m], y_send.at[chunk, m], y_recv.at[chunk, m], y_at(m)
        )

    def b_copy(chunk, k):
        return remote(
            back_out.at[chunk, k], back_in.at[chunk, k], b_send.at[chunk, k], b_recv.at[chunk, k], z_at(k)
        )

    def r_copy(chunk, k):
        piece = x * Z_SIZE + (z + Z_SIZE - k) % Z_SIZE
        return remote(
            x_out.at[chunk, k], result.at[chunk // 2, piece, head_rows(chunk)],
            r_send.at[chunk, k], r_recv.at[chunk, k], other,
        )

    def dx_copy():
        rows = pl.ds((1 - x) * Z_SIZE, Z_SIZE)
        return remote(d_own.at[rows], d_x, dx_send.at[0], dx_recv.at[0], other)

    def dz_copy(k):
        return remote(d_t.at[k], d_z.at[k], dz_send.at[k], dz_recv.at[k], z_at(k))

    def dy_copy(m):
        return remote(d_y.at[0], d_y.at[m], dy_send.at[m], dy_recv.at[m], y_at(m))


    decays = decay[...]
    lower_all = (iota((toks, toks), 1) <= iota((toks, toks), 0)).astype(BF16)
    decay_parts = three_parts(decays)
    cum_all = sum(dot(lower_all, piece, NT) for piece in decay_parts)
    factors = (two_parts(jnp.exp(cum_all[toks - 1 : toks, :] - cum_all)), two_parts(jnp.exp(cum_all)))
    sources = (conv, grad)
    total_all = jnp.exp(sum(dot(piece, jnp.ones((toks, STATE), BF16)) for piece in decay_parts))
    expand = (iota((heads * 4, heads), 0) // 4 == iota((heads * 4, heads), 1)).astype(BF16)
    d_own[...] = sum(dot(expand, piece) for piece in three_parts(total_all)).reshape(heads // 2, 8, STATE)

    def summarize(way, half):
        chunk = 8 * HEAD
        for piece in range(heads // 2 * HEAD // chunk):
            first = half * (heads // 2 * HEAD) + piece * chunk
            columns = pl.ds(pl.multiple_of(first, chunk), chunk)
            lanes = head_lanes(half * (heads // 2) + piece * 8, heads, chunk, HEAD)
            weighted = (widen(factors[way], lanes) * sources[way][:, columns].astype(F32)).astype(BF16)
            made = dot(weighted, maps[:, way * STATE : (way + 1) * STATE], TN)
            own[way, pl.ds(half * Z_SIZE + piece * 4, 4)] = made.reshape(4, PAIR, STATE)

    summarize(0, 1 - x)
    pl.semaphore_wait(barrier, len(partners))
    dx_copy().start()
    for chunk in range(2):
        for step in range(Z_SIZE):
            x_copy(chunk, order(step)).start()
    loads[0].wait()
    summarize(1, 1 - x)
    for chunk in range(2, CHUNKS):
        for step in range(Z_SIZE):
            x_copy(chunk, order(step)).start()
    summarize(0, x)
    summarize(1, x)


    causal = iota(square, 1) <= iota(square, 0)
    lower = causal.astype(F32)
    cum_parts, to_end, from_start, scores = [], [], [], []
    for block in range(count):
        rows = blocks[block]
        local = decay[:, rows]
        cum = dot(lower, local, NT, HIGHEST)
        high, middle = two_parts(cum)
        low = (cum - high.astype(F32) - middle.astype(F32)).astype(BF16)
        cum_parts.append((high, middle, low))
        to_end.append(two_parts(jnp.exp(cum[BLOCK - 1 : BLOCK, :] - cum)))
        from_start.append(two_parts(jnp.exp(cum)))
        cum_rows[block] = jnp.broadcast_to(dot(local, lower, NT, HIGHEST)[:, None, :], (heads, 8, BLOCK))
        whole = jnp.exp(dot(local, jnp.ones((BLOCK, STATE), F32), NN, HIGHEST))
        total_rows[block] = jnp.broadcast_to(whole[:, None, :], (heads, 8, STATE))
        scores.append(dot(maps[rows, STATE:], maps[rows, :STATE], NT))
    change[...] = jnp.zeros_like(change)
    mix[...] = jnp.zeros_like(mix)
    flow[...] = jnp.zeros_like(flow)

    def inside(index):
        columns = pl.ds(pl.multiple_of(index * width, width), width)
        pair_slices = pl.ds(index * 2, 2)
        lanes = head_lanes(index * 4, heads, width, HEAD)
        broad = head_lanes(index * 4, heads, 4 * BLOCK, BLOCK)
        in_first = iota((BLOCK, PAIR), 1) < HEAD
        for block in range(count):
            rows = blocks[block]
            xs, gs = conv[rows, columns], grad[rows, columns]
            te, fs = widen(to_end[block], lanes), widen(from_start[block], lanes)
            wide[0, rows, columns] = fs
            wide[1, rows, columns] = te
            xw = (te * xs.astype(F32)).astype(BF16)
            gw = (fs * gs.astype(F32)).astype(BF16)
            weighed[0, rows, columns] = gw
            weighed[1, rows, columns] = xw
            finals[block, pair_slices] = dot(xw, maps[rows, :STATE], TN).reshape(2, PAIR, STATE)
            if block:
                backs[block - 1, pair_slices] = dot(gw, maps[rows, STATE:], TN).reshape(2, PAIR, STATE)
            column = sum(dot(piece, broad) for piece in cum_parts[block])
            y_parts, d_parts, mixed = [], [], None
            for pair in range(2):
                lane = slice(pair * PAIR, (pair + 1) * PAIR)
                x_pair, g_pair = xs[:, lane], gs[:, lane]
                zero = jnp.zeros_like(x_pair)
                x_own = [jnp.where(in_first, x_pair, zero), jnp.where(in_first, zero, x_pair)]
                g_own = [jnp.where(in_first, g_pair, zero), jnp.where(in_first, zero, g_pair)]
                weights = []
                for one in range(2):
                    head = 2 * pair + one
                    col = column[:, head * BLOCK : (head + 1) * BLOCK].reshape(16, 8, BLOCK)
                    gap = (col - cum_rows[block, index * 4 + head][None]).reshape(square)
                    falls = jnp.exp(jnp.where(causal, gap, -1e30))
                    term = falls * dot(g_own[one], x_pair, NT)
                    weights.append((falls * scores[block]).astype(BF16))
                    mixed = term if mixed is None else mixed + term
                y_parts.append(dot(jnp.concatenate(weights, axis=1), jnp.concatenate(x_own, axis=0)))
                d_parts.append(dot(jnp.concatenate(weights, axis=0), jnp.concatenate(g_own, axis=0), TN))
            mix[block] += mixed
            inner_out[0, rows, columns] = jnp.concatenate(y_parts, axis=1)
            inner_out[1, rows, columns] = jnp.concatenate(d_parts, axis=1)


    def pass_decays():
        dx_copy().wait_recv()
        for step in range(Z_SIZE):
            k = order(step)
            piece = (z + k) % Z_SIZE
            target = d_t.at[k] if k else d_z.at[0]
            target[...] = d_own[x * Z_SIZE + piece] * d_x[piece]
            if k:
                dz_copy(k).start()

    def scan_decays():
        for k in range(1, Z_SIZE):
            dz_copy(k).wait_recv()
        for way in range(2):
            fade = jnp.ones((8, STATE), F32)
            for step in range(Z_SIZE):
                at = Z_SIZE - 1 - step if way else step
                d_before[way, (at + Z_SIZE - z) % Z_SIZE] = fade
                fade = fade * d_z[(z + Z_SIZE - at) % Z_SIZE]
        d_y[0] = fade
        for m in (2, 1, 3):
            dy_copy(m).start()

    def join(chunk, step):
        way, part, rows = chunk // 2, chunk % 2, head_rows(chunk)
        k = order(step)
        first = x == way
        x_copy(chunk, k).wait_recv()
        piece = (z + k) % Z_SIZE
        mine = own[way, x * Z_SIZE + piece, rows]
        theirs = x_in[way, piece, rows]
        early = jnp.where(first, mine, theirs)
        late = jnp.where(first, theirs, mine)
        fade = pick(jnp.where(first, d_x[piece], d_own[x * Z_SIZE + piece]), part)
        t_out[chunk, k] = fade * early + late

        @pl.when(step < Z_SIZE - 1)
        def _():
            z_copy(chunk, k).start()

    def scan(chunk):
        way, part = chunk // 2, chunk % 2
        for step in range(Z_SIZE - 1):
            z_copy(chunk, order(step)).wait_recv()
        z_in[chunk, 0] = t_out[chunk, 0]
        state = jnp.zeros((HEAD, STATE), F32)
        for step in range(Z_SIZE):
            at = step + way * (Z_SIZE - 1 - 2 * step)
            slot = (z + Z_SIZE - at) % Z_SIZE
            before[chunk, (at + Z_SIZE - z) % Z_SIZE] = state
            state = pick(d_z[slot], part) * state + z_in[chunk, slot]
        y_in[chunk, 0] = state
        for m in (2, 1, 3):
            y_copy(chunk, m).start()

    def spread(chunk):
        way, part = chunk // 2, chunk % 2
        for m in range(1, Y_SIZE):
            y_copy(chunk, m).wait_recv()
        state = jnp.zeros((HEAD, STATE), F32)
        for step in range(Y_SIZE):
            at = step + way * (Y_SIZE - 1 - 2 * step)
            slot = (y + Y_SIZE - at) % Y_SIZE
            counts = (at - y) * (1 - 2 * way) < 0
            state = jnp.where(counts, pick(d_y[slot], part) * state + y_in[chunk, slot], state)
        for step in range(Z_SIZE):
            k = order(step)
            target = back_out.at[chunk, k] if k else back_in.at[chunk, 0]
            target[...] = before[chunk, k] + pick(d_before[way, k], part) * state
            if k:
                b_copy(chunk, k).start()

    def hand_on(chunk, k):
        way, part, rows = chunk // 2, chunk % 2, head_rows(chunk)
        first = x == way

        @pl.when(k > 0)
        def _():
            b_copy(chunk, k).wait_recv()

        piece = (z + Z_SIZE - k) % Z_SIZE
        early = back_in[chunk, k]
        left = jnp.where(first, own[way, x * Z_SIZE + piece, rows], x_in[way, piece, rows])
        fade = pick(jnp.where(first, d_own[x * Z_SIZE + piece], d_x[piece]), part)
        late = fade * early + left
        x_out[chunk, k] = jnp.where(first, late, early)
        result[way, x * Z_SIZE + piece, rows] = jnp.where(first, early, late)
        r_copy(chunk, k).start()


    def fade_rows(block, index, state):
        tiles = total_rows[block, pl.ds(index * 2, 2)][:, None]
        return (state.reshape(2, 8, 8, STATE) * tiles).reshape(PAIR, STATE)

    def add_change(block, index, product):
        lanes = head_lanes(index * 2, heads, PAIR, HEAD)
        high, low = two_parts(product)
        change[block] += dot(lanes, high, NT) + dot(lanes, low, NT)

    def with_start(index):
        columns = pl.ds(pl.multiple_of(index * PAIR, PAIR), PAIR)
        state = result[0, index]
        for block in range(count):
            rows = blocks[block]
            low = state.astype(BF16)
            flow[0, block] += dot(weighed[0, rows, columns], low)
            outputs = inner_out[0, rows, columns] + wide[0, rows, columns] * dot(maps[rows, STATE:], low, NT)
            add_change(block, index, grad[rows, columns].astype(F32) * outputs)
            state = fade_rows(block, index, state) + finals[block, index]
            states[block, index] = state

    def with_finish(index):
        columns = pl.ds(pl.multiple_of(index * PAIR, PAIR), PAIR)
        state = result[1, index]
        for block in reversed(range(count)):
            rows = blocks[block]
            ends[block, pl.ds(index * 2, 2)] = jnp.sum(
                (state * states[block, index]).reshape(2, 8, 8, STATE), axis=1
            )
            low = state.astype(BF16)
            flow[1, block] += dot(weighed[1, rows, columns], low)
            inputs = inner_out[1, rows, columns] + wide[1, rows, columns] * dot(maps[rows, :STATE], low, NT)
            grad_conv[rows, columns] = inputs.astype(BF16)
            add_change(block, index, conv[rows, columns].astype(F32) * -inputs)
            if block:
                state = fade_rows(block, index, state) + backs[block - 1, index]


    core, chip = dp % 2, dp // 2
    share = toks // 2

    def p_copy(half):
        return remote(
            part.at[half], beside.at[half], p_send.at[half], p_recv.at[half],
            device(dp + 1 - 2 * core, y, z, x),
        )

    def g_copy(half, source, target):
        rows = pl.ds(pl.multiple_of(source * share, share), share)
        return remote(
            total.at[half, rows], across.at[half, rows], g_send.at[half, target], g_recv.at[half, source],
            device((1 - chip) * 2 + target, y, z, x),
        )

    def mix_maps():
        for block in range(count):
            rows = blocks[block]
            part[0, rows] = dot(mix[block], maps[rows, :STATE].astype(F32), NN, HIGHEST)
            part[1, rows] = dot(mix[block], maps[rows, STATE:].astype(F32), TN, HIGHEST)

    def sum_begin(half):
        for block in range(count):
            part[half, blocks[block]] += flow[half, block]
        p_copy(half).start()

    def sum_middle(half):
        p_copy(half).wait_recv()
        total[half] = part[half] + beside[half]
        for target in range(2):
            g_copy(half, core, target).start()

    def sum_end(half):
        for source in range(2):
            g_copy(half, source, 0).wait_recv()
        made = total[half] + across[half]
        grad_maps[:, (1 - half) * STATE : (2 - half) * STATE] = made
        return made.astype(BF16)


    def ry_copy(half, m):
        return remote(
            by_y[half].at[(y + m) % Y_SIZE], ry_in[half].at[m], ry_send.at[half, m], ry_recv.at[half, m], y_at(m)
        )

    def rx_copy():
        return remote(by_x.at[1 - x], rx_in, rx_send.at[0], rx_recv.at[0], other)

    def rz_copy(half, k):
        return remote(
            by_z[half].at[(z + k) % Z_SIZE], rz_in[half].at[k], rz_send.at[half, k], rz_recv.at[half, k], z_at(k)
        )

    def rzl_copy(half, k):
        return remote(
            ry_sum[half].at[(z + k) % Z_SIZE], rz_late[half].at[k],
            rzl_send.at[half, k], rzl_recv.at[half, k], z_at(k),
        )

    def ryl_copy(half, m):
        return remote(
            rz_sum[half].at[(y + m) % Y_SIZE], ry_late[half].at[m],
            ryl_send.at[half, m], ryl_recv.at[half, m], y_at(m),
        )

    def ryn_copy(m):
        return remote(
            rx_sum.at[(y + m) % Y_SIZE], ry_next.at[m], ryn_send.at[m], ryn_recv.at[m], y_at(m)
        )

    def rzn_copy(k):
        return remote(
            ry_total.at[(z + k) % Z_SIZE], rz_next.at[k], rzn_send.at[k], rzn_recv.at[k], z_at(k)
        )

    def rl_copy(half):
        return remote(
            rl_own[half].at[1 - x], rl_in[half], rl_send.at[half], rl_recv.at[half], other
        )

    def weigh(half, low):
        first, second, third = splits[half]
        for m in (2, 1, 3, 0):
            piece = (y + m) % Y_SIZE
            made = dot(flipped[piece], low) * scale
            made = made.reshape(Z_SIZE, 2, -1, STATE)
            by_z[half][:, piece] = made[:, :, :first]
            by_y[half][piece] = made[:, :, first : first + second]
            for side in range(2 if third else 0):
                by_x[side, piece] = made[:, side, first + second :]
            if m:
                ry_copy(half, m).start()
        for step in range(3):
            rz_copy(half, order(step)).start()
        if third:
            rx_copy().start()
        for step in range(3, Z_SIZE - 1):
            rz_copy(half, order(step)).start()

    def weigh_middle_x():
        rx_copy().wait_recv()
        rx_sum[...] = by_x[x] + rx_in[...]
        for m in (2, 1, 3):
            ryn_copy(m).start()

    def weigh_middle_y(half):
        for m in range(1, Y_SIZE):
            ry_copy(half, m).wait_recv()
        ry_sum[half][...] = by_y[half][y] + ry_in[half][1] + ry_in[half][2] + ry_in[half][3]
        for step in range(Z_SIZE - 1):
            rzl_copy(half, order(step)).start()

    def weigh_middle_z(half):
        for k in range(1, Z_SIZE):
            rz_copy(half, k).wait_recv()
        rz_sum[half][...] = by_z[half][z] + sum(rz_in[half][k] for k in range(1, Z_SIZE))
        for m in (2, 1, 3):
            ryl_copy(half, m).start()

    def weigh_next():
        for m in range(1, Y_SIZE):
            ryn_copy(m).wait_recv()
        ry_total[...] = rx_sum[y] + sum(ry_next[m] for m in range(1, Y_SIZE))
        for step in range(Z_SIZE - 1):
            rzn_copy(order(step)).start()

    def weigh_late(half):
        first = splits[half][0]
        for m in range(1, Y_SIZE):
            ryl_copy(half, m).wait_recv()
        rl_own[half][:, :first] = rz_sum[half][y] + sum(ry_late[half][m] for m in range(1, Y_SIZE))
        for k in range(1, Z_SIZE):
            rzl_copy(half, k).wait_recv()
        rl_own[half][:, first:] = ry_sum[half][z] + sum(rz_late[half][k] for k in range(1, Z_SIZE))
        rl_copy(half).start()

    def weigh_end(half):
        first, second, third = splits[half]
        columns = slice((1 - half) * STATE, (2 - half) * STATE)
        if third:
            for k in range(1, Z_SIZE):
                rzn_copy(k).wait_recv()
            weight[first + second :, columns] = ry_total[z] + sum(rz_next[k] for k in range(1, Z_SIZE))
        rl_copy(half).wait_recv()
        weight[: first + second, columns] = rl_own[half][x] + rl_in[half][...]


    def done(turn):
        return jnp.where(turn == 0, 0, jnp.minimum(turn + 1, heads * HEAD // width))

    def joins(turn, _):
        chunk = turn // 2

        def one_join(step, _):
            join(chunk, step)
            return 0

        def one_group(index, _):
            inside(index)
            return 0

        lax.fori_loop(turn % 2 * 4, turn % 2 * 4 + 4, one_join, 0)
        lax.fori_loop(done(turn), done(turn + 1), one_group, 0)

        @pl.when(turn == 1)
        def _():
            scan_decays()

        @pl.when(turn == 3)
        def _():
            for m in range(1, Y_SIZE):
                dy_copy(m).wait_recv()

        @pl.when(jnp.logical_and(turn >= 2, turn % 2 == 0))
        def _():
            scan(chunk - 1)

        @pl.when(jnp.logical_and(turn >= 3, turn % 2 == 1))
        def _():
            spread(chunk - 1)

        return 0

    def nearest(step):
        return order(Z_SIZE - 1 - step)

    def own_then_far(step):
        return order((step + Z_SIZE - 1) % Z_SIZE)

    def piece_of(half, k):
        return half * Z_SIZE + (z + Z_SIZE - k) % Z_SIZE

    def first_chunk(step, _):
        hand_on(0, nearest(step))
        return 0

    def second_chunk(step, _):
        hand_on(1, nearest(step))
        return 0

    def own_first(step, _):
        with_start(piece_of(x, nearest(step)))
        return 0

    def others_first(step, _):
        k = nearest(step)
        r_copy(0, k).wait_recv()
        r_copy(1, k).wait_recv()
        with_start(piece_of(1 - x, k))
        return 0

    def third_chunk(step, _):
        hand_on(2, nearest(step))
        return 0

    def last_chunk(step, _):
        hand_on(3, own_then_far(step))
        return 0

    def own_last(step, _):
        with_finish(piece_of(x, own_then_far(step)))
        return 0

    def others_last(step, _):
        k = own_then_far(step)
        r_copy(2, k).wait_recv()
        r_copy(3, k).wait_recv()
        with_finish(piece_of(1 - x, k))
        return 0

    pass_decays()
    lax.fori_loop(0, Z_SIZE, joins, 0)
    lax.fori_loop(0, Z_SIZE, first_chunk, 0)
    lax.fori_loop(0, Z_SIZE, second_chunk, 0)
    loads[1].wait()
    span = layer.shape[1] // Y_SIZE
    for piece in range(Y_SIZE):
        flipped[piece] = layer[:, piece * span : (piece + 1) * span].T
    mix_maps()
    scan(3)
    lax.fori_loop(0, Z_SIZE, own_first, 0)
    spread(3)
    lax.fori_loop(0, Z_SIZE // 2, others_first, 0)
    lax.fori_loop(0, Z_SIZE, third_chunk, 0)
    lax.fori_loop(Z_SIZE // 2, Z_SIZE, others_first, 0)
    sum_begin(0)
    sum_middle(0)
    lax.fori_loop(0, Z_SIZE, last_chunk, 0)
    low = sum_end(0)
    weigh(0, low)
    lax.fori_loop(0, Z_SIZE, own_last, 0)
    lax.fori_loop(0, Z_SIZE, others_last, 0)
    sum_begin(1)
    sum_middle(1)
    weigh_middle_y(0)
    weigh_middle_z(0)
    low = sum_end(1)
    weigh(1, low)
    for block in range(count):
        end_term = jnp.sum(jnp.sum(ends[block], axis=1), axis=1, keepdims=True)
        at_last = iota((heads, BLOCK), 1) == BLOCK - 1
        changes = change[block] + jnp.where(at_last, end_term, 0.0)
        grad_decay[:, blocks[block]] = dot(changes, lower, NN, HIGHEST)
    weigh_middle_x()
    weigh_middle_y(1)
    weigh_next()
    weigh_middle_z(1)
    weigh_late(0)
    weigh_late(1)
    weigh_end(0)
    weigh_end(1)

    dx_copy().wait_send()
    for chunk in range(CHUNKS):
        for k in range(Z_SIZE):
            x_copy(chunk, k).wait_send()
            r_copy(chunk, k).wait_send()
            if k:
                z_copy(chunk, k).wait_send()
                b_copy(chunk, k).wait_send()
        for m in range(1, Y_SIZE):
            y_copy(chunk, m).wait_send()
    for k in range(1, Z_SIZE):
        dz_copy(k).wait_send()
        rzn_copy(k).wait_send()
        for half in range(2):
            rz_copy(half, k).wait_send()
            rzl_copy(half, k).wait_send()
    for m in range(1, 4):
        dy_copy(m).wait_send()
        ryn_copy(m).wait_send()
        for half in range(2):
            ry_copy(half, m).wait_send()
            ryl_copy(half, m).wait_send()
    rx_copy().wait_send()
    for half in range(2):
        rl_copy(half).wait_send()
        p_copy(half).wait_send()
        for target in range(2):
            g_copy(half, core, target).wait_send()


def dma(*shape):
    return pltpu.SemaphoreType.DMA(shape)


def hand_out_kernel(a, b, c, d, a_out, b_out, c_out, d_out, sems):
    pairs = ((a, a_out), (b, b_out), (c, c_out), (d, d_out))
    copies = [pltpu.make_async_copy(one, out, sems.at[i]) for i, (one, out) in enumerate(pairs)]
    for copy in copies:
        copy.start()
    for copy in copies:
        copy.wait()


def on_device(layer_input, conv_output, state_maps, log_decay, out_grad):
    toks, columns = conv_output.shape
    heads = log_decay.shape[0]
    slices = heads // 2
    count = toks // BLOCK
    tile = columns // (Y_SIZE * Z_SIZE * 2)
    splits = ((tile // 4, tile // 4 * 3, 0), (tile // 4, tile // 2, tile // 4))
    third = splits[1][2]

    def floats(*shape):
        return pltpu.VMEM(shape, F32)

    def both(which, *shape):
        return [floats(*shape, splits[half][which], STATE) for half in range(2)]

    grad_conv, grad_maps, grad_decay, grad_weight = pl.pallas_call(
        functools.partial(kernel, 1.0 / math.sqrt(toks * lax.axis_size("ctx")), splits),
        out_shape=(
            pltpu.VMEM((toks, columns), BF16),
            pltpu.VMEM((toks, 2 * STATE), F32),
            pltpu.VMEM((heads, toks), F32),
            pltpu.VMEM((tile, 2 * STATE), F32),
        ),
        in_specs=[VMEM, FAR, VMEM, VMEM, FAR],
        out_specs=(VMEM,) * 4,
        scratch_shapes=[
            floats(2, slices, PAIR, STATE),
            floats(2, Z_SIZE, PAIR, STATE),
            floats(CHUNKS, Z_SIZE, HEAD, STATE),
            floats(CHUNKS, Z_SIZE, HEAD, STATE),
            floats(CHUNKS, Y_SIZE, HEAD, STATE),
            floats(CHUNKS, Z_SIZE, HEAD, STATE),
            floats(CHUNKS, Z_SIZE, HEAD, STATE),
            floats(CHUNKS, Z_SIZE, HEAD, STATE),
            floats(CHUNKS, Z_SIZE, HEAD, STATE),
            floats(2, slices, PAIR, STATE),
            floats(slices, 8, STATE),
            floats(Z_SIZE, 8, STATE),
            floats(Z_SIZE, 8, STATE),
            floats(Z_SIZE, 8, STATE),
            floats(Y_SIZE, 8, STATE),
            floats(2, Z_SIZE, 8, STATE),
            floats(count, heads, 8, BLOCK),
            floats(count, heads, 8, STATE),
            floats(count, heads, BLOCK),
            floats(count, heads, 8, STATE),
            floats(count, BLOCK, BLOCK),
            floats(2, count, BLOCK, STATE),
            floats(2, toks, columns),
            pltpu.VMEM((2, toks, columns), BF16),
            floats(2, toks, columns),
            floats(count, slices, PAIR, STATE),
            floats(max(count - 1, 1), slices, PAIR, STATE),
            floats(count, slices, PAIR, STATE),
            floats(2, toks, STATE),
            floats(2, toks, STATE),
            floats(2, toks, STATE),
            floats(2, toks, STATE),
            pltpu.VMEM((Y_SIZE, columns // Y_SIZE, toks), BF16),
            both(1, Y_SIZE, Z_SIZE, 2),
            floats(2, Y_SIZE, Z_SIZE, third, STATE),
            both(0, Z_SIZE, Y_SIZE, 2),
            both(1, Y_SIZE, Z_SIZE, 2),
            floats(Y_SIZE, Z_SIZE, third, STATE),
            both(0, Z_SIZE, Y_SIZE, 2),
            both(1, Z_SIZE, 2),
            floats(Y_SIZE, Z_SIZE, third, STATE),
            both(0, Y_SIZE, 2),
            both(1, Z_SIZE, 2),
            both(0, Y_SIZE, 2),
            floats(Y_SIZE, Z_SIZE, third, STATE),
            floats(Z_SIZE, third, STATE),
            floats(Z_SIZE, third, STATE),
            [floats(2, sum(split[:2]), STATE) for split in splits],
            [floats(sum(split[:2]), STATE) for split in splits],
            dma(CHUNKS, Z_SIZE), dma(CHUNKS, Z_SIZE), dma(CHUNKS, Z_SIZE), dma(CHUNKS, Z_SIZE),
            dma(CHUNKS, Y_SIZE), dma(CHUNKS, Y_SIZE), dma(CHUNKS, Z_SIZE), dma(CHUNKS, Z_SIZE),
            dma(CHUNKS, Z_SIZE), dma(CHUNKS, Z_SIZE),
            dma(1), dma(1), dma(Z_SIZE), dma(Z_SIZE), dma(Y_SIZE), dma(Y_SIZE),
            dma(2), dma(2), dma(2, 2), dma(2, 2),
            dma(2, Y_SIZE), dma(2, Y_SIZE), dma(2, Z_SIZE), dma(2, Z_SIZE),
            dma(1), dma(1), dma(2, Z_SIZE), dma(2, Z_SIZE), dma(2, Y_SIZE), dma(2, Y_SIZE),
            dma(Y_SIZE), dma(Y_SIZE), dma(Z_SIZE), dma(Z_SIZE),
            dma(2), dma(2),
            pltpu.VMEM((toks, columns), BF16), pltpu.VMEM((toks, columns), BF16), dma(2),
        ],
        compiler_params=pltpu.CompilerParams(
            collective_id=0, has_side_effects=True, vmem_limit_bytes=LIMIT
        ),
        name="backward",
    )(
        *(
            pltpu.with_memory_space_constraint(one, pltpu.HBM)
            for one in (conv_output, out_grad, state_maps, log_decay, layer_input)
        )
    )
    results = [
        pltpu.with_memory_space_constraint(one, pltpu.VMEM)
        for one in (grad_conv, grad_maps, grad_decay, grad_weight)
    ]
    return pl.pallas_call(
        hand_out_kernel,
        out_shape=tuple(jax.ShapeDtypeStruct(one.shape, one.dtype) for one in results),
        in_specs=[pl.BlockSpec(memory_space=pl.ANY)] * 4,
        out_specs=(pl.BlockSpec(memory_space=pl.ANY),) * 4,
        scratch_shapes=[dma(4)],
        name="hand_out",
    )(*results)


def solution(mesh):
    placed = (P("ctx", "dp"), P("ctx", "dp"), P("ctx", None), P("dp", "ctx"), P("ctx", "dp"))
    return jax.shard_map(
        on_device,
        mesh=mesh,
        in_specs=placed,
        out_specs=(P("ctx", "dp"), P("ctx", None), P("dp", "ctx"), P(("dp", "ctx"), None)),
        check_vma=False,
    )
```
